128 devices in a mesh: role: 2 (over y_lo), grp: 16 (over x, z), tp: 4 (over y_hi, core).
Axes of the slice: x: 4, y: 4 (y_hi: 2, y_lo: 2; y = y_hi * 2 + y_lo), z: 4, core: 2. Of those that a mesh axis runs over, the one named last changes fastest.
Arguments:
- q_latent: bfloat16 [1024, 64, 576], P(('role', 'grp', 'tp')), may hold values from -60 to 60
- kv_new: bfloat16 [1024, 576], P(('role', 'grp', 'tp')), may hold values from -6 to 6
- kv_cache: bfloat16 [1024, 1024, 576], P(('role', 'grp', 'tp')), may hold values from -6 to 6
- lengths: int32 [1024], P(('role', 'grp', 'tp')), may hold values from 2 to 1024, as said below
- members: int32 [1024], P(('role', 'grp', 'tp')), may hold values from 0 to 7, as said below
- hidden_in: bfloat16 [1024, 7168], P('role', 'grp'), may hold values from -40 to 40
- w_uv: bfloat16 [64, 512, 128], P('tp'), may hold values from -1.5 to 1.5
- w_o: bfloat16 [8192, 7168], P('tp', 'grp'), may hold values from -0.0625 to 0.0625
- norm_gain: bfloat16 [7168], P('grp'), may hold values from 0.5 to 1.5
- w_gate: bfloat16 [7168, 18432], P('grp', ('role', 'tp')), may hold values from -0.09375 to 0.09375
- w_up: bfloat16 [7168, 18432], P('grp', ('role', 'tp')), may hold values from -0.0625 to 0.0625
- w_down: bfloat16 [18432, 7168], P(('role', 'tp'), 'grp'), may hold values from -0.046875 to 0.046875
Outputs:
- layer_out: bfloat16 [1024, 7168], P(('role', 'grp'))
The draws below stay inside these ranges and needn't reach their ends.
Inputs may be any that keep to these rules, and one draw needn't show every extreme that they name: `lengths`: each request's cache is valid at positions 0 to its length - 1. Within each aligned block of 8 tokens, members is a permutation of 0 to 7.
All inputs are finite; a program needn't handle non-finite values.
Results may differ from the reference program's by a relative error of at most 0.017.
Values may be sent and summed in bfloat16 or wider, within the bound.
No kernel may reach another device: no remote copies, remote signals or barrier semaphores. Data moves between devices by JAX's collectives and lax.ppermute only.
A program may use at most 128 MiB of HBM per device.

```python
import math
import jax
import jax.numpy as jnp
from jax import lax

D = 7168
FF = 18432
LAT = 512
ROPE = 64
VH = 128
HEADS = 64
CTX = 1024
REQ_T = 8
KV = 576
TOKENS = 1024


def lead_rows(key):
    lead_key = jax.random.fold_in(key, 102)
    return jnp.clip(jax.random.normal(lead_key, (TOKENS, 2, KV), jnp.float32), -6.0, 6.0)


def member_table(key):
    table_key = jax.random.fold_in(key, 103)
    block_keys = jax.random.split(table_key, TOKENS // REQ_T)
    orders = jax.vmap(lambda one_key: jax.random.permutation(one_key, REQ_T))(block_keys)
    return orders.reshape(-1).astype(jnp.int32)


def draw_kv_cache(key, part):
    leading = lead_rows(key)
    key = jax.random.fold_in(key, 3)
    cache_rows = jnp.clip(jax.random.normal(key, (TOKENS, CTX, KV), jnp.float32), -6.0, 6.0)
    return cache_rows.at[:, :2].set(leading).astype(jnp.bfloat16)


def draw_members(key, part):
    return member_table(key)


def draw_q_latent(key, part):
    key = jax.random.fold_in(key, 5)
    base_draw = 0.5 * jnp.clip(jax.random.normal(key, (TOKENS, HEADS, KV), jnp.float32), -6.0, 6.0)
    return base_draw.astype(jnp.bfloat16)


def draw_lengths(key, part):
    key = jax.random.fold_in(key, 9)
    cap_key, len_key = jax.random.split(key)
    block_count = TOKENS // REQ_T
    ceilings = jax.random.randint(cap_key, (block_count, 1), CTX // 4, CTX + 1)
    ceilings = ceilings.at[0, 0].set(CTX)
    raw_len = jax.random.randint(len_key, (block_count, REQ_T), 2, CTX + 1)
    scaled = jnp.maximum(2, raw_len * ceilings // CTX)
    scaled = scaled.at[:, 0].set(ceilings[:, 0])
    return scaled.reshape(-1).astype(jnp.int32)


def draw_hidden_in(key, part):
    key = jax.random.fold_in(key, 13)
    row_key, col_key, base_key = jax.random.split(key, 3)
    slope = 1.0 + 2.0 * jnp.arange(D, dtype=jnp.float32) / (D - 1)
    columns = slope * jax.random.uniform(col_key, (D,), jnp.float32, 1.0, 2.0)
    row_scale = jnp.exp(jax.random.uniform(row_key, (TOKENS, 1), jnp.float32, math.log(0.03), math.log(0.3)))
    base_draw = jnp.clip(jax.random.normal(base_key, (TOKENS, D), jnp.float32), -6.0, 6.0)
    return (base_draw * row_scale * columns).astype(jnp.bfloat16)


def with_spikes(entries, rng, source, target, blocks, factor):
    def block_of(dim):
        return (jnp.arange(entries.shape[dim]) // (entries.shape[dim] // blocks)).reshape((-1,) + (1,) * (entries.ndim - 1 - dim))

    one_side = jax.random.permutation(rng, blocks)[block_of(target)]
    far = (block_of(target) + blocks // 2) % blocks
    return jnp.where((block_of(source) == one_side) | (block_of(source) == far), factor * entries, entries)


def steps_of(own_key, shape, cuts, least, largest):
    level, own = 1.0, jax.random.fold_in(own_key, 6)
    for position, parts in cuts:
        steps = jnp.exp(jax.random.uniform(jax.random.fold_in(own, position), (parts,), jnp.float32, least / len(cuts), largest / len(cuts)))
        level = level * jnp.repeat(steps, shape[position] // parts).reshape([-1 if axis == position else 1 for axis in range(len(shape))])
    return level


def noise(key, dims, spread, bound, shards=(), held_as=jnp.bfloat16):
    result = jax.random.normal(key, dims, jnp.float32) * spread
    if len(shards) > 0:
        result = steps_of(key, dims, shards, -0.22, 0.18) * result
    return jnp.clip(result, min=-bound, max=bound).astype(held_as)


def bell_draw_with(key, dims, scale, limit, cuts, heavy, kind=jnp.bfloat16):
    entries = scale * jax.random.normal(key, dims, jnp.float32)
    if cuts:
        entries = entries * steps_of(key, dims, cuts, -0.22, 0.18)
    return jnp.clip(with_spikes(entries, jax.random.fold_in(key, 3), *heavy), -limit, limit).astype(kind)


def setup_inputs(seed: int = 0) -> dict:
    streams_of = jax.random.split(jax.random.key(seed), 13)
    q_latent = draw_q_latent(jax.random.fold_in(streams_of[12], 71), 0)
    kv_new = noise(streams_of[1], (TOKENS, KV), 1.0, 6.0, ((0, 128),))
    kv_cache = draw_kv_cache(jax.random.fold_in(streams_of[12], 71), 0)
    lengths = draw_lengths(jax.random.fold_in(streams_of[12], 71), 0)
    members = draw_members(jax.random.fold_in(streams_of[12], 71), 0)
    hidden_in = draw_hidden_in(jax.random.fold_in(streams_of[12], 71), 0)
    w_uv = noise(streams_of[6], (HEADS, LAT, VH), 16 ** -0.5, 1.5, ((0, 4),))
    w_o = noise(streams_of[7], (HEADS * VH, D), (HEADS * VH) ** -0.5, 0.0625, ((0, 4), (1, 16)))
    norm_gain = jnp.clip(1.0 + 0.1 * jax.random.normal(streams_of[8], (D,), jnp.float32), 0.5, 1.5).astype(jnp.bfloat16)
    w_gate = bell_draw_with(streams_of[9], (D, FF), D ** -0.5, 0.09375, ((0, 16), (1, 8)), (0, 1, 16, 2.0))
    w_up = noise(streams_of[10], (D, FF), D ** -0.5, 0.0625, ((0, 16), (1, 8)))
    w_down = noise(streams_of[11], (FF, D), FF ** -0.5, 0.046875, ((0, 8), (1, 16)))
    return dict(q_latent=q_latent, kv_new=kv_new, kv_cache=kv_cache, lengths=lengths, members=members, hidden_in=hidden_in, w_uv=w_uv, w_o=w_o, norm_gain=norm_gain, w_gate=w_gate, w_up=w_up, w_down=w_down)


def reference(q_latent, kv_new, kv_cache, lengths, members, hidden_in, w_uv, w_o, norm_gain, w_gate, w_up, w_down):
    score_scale = (VH + ROPE) ** (-0.5)
    block_count = TOKENS // REQ_T
    positions = jnp.arange(CTX, dtype=jnp.int32)

    def attend(block_id):
        first_row = (block_id * REQ_T).astype(jnp.int32)
        row_ids = first_row + lax.dynamic_slice_in_dim(members, first_row, REQ_T).astype(jnp.int32)
        queries = lax.dynamic_slice_in_dim(q_latent, first_row, REQ_T).astype(jnp.float32)
        newest = lax.dynamic_slice_in_dim(kv_new, first_row, REQ_T).astype(jnp.float32)
        cache_rows = jnp.take(kv_cache, row_ids, axis=0).astype(jnp.float32)
        cache_len = jnp.take(lengths, row_ids)
        scores = jnp.einsum('rhk,rpk->rhp', queries, cache_rows) * score_scale
        own_score = jnp.einsum('rhk,rk->rh', queries, newest) * score_scale
        usable = positions[None, None, :] < cache_len[:, None, None]
        peak = jnp.maximum(lax.optimization_barrier(jnp.max(jnp.where(usable, scores, -1e+30), axis=2)), own_score)
        probs = jnp.where(usable, jnp.exp(scores - peak[..., None]), 0.0)
        probs = lax.optimization_barrier(probs.astype(jnp.bfloat16)).astype(jnp.float32)
        self_weight = jnp.exp(own_score - peak)
        denom = lax.optimization_barrier(jnp.sum(probs, axis=2)) + self_weight
        accum = jnp.einsum('rhp,rpl->rhl', probs, cache_rows[:, :, :LAT])
        accum = accum + self_weight[..., None] * newest[:, None, :LAT]
        return (accum / denom[..., None]).astype(jnp.bfloat16)
    context = lax.map(attend, jnp.arange(block_count, dtype=jnp.int32)).reshape(TOKENS, HEADS, LAT)
    values = jnp.einsum('thl,hlv->thv', context.astype(jnp.float32), w_uv.astype(jnp.float32))
    values = values.astype(jnp.bfloat16).reshape(TOKENS, HEADS * VH)
    stream = hidden_in.astype(jnp.float32) + jnp.dot(values, w_o, preferred_element_type=jnp.float32)
    square_sum = lax.optimization_barrier(jnp.sum(stream * stream, axis=1, keepdims=True))
    normed = (stream * lax.rsqrt(square_sum / D + 1e-06) * norm_gain.astype(jnp.float32)).astype(jnp.bfloat16)
    gate = jnp.dot(normed, w_gate, preferred_element_type=jnp.float32)
    up = jnp.dot(normed, w_up, preferred_element_type=jnp.float32)
    activated = (jax.nn.silu(gate) * up).astype(jnp.bfloat16)
    down = jnp.dot(activated, w_down, preferred_element_type=jnp.float32)
    return (stream + down).astype(jnp.bfloat16)
```

```python
import functools

import jax
import jax.numpy as jnp
from jax import lax
from jax.experimental import pallas as pl
from jax.experimental.pallas import tpu as pltpu
from jax.sharding import PartitionSpec as P

epsilon = 1e-06
VMEM_LIMIT = 48 * 1024 * 1024


def attend_kernel(scale, latent, members_ref, lengths_ref, q_ref, new_ref, kv_ref, out_ref):
    token = pl.program_id(0)
    length = lengths_ref[members_ref[token]]
    queries = q_ref[0]
    cache = kv_ref[0]
    newest = new_ref[0]
    scores = scale * lax.dot_general(
        queries, cache, (((1,), (1,)), ((), ())), preferred_element_type=jnp.float32
    )
    own = scale * jnp.sum(queries.astype(jnp.float32) * newest, axis=1, keepdims=True)
    usable = lax.broadcasted_iota(jnp.int32, scores.shape, 1) < length
    scores = jnp.where(usable, scores, -1e30)
    peak = jnp.maximum(jnp.max(scores, axis=1, keepdims=True), own)
    probs = jnp.exp(scores - peak).astype(jnp.bfloat16)
    self_weight = jnp.exp(own - peak)
    denom = jnp.sum(probs.astype(jnp.float32), axis=1, keepdims=True) + self_weight
    accum = jnp.dot(probs, cache[:, :latent], preferred_element_type=jnp.float32)
    accum = accum + self_weight * newest[:, :latent]
    out_ref[0] = (accum / denom).astype(out_ref.dtype)


def attend(q_latent, kv_new, kv_cache, lengths, members, scale, latent):
    tokens, heads, kv = q_latent.shape
    ctx = kv_cache.shape[1]
    grid_spec = pltpu.PrefetchScalarGridSpec(
        num_scalar_prefetch=2,
        grid=(tokens,),
        in_specs=[
            pl.BlockSpec((1, heads, kv), lambda t, m, n: (t, 0, 0)),
            pl.BlockSpec((1, 1, kv), lambda t, m, n: (t, 0, 0)),
            pl.BlockSpec((1, ctx, kv), lambda t, m, n: (m[t], 0, 0)),
        ],
        out_specs=pl.BlockSpec((1, heads, latent), lambda t, m, n: (t, 0, 0)),
    )
    return pl.pallas_call(
        functools.partial(attend_kernel, scale, latent),
        grid_spec=grid_spec,
        out_shape=jax.ShapeDtypeStruct((tokens, heads, latent), jnp.bfloat16),
        compiler_params=pltpu.CompilerParams(vmem_limit_bytes=VMEM_LIMIT),
        name="attend",
    )(members, lengths, q_latent, kv_new.astype(jnp.float32)[:, None, :], kv_cache)


def gate_up_kernel(x_ref, gain_ref, gate_ref, up_ref, out_ref):
    hidden = gate_ref.shape[1]
    x = x_ref[...].astype(jnp.float32)
    square = jnp.sum(x * x, axis=1, keepdims=True)
    scaled = (x * gain_ref[...]).astype(jnp.bfloat16)
    out_ref[:, :hidden] = jnp.dot(
        scaled, gate_ref[...], preferred_element_type=jnp.float32
    ).astype(jnp.bfloat16)
    out_ref[:, hidden : 2 * hidden] = jnp.dot(
        scaled, up_ref[...], preferred_element_type=jnp.float32
    ).astype(jnp.bfloat16)
    high = square.astype(jnp.bfloat16).astype(jnp.float32)
    lane = lax.broadcasted_iota(jnp.int32, (x.shape[0], 128), 1)
    out_ref[:, 2 * hidden :] = jnp.where(lane < 64, high, square - high).astype(jnp.bfloat16)


def gate_up(rows, gain, w_gate, w_up):
    count, width = rows.shape
    hidden = w_gate.shape[1]
    block = 256
    return pl.pallas_call(
        gate_up_kernel,
        grid=(count // block,),
        in_specs=[
            pl.BlockSpec((block, width), lambda i: (i, 0)),
            pl.BlockSpec((1, width), lambda i: (0, 0)),
            pl.BlockSpec((width, hidden), lambda i: (0, 0)),
            pl.BlockSpec((width, hidden), lambda i: (0, 0)),
        ],
        out_specs=pl.BlockSpec((block, 2 * hidden + 128), lambda i: (i, 0)),
        out_shape=jax.ShapeDtypeStruct((count, 2 * hidden + 128), jnp.bfloat16),
        compiler_params=pltpu.CompilerParams(vmem_limit_bytes=VMEM_LIMIT),
        name="gate_up",
    )(rows, gain, w_gate, w_up)


def spread_to(block, axis):
    size = lax.axis_size(axis)
    copies = jnp.broadcast_to(block[None], (size,) + block.shape)
    copies = lax.optimization_barrier(copies)
    landed = lax.all_to_all(copies, axis, split_axis=0, concat_axis=0)
    return landed.reshape((size * block.shape[0],) + block.shape[1:])


def body(
    q_latent,
    kv_new,
    kv_cache,
    lengths,
    members,
    hidden_in,
    w_uv,
    w_o,
    norm_gain,
    w_gate,
    w_up,
    w_down,
):
    groups = lax.axis_size("grp")
    splits = lax.axis_size("tp")
    roles = lax.axis_size("role")
    tokens, heads, kv = q_latent.shape
    latent = w_uv.shape[1]
    value_width = w_uv.shape[2]
    width_dev = w_o.shape[1]
    model_width = width_dev * groups
    hidden = w_gate.shape[1]
    score_scale = (value_width + kv - latent) ** (-0.5)

    context = attend(q_latent, kv_new, kv_cache, lengths, members, score_scale, latent)
    spread = lax.all_to_all(context, "tp", split_axis=1, concat_axis=0, tiled=True)
    values = jnp.einsum("thl,hlv->thv", spread, w_uv, preferred_element_type=jnp.float32)
    values = values.astype(jnp.bfloat16).reshape(spread.shape[0], -1)
    attn_part = jnp.dot(spread_to(values, "grp"), w_o, preferred_element_type=jnp.float32)
    attn_part = attn_part.astype(jnp.bfloat16).reshape(groups, splits, tokens, width_dev)
    landed = lax.all_to_all(attn_part, "tp", split_axis=1, concat_axis=1, tiled=True)
    attn_out = jnp.sum(landed.astype(jnp.float32), axis=1)
    residual = lax.dynamic_index_in_dim(
        hidden_in.reshape(groups, splits, tokens, width_dev),
        lax.axis_index("tp"),
        axis=1,
        keepdims=False,
    )
    stream = (residual.astype(jnp.float32) + attn_out).reshape(groups * tokens, width_dev)

    rows = spread_to(stream.astype(jnp.bfloat16), ("role", "tp"))
    parts = gate_up(rows, norm_gain.astype(jnp.float32)[None], w_gate, w_up)
    per_group = rows.shape[0] // groups
    landed = lax.all_to_all(
        parts.reshape(groups, per_group, -1), "grp", split_axis=0, concat_axis=0
    )
    sums = jnp.sum(landed.astype(jnp.float32), axis=0)
    square = sums[:, 2 * hidden : 2 * hidden + 1] + sums[:, 2 * hidden + 64 : 2 * hidden + 65]
    scale = lax.rsqrt(square / model_width + epsilon)
    activated = (
        jax.nn.silu(sums[:, :hidden] * scale) * (sums[:, hidden : 2 * hidden] * scale)
    ).astype(jnp.bfloat16)

    down_part = jnp.dot(spread_to(activated, "grp"), w_down, preferred_element_type=jnp.float32)
    down_part = down_part.astype(jnp.bfloat16).reshape(
        roles * splits, groups * tokens, width_dev
    )
    landed = lax.all_to_all(down_part, ("role", "tp"), split_axis=0, concat_axis=0)
    down = jnp.sum(landed.astype(jnp.float32), axis=0)
    result = (stream + down).astype(jnp.bfloat16).reshape(groups, tokens, width_dev)
    whole = lax.all_to_all(result, "grp", split_axis=0, concat_axis=2, tiled=True)
    return spread_to(whole.reshape(tokens, model_width), "tp")


def solution(mesh):
    in_specs = (
        P(("role", "grp", "tp"), None, None),
        P(("role", "grp", "tp"), None),
        P(("role", "grp", "tp"), None, None),
        P(("role", "grp", "tp")),
        P(("role", "grp", "tp")),
        P("role", "grp"),
        P("tp", None, None),
        P("tp", "grp"),
        P("grp"),
        P("grp", ("role", "tp")),
        P("grp", ("role", "tp")),
        P(("role", "tp"), "grp"),
    )
    out_specs = P(("role", "grp"), None)
    return jax.shard_map(body, mesh=mesh, in_specs=in_specs, out_specs=out_specs, check_vma=False)
```

```python
import functools

import jax
import jax.numpy as jnp
from jax import lax
from jax.experimental import pallas as pl
from jax.experimental.pallas import tpu as pltpu
from jax.sharding import PartitionSpec as P

epsilon = 1e-06
VMEM_LIMIT = 48 * 1024 * 1024


SHIFTS = (0, 1, -1, 2)
FACING = (0, 2, 1, 3)


def attend_kernel(scale, latent, members_ref, lengths_ref, q_ref, new_ref, kv_ref, out_ref):
    token = pl.program_id(0)
    length = lengths_ref[members_ref[token]]
    queries = q_ref[0]
    cache = kv_ref[0]
    newest = new_ref[0]
    scores = scale * jnp.dot(queries, cache, preferred_element_type=jnp.float32)
    own = scale * jnp.sum(queries.astype(jnp.float32) * newest, axis=1, keepdims=True)
    usable = lax.broadcasted_iota(jnp.int32, scores.shape, 1) < length
    scores = jnp.where(usable, scores, -1e30)
    peak = jnp.maximum(jnp.max(scores, axis=1, keepdims=True), own)
    probs = jnp.exp(scores - peak).astype(jnp.bfloat16)
    self_weight = jnp.exp(own - peak)
    denom = jnp.sum(probs.astype(jnp.float32), axis=1, keepdims=True) + self_weight
    accum = lax.dot_general(
        probs, cache[:latent], (((1,), (1,)), ((), ())), preferred_element_type=jnp.float32
    )
    accum = accum + self_weight * newest[:, :latent]
    out_ref[...] = (accum / denom).astype(out_ref.dtype).reshape(out_ref.shape)


def attend(q_latent, kv_new, kv_cache, lengths, members, scale, latent, splits):
    tokens, heads, kv = q_latent.shape
    ctx = kv_cache.shape[1]
    grid_spec = pltpu.PrefetchScalarGridSpec(
        num_scalar_prefetch=2,
        grid=(tokens,),
        in_specs=[
            pl.BlockSpec((1, heads, kv), lambda t, m, n: (t, 0, 0)),
            pl.BlockSpec((1, 1, kv), lambda t, m, n: (t, 0, 0)),
            pl.BlockSpec((1, kv, ctx), lambda t, m, n: (m[t], 0, 0)),
        ],
        out_specs=pl.BlockSpec((splits, 1, heads // splits, latent), lambda t, m, n: (0, t, 0, 0)),
    )
    return pl.pallas_call(
        functools.partial(attend_kernel, scale, latent),
        grid_spec=grid_spec,
        out_shape=jax.ShapeDtypeStruct((splits, tokens, heads // splits, latent), jnp.bfloat16),
        compiler_params=pltpu.CompilerParams(vmem_limit_bytes=VMEM_LIMIT),
        name="attend",
    )(
        members,
        lengths,
        q_latent,
        kv_new.astype(jnp.float32)[:, None, :],
        jnp.swapaxes(kv_cache, 1, 2),
    )


def gate_up_kernel(
    x_ref, z_ref, gain_ref, gate_ref, up_ref, gate_a_ref, gate_c_ref, up_a_ref, up_c_ref
):
    width = x_ref.shape[-1]
    half = up_a_ref.shape[1]
    gain = gain_ref[...]
    x = x_ref[...].reshape(-1, width).astype(jnp.float32)
    square = jnp.sum(x * x, axis=1, keepdims=True)
    scaled = (x * gain).astype(jnp.bfloat16)
    for out, cols in ((gate_a_ref, slice(0, half)), (gate_c_ref, slice(half, 2 * half))):
        out[:, :half] = jnp.dot(
            scaled, gate_ref[:, cols], preferred_element_type=jnp.float32
        ).astype(jnp.bfloat16)
    high = square.astype(jnp.bfloat16).astype(jnp.float32)
    lane = lax.broadcasted_iota(jnp.int32, (x.shape[0], 128), 1)
    gate_a_ref[:, half:] = jnp.where(lane < 64, high, square - high).astype(jnp.bfloat16)
    scaled = (z_ref[...].reshape(-1, width).astype(jnp.float32) * gain).astype(jnp.bfloat16)
    for out, cols in ((up_a_ref, slice(0, half)), (up_c_ref, slice(half, 2 * half))):
        out[...] = jnp.dot(
            scaled, up_ref[:, cols], preferred_element_type=jnp.float32
        ).astype(jnp.bfloat16)


def gate_up(rows, place, gain, w_gate, w_up):
    _, _, per_group, width = rows.shape
    hidden = w_gate.shape[1]
    half = hidden // 2
    count = 4 * per_group
    whole = lambda i: (0, 0)
    out = lambda cols: jax.ShapeDtypeStruct((count, cols), jnp.bfloat16)
    return pl.pallas_call(
        gate_up_kernel,
        grid=(1,),
        in_specs=[
            pl.BlockSpec((4, 1, per_group, width), lambda i: (0, place, 0, 0)),
            pl.BlockSpec((1, 4, per_group, width), lambda i: (place, 0, 0, 0)),
            pl.BlockSpec((1, width), whole),
            pl.BlockSpec((width, hidden), whole),
            pl.BlockSpec((width, hidden), whole),
        ],
        out_specs=[
            pl.BlockSpec((count, half + 128), whole),
            pl.BlockSpec((count, half), whole),
            pl.BlockSpec((count, half), whole),
            pl.BlockSpec((count, half), whole),
        ],
        out_shape=[out(half + 128), out(half), out(half), out(half)],
        compiler_params=pltpu.CompilerParams(vmem_limit_bytes=VMEM_LIMIT),
        cost_estimate=pl.CostEstimate(
            flops=4 * count * width * hidden,
            bytes_accessed=4 * (width * hidden + count * hidden),
            transcendentals=0,
        ),
        name="gate_up",
    )(rows, rows, gain, w_gate, w_up)


def shift_x(value, shift):
    return lax.ppermute(value, "grp", [(g, (g // 4 + shift) % 4 * 4 + g % 4) for g in range(16)])


def shift_z(value, shift):
    return lax.ppermute(value, "grp", [(g, g // 4 * 4 + (g + shift) % 4) for g in range(16)])


def shift_y(value, shift):
    def moved(place):
        role, tp = place // 4, place % 4
        y = (tp // 2 * 2 + role + shift) % 4
        return y % 2 * 4 + y // 2 * 2 + tp % 2

    return lax.ppermute(value, ("role", "tp"), [(p, moved(p)) for p in range(8)])


def swap_core(value):
    return lax.ppermute(value, "tp", [(t, t ^ 1) for t in range(4)])


def gather(block, shift):
    return jnp.stack([block] + [shift(block, s) for s in SHIFTS[1:]])


def gather_ring(block, shift):
    behind, ahead = shift(block, 1), shift(block, -1)
    middle = block.shape[0] // 2
    far = [shift(behind[:middle], 1), shift(ahead[middle:], -1)]
    return jnp.stack([block, behind, ahead, jnp.concatenate(far)])


def wide(value):
    return value.astype(jnp.float32)


def add(*values):
    return sum(wide(v) for v in values)


def scatter_ring(parts, shift):
    (own_a, own_c), (ahead_a, ahead_c), (behind_a, behind_c), (far_a, far_c) = parts
    far_a, far_c = shift(far_a, 1), shift(far_c, -1)
    direct_c, direct_a = shift(ahead_c, 1), shift(behind_a, -1)
    relay_a = shift(add(ahead_a, far_a).astype(jnp.bfloat16), 1)
    relay_c = shift(add(behind_c, far_c).astype(jnp.bfloat16), -1)
    return add(own_a, relay_a, direct_a), add(own_c, direct_c, relay_c)


def absolute(blocks, place, axis):
    take = lambda i: lax.slice_in_dim(blocks, i, i + 1, axis=axis)
    doubled = jnp.concatenate([take(i) for i in (2, 3, 1, 0, 2, 3, 1)], axis=axis)
    return lax.dynamic_slice_in_dim(doubled, (3 - place) % 4, 4, axis=axis)


def relative(blocks, place, axis):
    doubled = jnp.concatenate([blocks, lax.slice_in_dim(blocks, 0, 3, axis=axis)], axis=axis)
    turned = lax.dynamic_slice_in_dim(doubled, place, 4, axis=axis)
    return jnp.concatenate(
        [lax.slice_in_dim(turned, i, i + 1, axis=axis) for i in (0, 3, 1, 2)], axis=axis
    )


def body(
    q_latent,
    kv_new,
    kv_cache,
    lengths,
    members,
    hidden_in,
    w_uv,
    w_o,
    norm_gain,
    w_gate,
    w_up,
    w_down,
):
    groups = lax.axis_size("grp")
    splits = lax.axis_size("tp")
    place_x, place_z = lax.axis_index("grp") // 4, lax.axis_index("grp") % 4
    tokens, heads, kv = q_latent.shape
    latent = w_uv.shape[1]
    value_width = w_uv.shape[2]
    width = w_o.shape[1]
    model_width = width * groups
    hidden = w_gate.shape[1]
    half = hidden // 2
    score_scale = (value_width + kv - latent) ** (-0.5)

    residual = lax.dynamic_index_in_dim(
        hidden_in.reshape(4, 4, splits, tokens, width), lax.axis_index("tp"), 2, keepdims=False
    )
    residual = wide(relative(relative(residual, place_x, 0), place_z, 1))
    residual = jnp.swapaxes(residual, 0, 1)

    context = attend(q_latent, kv_new, kv_cache, lengths, members, score_scale, latent, splits)
    spread = lax.all_to_all(context, "tp", split_axis=0, concat_axis=0)
    spread = spread.reshape(splits * tokens, heads // splits, latent)
    values = jnp.einsum("thl,hlv->thv", spread, w_uv, preferred_element_type=jnp.float32)
    values = values.astype(jnp.bfloat16).reshape(2, splits * tokens // 2, -1)
    first = gather(gather(values[0], shift_x), shift_z)
    second = gather(gather(values[1], shift_z), shift_x)
    second = jnp.swapaxes(second, 0, 1)
    first, second = (
        jnp.dot(v.reshape(-1, v.shape[-1]), w_o, preferred_element_type=jnp.float32)
        .astype(jnp.bfloat16)
        .reshape(4, 4, splits // 2, tokens, width)
        for v in (first, second)
    )
    attn_part = jnp.concatenate([first, second], axis=2)
    attn_part = jnp.moveaxis(attn_part, 2, 0)
    landed = lax.all_to_all(attn_part, "tp", split_axis=0, concat_axis=0)
    stream = residual + jnp.sum(wide(landed), axis=0)

    rows = gather(stream.astype(jnp.bfloat16), shift_y)
    rows = jnp.stack([rows, swap_core(rows)])
    rows = jnp.transpose(rows, (2, 3, 0, 1, 4, 5)).reshape(4, 4, 8 * tokens, width)
    gain = wide(norm_gain)[None]
    parts = [None] * 4
    for i in (3, 1, 2, 0):
        parts[i] = gate_up(rows, FACING[i], gain, w_gate, w_up)
    gate = scatter_ring([p[:2] for p in parts], shift_x)
    up = scatter_ring([p[2:] for p in parts], shift_z)
    cut = lambda pair: [
        tuple(h.reshape(4, 8 * tokens, -1)[FACING[i]].astype(jnp.bfloat16) for h in pair)
        for i in range(4)
    ]
    gate_a, gate_c = scatter_ring(cut(gate), shift_z)
    up_a, up_c = scatter_ring(cut(up), shift_x)
    square = gate_a[:, half : half + 1] + gate_a[:, half + 64 : half + 65]
    scale = lax.rsqrt(square / model_width + epsilon)
    activated = jnp.concatenate(
        [
            (jax.nn.silu(g * scale) * (u * scale)).astype(jnp.bfloat16)
            for g, u in ((gate_a[:, :half], up_a), (gate_c, up_c))
        ],
        axis=1,
    )

    own_core, other_core = activated[: 4 * tokens], activated[4 * tokens :]
    own_core = gather_ring(gather_ring(own_core, shift_x).reshape(-1, hidden), shift_z)
    other_core = gather_ring(gather_ring(other_core, shift_z).reshape(-1, hidden), shift_x)
    own_core, other_core = (
        jnp.dot(a.reshape(-1, hidden), w_down, preferred_element_type=jnp.float32)
        .astype(jnp.bfloat16)
        .reshape(4, 4, 4, tokens, width)
        for a in (own_core, other_core)
    )
    down = add(own_core, swap_core(jnp.swapaxes(other_core, 0, 1)))
    down = jnp.moveaxis(down, 2, 0)
    total = add(
        stream,
        down[0],
        *(shift_y(down[i].astype(jnp.bfloat16), -SHIFTS[i]) for i in range(1, 4)),
    )
    result = jnp.swapaxes(total.astype(jnp.bfloat16), 0, 1)
    result = absolute(absolute(result, place_x, 0), place_z, 1).reshape(groups, tokens, width)
    whole = lax.all_to_all(result, "grp", split_axis=0, concat_axis=2, tiled=True)
    return lax.all_gather(whole.reshape(tokens, model_width), "tp", axis=0, tiled=True)


def solution(mesh):
    in_specs = (
        P(("role", "grp", "tp"), None, None),
        P(("role", "grp", "tp"), None),
        P(("role", "grp", "tp"), None, None),
        P(("role", "grp", "tp")),
        P(("role", "grp", "tp")),
        P("role", "grp"),
        P("tp", None, None),
        P("tp", "grp"),
        P("grp"),
        P("grp", ("role", "tp")),
        P("grp", ("role", "tp")),
        P(("role", "tp"), "grp"),
    )
    out_specs = P(("role", "grp"), None)
    return jax.shard_map(body, mesh=mesh, in_specs=in_specs, out_specs=out_specs, check_vma=False)
```

```python
import functools

import jax
import jax.numpy as jnp
from jax import lax
from jax.experimental import pallas as pl
from jax.experimental.pallas import tpu as pltpu
from jax.sharding import PartitionSpec as P

epsilon = 1e-06
VMEM_LIMIT = 48 * 1024 * 1024


SHIFTS = (0, 1, -1, 2)
FACING = (0, 2, 1, 3)


def attend_kernel(scale, latent, members_ref, lengths_ref, q_ref, new_ref, kv_ref, out_ref):
    token = pl.program_id(0)
    length = lengths_ref[members_ref[token]]
    queries = q_ref[0]
    cache = kv_ref[0]
    newest = new_ref[0]
    scores = scale * jnp.dot(queries, cache, preferred_element_type=jnp.float32)
    own = scale * jnp.sum(queries.astype(jnp.float32) * newest, axis=1, keepdims=True)
    usable = lax.broadcasted_iota(jnp.int32, scores.shape, 1) < length
    scores = jnp.where(usable, scores, -1e30)
    peak = jnp.maximum(jnp.max(scores, axis=1, keepdims=True), own)
    probs = jnp.exp(scores - peak).astype(jnp.bfloat16)
    self_weight = jnp.exp(own - peak)
    denom = jnp.sum(probs.astype(jnp.float32), axis=1, keepdims=True) + self_weight
    accum = lax.dot_general(
        probs, cache[:latent], (((1,), (1,)), ((), ())), preferred_element_type=jnp.float32
    )
    accum = accum + self_weight * newest[:, :latent]
    out_ref[...] = (accum / denom).astype(out_ref.dtype).reshape(out_ref.shape)


def attend(q_latent, kv_new, kv_cache, lengths, members, scale, latent, splits):
    tokens, heads, kv = q_latent.shape
    ctx = kv_cache.shape[1]
    grid_spec = pltpu.PrefetchScalarGridSpec(
        num_scalar_prefetch=2,
        grid=(tokens,),
        in_specs=[
            pl.BlockSpec((1, heads, kv), lambda t, m, n: (t, 0, 0)),
            pl.BlockSpec((1, 1, kv), lambda t, m, n: (t, 0, 0)),
            pl.BlockSpec((1, kv, ctx), lambda t, m, n: (m[t], 0, 0)),
        ],
        out_specs=pl.BlockSpec((splits, 1, heads // splits, latent), lambda t, m, n: (0, t, 0, 0)),
    )
    return pl.pallas_call(
        functools.partial(attend_kernel, scale, latent),
        grid_spec=grid_spec,
        out_shape=jax.ShapeDtypeStruct((splits, tokens, heads // splits, latent), jnp.bfloat16),
        compiler_params=pltpu.CompilerParams(vmem_limit_bytes=VMEM_LIMIT),
        name="attend",
    )(
        members,
        lengths,
        q_latent,
        kv_new.astype(jnp.float32)[:, None, :],
        jnp.swapaxes(kv_cache, 1, 2),
    )


def partial_kernel(jobs, squares, half, *refs):
    count = 1 + max(rows for pieces in jobs for rows, _ in pieces)
    row_refs, gain_ref, weight_ref, outs = (
        refs[:count],
        refs[count],
        refs[count + 1],
        refs[count + 2 :],
    )
    gain = gain_ref[...]
    ready = []
    for ref in row_refs:
        x = ref[...].reshape(-1, ref.shape[-1]).astype(jnp.float32)
        ready.append(((x * gain).astype(jnp.bfloat16), jnp.sum(x * x, axis=1, keepdims=True)))
    for pieces, out in zip(jobs, outs):
        start = 0
        for rows, side in pieces:
            scaled, square = ready[rows]
            out[:, start : start + half] = jnp.dot(
                scaled,
                weight_ref[:, side * half : (side + 1) * half],
                preferred_element_type=jnp.float32,
            ).astype(jnp.bfloat16)
            start += half
            if squares and side == 0:
                high = square.astype(jnp.bfloat16).astype(jnp.float32)
                lane = lax.broadcasted_iota(jnp.int32, (scaled.shape[0], 128), 1)
                out[:, start : start + 128] = jnp.where(lane < 64, high, square - high).astype(
                    jnp.bfloat16
                )
                start += 128


def partial_sums(rows, axis, places, gain, weight, jobs, squares):
    _, _, per_group, width = rows.shape
    hidden = weight.shape[1]
    half = hidden // 2
    count = 4 * per_group
    whole = lambda i: (0, 0)
    block = (4, 1, per_group, width) if axis == 1 else (1, 4, per_group, width)

    def at(place):
        return lambda i: (0, place, 0, 0) if axis == 1 else (place, 0, 0, 0)

    widths = [
        sum(half + (128 if squares and side == 0 else 0) for _, side in pieces) for pieces in jobs
    ]
    return pl.pallas_call(
        functools.partial(partial_kernel, jobs, squares, half),
        grid=(1,),
        in_specs=[pl.BlockSpec(block, at(p)) for p in places]
        + [pl.BlockSpec((1, width), whole), pl.BlockSpec((width, hidden), whole)],
        out_specs=[pl.BlockSpec((count, w), whole) for w in widths],
        out_shape=[jax.ShapeDtypeStruct((count, w), jnp.bfloat16) for w in widths],
        compiler_params=pltpu.CompilerParams(vmem_limit_bytes=VMEM_LIMIT),
        cost_estimate=pl.CostEstimate(
            flops=2 * count * width * sum(widths),
            bytes_accessed=2 * (width * hidden + count * sum(widths)),
            transcendentals=0,
        ),
        name="partial_sums",
    )(*([rows] * len(places)), gain, weight)


def scatter_step(plus, minus, ahead_a, behind_c, shift):
    wide_a, wide_c = ahead_a.shape[1], behind_c.shape[1]
    plus, minus = shift(plus, 1), shift(minus, -1)
    relay_a = shift(add(ahead_a, plus[:, :wide_a]).astype(jnp.bfloat16), 1)
    relay_c = shift(add(behind_c, minus[:, :wide_c]).astype(jnp.bfloat16), -1)
    return plus, minus, relay_a, relay_c


def merge_kernel(
    own_a, own_c, plus, minus, relay_a, relay_c, plus2, minus2, ahead_a2, behind_c2, own_a2, own_c2
):
    wide_a, wide_c = own_a.shape[1], own_c.shape[1]
    rows = plus2.shape[0]
    for place, outs_a, outs_c in (
        (3, (plus2, 0), (minus2, 0)),
        (FACING[1], (ahead_a2, 0), (plus2, wide_a)),
        (FACING[2], (minus2, wide_c), (behind_c2, 0)),
        (0, (own_a2, 0), (own_c2, 0)),
    ):
        part = pl.ds(place * rows, rows)
        total = wide(own_a[part, :]) + wide(relay_a[part, :]) + wide(minus[part, wide_c:])
        outs_a[0][:, outs_a[1] : outs_a[1] + wide_a] = total.astype(jnp.bfloat16)
        total = wide(own_c[part, :]) + wide(relay_c[part, :]) + wide(plus[part, wide_a:])
        outs_c[0][:, outs_c[1] : outs_c[1] + wide_c] = total.astype(jnp.bfloat16)


def merge(own_a, own_c, plus, minus, relay_a, relay_c):
    rows = own_a.shape[0] // 4
    a, c = own_a.shape[1], own_c.shape[1]
    operands = (own_a, own_c, plus, minus, relay_a, relay_c)
    widths = (a + c, a + c, a, c, a, c)
    return pl.pallas_call(
        merge_kernel,
        out_shape=[jax.ShapeDtypeStruct((rows, w), jnp.bfloat16) for w in widths],
        in_specs=[pl.BlockSpec(memory_space=pltpu.VMEM)] * 6,
        out_specs=[pl.BlockSpec(memory_space=pltpu.VMEM)] * 6,
        compiler_params=pltpu.CompilerParams(vmem_limit_bytes=VMEM_LIMIT),
        cost_estimate=pl.CostEstimate(
            flops=12 * rows * (a + c), bytes_accessed=32 * rows * (a + c), transcendentals=0
        ),
        name="merge",
    )(*operands)


def shift_x(value, shift):
    return lax.ppermute(value, "grp", [(g, (g // 4 + shift) % 4 * 4 + g % 4) for g in range(16)])


def shift_z(value, shift):
    return lax.ppermute(value, "grp", [(g, g // 4 * 4 + (g + shift) % 4) for g in range(16)])


def shift_y(value, shift):
    def moved(place):
        role, tp = place // 4, place % 4
        y = (tp // 2 * 2 + role + shift) % 4
        return y % 2 * 4 + y // 2 * 2 + tp % 2

    return lax.ppermute(value, ("role", "tp"), [(p, moved(p)) for p in range(8)])


def swap_core(value):
    return lax.ppermute(value, "tp", [(t, t ^ 1) for t in range(4)])


def gather(block, shift):
    return jnp.stack([block] + [shift(block, s) for s in SHIFTS[1:]])


def gather_ring(block, shift):
    behind, ahead = shift(block, 1), shift(block, -1)
    middle = block.shape[0] // 2
    far = [shift(behind[:middle], 1), shift(ahead[middle:], -1)]
    return jnp.stack([block, behind, ahead, jnp.concatenate(far)])


def wide(value):
    return value.astype(jnp.float32)


def add(*values):
    return sum(wide(v) for v in values)


def absolute(blocks, place, axis):
    take = lambda i: lax.slice_in_dim(blocks, i, i + 1, axis=axis)
    doubled = jnp.concatenate([take(i) for i in (2, 3, 1, 0, 2, 3, 1)], axis=axis)
    return lax.dynamic_slice_in_dim(doubled, (3 - place) % 4, 4, axis=axis)


def relative(blocks, place, axis):
    doubled = jnp.concatenate([blocks, lax.slice_in_dim(blocks, 0, 3, axis=axis)], axis=axis)
    turned = lax.dynamic_slice_in_dim(doubled, place, 4, axis=axis)
    return jnp.concatenate(
        [lax.slice_in_dim(turned, i, i + 1, axis=axis) for i in (0, 3, 1, 2)], axis=axis
    )


def body(
    q_latent,
    kv_new,
    kv_cache,
    lengths,
    members,
    hidden_in,
    w_uv,
    w_o,
    norm_gain,
    w_gate,
    w_up,
    w_down,
):
    groups = lax.axis_size("grp")
    splits = lax.axis_size("tp")
    place_x, place_z = lax.axis_index("grp") // 4, lax.axis_index("grp") % 4
    tokens, heads, kv = q_latent.shape
    latent = w_uv.shape[1]
    value_width = w_uv.shape[2]
    width = w_o.shape[1]
    model_width = width * groups
    hidden = w_gate.shape[1]
    half = hidden // 2
    score_scale = (value_width + kv - latent) ** (-0.5)

    core = lax.axis_index("tp") % 2
    residual = lax.dynamic_index_in_dim(
        hidden_in.reshape(4, 4, 2, 2, tokens, width), core, 3, keepdims=False
    )
    residual = wide(relative(relative(residual, place_x, 0), place_z, 1))
    residual = jnp.swapaxes(residual, 0, 1)

    context = attend(q_latent, kv_new, kv_cache, lengths, members, score_scale, latent, splits)
    spread = lax.all_to_all(context, "tp", split_axis=0, concat_axis=0)
    spread = spread.reshape(splits * tokens, heads // splits, latent)
    values = jnp.einsum("thl,hlv->thv", spread, w_uv, preferred_element_type=jnp.float32)
    values = values.astype(jnp.bfloat16).reshape(2, splits * tokens // 2, -1)
    first = gather(gather(values[0], shift_x), shift_z)
    second = gather(gather(values[1], shift_z), shift_x)
    second = jnp.swapaxes(second, 0, 1)
    first, second = (
        jnp.dot(v.reshape(-1, v.shape[-1]), w_o, preferred_element_type=jnp.float32).reshape(
            4, 4, 2, tokens, width
        )
        for v in (first, second)
    )
    attn_part = jnp.stack([first, second], axis=2)
    mine = jnp.where(core == 0, attn_part[:, :, :, 0], attn_part[:, :, :, 1])
    theirs = jnp.where(core == 0, attn_part[:, :, :, 1], attn_part[:, :, :, 0])
    shared = 0.5 * residual + mine + wide(swap_core(theirs.astype(jnp.bfloat16)))
    sent = shared.astype(jnp.bfloat16)
    behind, ahead, far = (shift_y(sent, s) for s in SHIFTS[1:])
    stream = shared + wide(far)
    rows = jnp.stack([stream, add(behind, ahead)]).astype(jnp.bfloat16)
    rows = jnp.stack([rows, swap_core(rows)])
    rows = jnp.transpose(rows, (2, 3, 0, 1, 4, 5, 6)).reshape(4, 4, 8 * tokens, width)

    gain = wide(norm_gain)[None]
    places = (3, FACING[1], FACING[2])
    sends = (((0, 0), (1, 1)), ((0, 1), (2, 0)))
    gate_sends = partial_sums(rows, 1, places, gain, w_gate, sends, True)
    up_sends = partial_sums(rows, 0, places, gain, w_up, sends, False)
    places = (FACING[1], FACING[2], 0)
    rest = (((0, 0),), ((1, 1),), ((2, 0),), ((2, 1),))
    gate_rest = partial_sums(rows, 1, places, gain, w_gate, rest, True)
    up_rest = partial_sums(rows, 0, places, gain, w_up, rest, False)
    gate = scatter_step(*gate_sends, *gate_rest[:2], shift_x)
    up = scatter_step(*up_sends, *up_rest[:2], shift_z)
    gate = merge(*gate_rest[2:], *gate)
    up = merge(*up_rest[2:], *up)
    sums = []
    for whole, shift in ((gate, shift_z), (up, shift_x)):
        plus, minus, relay_a, relay_c = scatter_step(*whole[:4], shift)
        own_a, own_c = whole[4:]
        sums.append(add(own_a, relay_a, minus[:, own_c.shape[1] :]))
        sums.append(add(own_c, relay_c, plus[:, own_a.shape[1] :]))
    gate_a, gate_c, up_a, up_c = sums
    square = gate_a[:, half : half + 1] + gate_a[:, half + 64 : half + 65]
    scale = lax.rsqrt(square / model_width + epsilon)
    activated = jnp.concatenate(
        [
            (jax.nn.silu(g * scale) * (u * scale)).astype(jnp.bfloat16)
            for g, u in ((gate_a[:, :half], up_a), (gate_c, up_c))
        ],
        axis=1,
    )

    own_core, other_core = activated[: 4 * tokens], activated[4 * tokens :]
    own_core = gather_ring(gather_ring(own_core, shift_x).reshape(-1, hidden), shift_z)
    other_core = gather_ring(gather_ring(other_core, shift_z).reshape(-1, hidden), shift_x)
    own_core, other_core = (
        jnp.dot(a.reshape(-1, hidden), w_down, preferred_element_type=jnp.float32)
        .astype(jnp.bfloat16)
        .reshape(4, 4, 4, tokens, width)
        for a in (own_core, other_core)
    )
    down = add(own_core, swap_core(jnp.swapaxes(other_core, 0, 1)))
    down = down.reshape(4, 4, 2, 2, tokens, width)
    near = down[:, :, 1].astype(jnp.bfloat16)
    total = add(
        stream,
        down[:, :, 0],
        shift_y(near, 1),
        shift_y(near, -1),
        shift_y(down[:, :, 0].astype(jnp.bfloat16), 2),
    )
    result = jnp.swapaxes(total.astype(jnp.bfloat16), 0, 1)
    result = absolute(absolute(result, place_x, 0), place_z, 1)
    result = result.reshape(groups, 2 * tokens, width)
    whole = lax.all_to_all(result, "grp", split_axis=0, concat_axis=2, tiled=True)
    whole = whole.reshape(2, tokens, model_width)
    other = swap_core(whole)
    whole = jnp.stack(
        [jnp.where(core == 0, whole, other), jnp.where(core == 0, other, whole)], axis=1
    )
    return whole.reshape(splits * tokens, model_width)


def solution(mesh):
    in_specs = (
        P(("role", "grp", "tp"), None, None),
        P(("role", "grp", "tp"), None),
        P(("role", "grp", "tp"), None, None),
        P(("role", "grp", "tp")),
        P(("role", "grp", "tp")),
        P("role", "grp"),
        P("tp", None, None),
        P("tp", "grp"),
        P("grp"),
        P("grp", ("role", "tp")),
        P("grp", ("role", "tp")),
        P(("role", "tp"), "grp"),
    )
    out_specs = P(("role", "grp"), None)
    return jax.shard_map(body, mesh=mesh, in_specs=in_specs, out_specs=out_specs, check_vma=False)
```

```python
import functools

import jax
import jax.numpy as jnp
from jax import lax
from jax.experimental import pallas as pl
from jax.experimental.pallas import tpu as pltpu
from jax.sharding import Mesh
from jax.sharding import PartitionSpec as P

epsilon = 1e-06
VMEM_LIMIT = 48 * 1024 * 1024


SHIFTS = (0, 1, -1, 2)
FACING = (0, 2, 1, 3)


def attend_kernel(
    scale, latent, members_ref, lengths_ref, place_ref, q_ref, new_ref, kv_ref, near_ref, far_ref
):
    token = pl.program_id(0)
    length = lengths_ref[members_ref[token]]
    place = place_ref[0]
    queries = jnp.concatenate([q_ref[0, place ^ i] for i in range(4)], axis=0)
    cache = kv_ref[0]
    newest = new_ref[0]
    scores = scale * jnp.dot(queries, cache, preferred_element_type=jnp.float32)
    own = scale * jnp.sum(queries.astype(jnp.float32) * newest, axis=1, keepdims=True)
    usable = lax.broadcasted_iota(jnp.int32, scores.shape, 1) < length
    scores = jnp.where(usable, scores, -1e30)
    peak = jnp.maximum(jnp.max(scores, axis=1, keepdims=True), own)
    probs = jnp.exp(scores - peak).astype(jnp.bfloat16)
    self_weight = jnp.exp(own - peak)
    denom = jnp.sum(probs.astype(jnp.float32), axis=1, keepdims=True) + self_weight
    accum = lax.dot_general(
        probs, cache[:latent], (((1,), (1,)), ((), ())), preferred_element_type=jnp.float32
    )
    accum = accum + self_weight * newest[:, :latent]
    context = (accum / denom).astype(near_ref.dtype)
    half = context.shape[0] // 2
    near_ref[...] = context[:half].reshape(near_ref.shape)
    far_ref[...] = context[half:].reshape(far_ref.shape)


def attend(q_latent, kv_new, kv_cache, lengths, members, place, scale, latent):
    tokens, heads, kv = q_latent.shape
    ctx = kv_cache.shape[1]
    block = heads // 4
    grid_spec = pltpu.PrefetchScalarGridSpec(
        num_scalar_prefetch=3,
        grid=(tokens,),
        in_specs=[
            pl.BlockSpec((1, 4, block, kv), lambda t, m, n, p: (t, 0, 0, 0)),
            pl.BlockSpec((1, 1, kv), lambda t, m, n, p: (t, 0, 0)),
            pl.BlockSpec((1, kv, ctx), lambda t, m, n, p: (m[t], 0, 0)),
        ],
        out_specs=[pl.BlockSpec((2, 1, block, latent), lambda t, m, n, p: (0, t, 0, 0))] * 2,
    )
    return pl.pallas_call(
        functools.partial(attend_kernel, scale, latent),
        grid_spec=grid_spec,
        out_shape=[jax.ShapeDtypeStruct((2, tokens, block, latent), jnp.bfloat16)] * 2,
        compiler_params=pltpu.CompilerParams(vmem_limit_bytes=VMEM_LIMIT),
        cost_estimate=pl.CostEstimate(
            flops=2 * tokens * heads * ctx * (kv + latent),
            bytes_accessed=2 * tokens * ctx * kv,
            transcendentals=tokens * heads * ctx,
        ),
        name="attend",
    )(
        members,
        lengths,
        place,
        q_latent.reshape(tokens, 4, block, kv),
        kv_new.astype(jnp.float32)[:, None, :],
        jnp.swapaxes(kv_cache, 1, 2),
    )


def partial_kernel(jobs, *refs):
    count = 1 + max(rows for pieces in jobs for rows, _ in pieces)
    row_refs, gain_ref, weight_refs, outs = (
        refs[:count],
        refs[count],
        refs[count + 1 : count + 3],
        refs[count + 3 :],
    )
    half = weight_refs[0].shape[1]
    gain = gain_ref[...]
    ready = []
    for ref in row_refs:
        x = ref[...].reshape(-1, ref.shape[-1]).astype(jnp.float32)
        ready.append(((x * gain).astype(jnp.bfloat16), jnp.sum(x * x, axis=1, keepdims=True)))
    for pieces, out in zip(jobs, outs):
        start = 0
        for rows, side in pieces:
            scaled, square = ready[rows]
            out[:, start : start + half] = jnp.dot(
                scaled, weight_refs[side][...], preferred_element_type=jnp.float32
            ).astype(jnp.bfloat16)
            start += half
            if side == 0:
                high = square.astype(jnp.bfloat16).astype(jnp.float32)
                lane = lax.broadcasted_iota(jnp.int32, (scaled.shape[0], 128), 1)
                out[:, start : start + 128] = jnp.where(lane < 64, high, square - high).astype(
                    jnp.bfloat16
                )
                start += 128


def partial_sums(rows, places, gain, weights, jobs):
    _, _, per_group, width = rows.shape
    half = weights[0].shape[1]
    count = 4 * per_group
    whole = lambda i: (0, 0)

    def at(place):
        return lambda i: (0, place, 0, 0)

    widths = [sum(half + (128 if side == 0 else 0) for _, side in pieces) for pieces in jobs]
    return pl.pallas_call(
        functools.partial(partial_kernel, jobs),
        grid=(1,),
        in_specs=[pl.BlockSpec((4, 1, per_group, width), at(p)) for p in places]
        + [pl.BlockSpec((1, width), whole)]
        + [pl.BlockSpec((width, half), whole)] * 2,
        out_specs=[pl.BlockSpec((count, w), whole) for w in widths],
        out_shape=[jax.ShapeDtypeStruct((count, w), jnp.bfloat16) for w in widths],
        compiler_params=pltpu.CompilerParams(vmem_limit_bytes=VMEM_LIMIT),
        cost_estimate=pl.CostEstimate(
            flops=2 * count * width * sum(widths),
            bytes_accessed=2 * (2 * width * half + count * sum(widths)),
            transcendentals=0,
        ),
        name="partial_sums",
    )(*([rows] * len(places)), gain, *weights)


def merge_kernel(own_a, own_c, plus, minus, relay_a, relay_c, *outs):
    wide_a, wide_c = own_a.shape[1], own_c.shape[1]
    rows = outs[0].shape[0]
    for out, place in zip(outs, FACING):
        part = pl.ds(place * rows, rows)
        total = wide(own_a[part, :]) + wide(relay_a[part, :]) + wide(minus[part, wide_c:])
        out[:, :wide_a] = total.astype(jnp.bfloat16)
        total = wide(own_c[part, :]) + wide(relay_c[part, :]) + wide(plus[part, wide_a:])
        out[:, wide_a:] = total.astype(jnp.bfloat16)


def merge(*operands):
    own_a, own_c = operands[:2]
    rows = own_a.shape[0] // 4
    cols = own_a.shape[1] + own_c.shape[1]
    return pl.pallas_call(
        merge_kernel,
        out_shape=[jax.ShapeDtypeStruct((rows, cols), jnp.bfloat16)] * 4,
        in_specs=[pl.BlockSpec(memory_space=pltpu.VMEM)] * 6,
        out_specs=[pl.BlockSpec(memory_space=pltpu.VMEM)] * 4,
        compiler_params=pltpu.CompilerParams(vmem_limit_bytes=VMEM_LIMIT),
        cost_estimate=pl.CostEstimate(
            flops=12 * rows * cols, bytes_accessed=32 * rows * cols, transcendentals=0
        ),
        name="merge",
    )(*operands)


def ring(first):
    def shift(value, by):
        pairs = []
        for g in range(16):
            for tp in range(4):
                x, z = g // 4, g % 4
                if (tp % 2 == 0) == first:
                    x = (x + by) % 4
                else:
                    z = (z + by) % 4
                pairs.append((g * 4 + tp, (x * 4 + z) * 4 + tp))
        return lax.ppermute(value, ("grp", "yh", "core"), pairs)

    return shift


shift_1, shift_2 = ring(True), ring(False)


def shift_y(value, by):
    def moved(place):
        role, yh, core = place // 4, place // 2 % 2, place % 2
        y = (yh * 2 + role + by) % 4
        return y % 2 * 4 + y // 2 * 2 + core

    return lax.ppermute(value, ("role", "yh", "core"), [(p, moved(p)) for p in range(8)])


def swap(value, axis):
    return lax.ppermute(value, axis, [(0, 1), (1, 0)])


def gather(block, shift):
    return jnp.stack([block] + [shift(block, s) for s in SHIFTS[1:]])


def gather_ring(block, shift):
    behind, ahead = shift(block, 1), shift(block, -1)
    middle = block.shape[0] // 2
    far = [shift(behind[:middle], 1), shift(ahead[middle:], -1)]
    return jnp.stack([block, behind, ahead, jnp.concatenate(far)])


def wide(value):
    return value.astype(jnp.float32)


def add(*values):
    return sum(wide(v) for v in values)


def scatter_step(plus, minus, ahead_a, behind_c, shift):
    wide_a, wide_c = ahead_a.shape[1], behind_c.shape[1]
    plus, minus = shift(plus, 1), shift(minus, -1)
    relay_a = shift(add(ahead_a, plus[:, :wide_a]).astype(jnp.bfloat16), 1)
    relay_c = shift(add(behind_c, minus[:, :wide_c]).astype(jnp.bfloat16), -1)
    return plus, minus, relay_a, relay_c


def absolute(blocks, place, axis):
    take = lambda i: lax.slice_in_dim(blocks, i, i + 1, axis=axis)
    doubled = jnp.concatenate([take(i) for i in (2, 3, 1, 0, 2, 3, 1)], axis=axis)
    return lax.dynamic_slice_in_dim(doubled, (3 - place) % 4, 4, axis=axis)


def relative(blocks, place, axis):
    doubled = jnp.concatenate([blocks, lax.slice_in_dim(blocks, 0, 3, axis=axis)], axis=axis)
    turned = lax.dynamic_slice_in_dim(doubled, place, 4, axis=axis)
    return jnp.concatenate(
        [lax.slice_in_dim(turned, i, i + 1, axis=axis) for i in (0, 3, 1, 2)], axis=axis
    )


def body(
    q_latent,
    kv_new,
    kv_cache,
    lengths,
    members,
    hidden_in,
    w_uv,
    w_o,
    norm_gain,
    w_gate,
    w_up,
    w_down,
):
    groups = lax.axis_size("grp")
    place_x, place_z = lax.axis_index("grp") // 4, lax.axis_index("grp") % 4
    core, yh = lax.axis_index("core"), lax.axis_index("yh")
    place_1 = jnp.where(core == 0, place_x, place_z)
    place_2 = jnp.where(core == 0, place_z, place_x)
    tokens, heads, kv = q_latent.shape
    latent = w_uv.shape[1]
    value_width = w_uv.shape[2]
    width = w_o.shape[1]
    model_width = width * groups
    hidden = w_gate.shape[1]
    score_scale = (value_width + kv - latent) ** (-0.5)

    uv_pair = (w_uv, swap(w_uv, "core"))
    o_pair = (w_o, swap(w_o, "core"))
    down_pair = (w_down, swap(w_down, "core"))
    in_pair = (
        jnp.where(core == 0, w_gate, w_up),
        swap(jnp.where(core == 0, w_up, w_gate), "core"),
    )

    residual = lax.dynamic_index_in_dim(
        hidden_in.reshape(4, 4, 2, 2, tokens, width), core, 3, keepdims=False
    )
    residual = jnp.where(core == 0, jnp.swapaxes(residual, 0, 1), residual)
    residual = wide(relative(relative(residual, place_2, 0), place_1, 1))

    near, far = attend(
        q_latent,
        kv_new,
        kv_cache,
        lengths,
        members,
        (2 * yh + core).astype(jnp.int32)[None],
        score_scale,
        latent,
    )
    far = swap(far, "yh")
    context = jnp.stack([jnp.where(yh == 0, near, far), jnp.where(yh == 0, far, near)], axis=1)
    context = context.reshape(2, 2 * tokens, heads // 4, latent)
    values = jnp.concatenate(
        [
            jnp.einsum("thl,hlv->thv", c, w, preferred_element_type=jnp.float32)
            .astype(jnp.bfloat16)
            .reshape(2 * tokens, -1)
            for c, w in zip(context, uv_pair)
        ],
        axis=1,
    )
    values = gather(gather(values, shift_1), shift_2)
    values = values.reshape(groups * 2 * tokens, 2, -1)
    attn_part = sum(
        jnp.dot(values[:, i], o_pair[i], preferred_element_type=jnp.float32) for i in range(2)
    ).reshape(4, 4, 2, tokens, width)
    shared = 0.5 * residual + attn_part
    sent = shared.astype(jnp.bfloat16)
    behind, ahead, across = (shift_y(sent, s) for s in SHIFTS[1:])
    stream = shared + wide(across)
    rows = jnp.stack([stream, add(behind, ahead)]).astype(jnp.bfloat16)
    rows = jnp.stack([rows, jnp.swapaxes(swap(rows, "core"), 1, 2)])
    rows = jnp.transpose(rows, (2, 3, 0, 1, 4, 5, 6)).reshape(4, 4, 8 * tokens, width)

    gain = wide(norm_gain)[None]
    places = (3, FACING[1], FACING[2])
    (plus,) = partial_sums(rows, places[:2], gain, in_pair, (((0, 0), (1, 1)),))
    (minus,) = partial_sums(rows, places[::2], gain, in_pair, (((0, 1), (1, 0)),))
    places = (FACING[1], FACING[2], 0)
    rest = (((0, 0),), ((1, 1),), ((2, 0),), ((2, 1),))
    ahead_a, behind_c, own_a, own_c = partial_sums(rows, places, gain, in_pair, rest)
    arrived = scatter_step(plus, minus, ahead_a, behind_c, shift_1)
    blocks = merge(own_a, own_c, *arrived)
    sums = add(blocks[0], *(shift_2(blocks[i], SHIFTS[i]) for i in range(1, 4)))
    square = sums[:, hidden : hidden + 1] + sums[:, hidden + 64 : hidden + 65]
    scale = lax.rsqrt(square / model_width + epsilon)
    sums = [sums[:, :hidden] * scale, sums[:, hidden + 128 :] * scale]
    own = [s[: 4 * tokens] for s in sums]
    other = swap(
        jnp.concatenate([s[4 * tokens :].astype(jnp.bfloat16) for s in sums], axis=1), "core"
    )
    other = [wide(other[:, hidden:]), wide(other[:, :hidden])]
    activated = jnp.concatenate(
        [
            (jax.nn.silu(jnp.where(core == 0, a, b)) * jnp.where(core == 0, b, a)).astype(
                jnp.bfloat16
            )
            for a, b in zip(own, other)
        ],
        axis=1,
    )

    activated = gather(activated, shift_1).reshape(-1, 2 * hidden)
    activated = gather_ring(activated, shift_2).reshape(-1, 2, hidden)
    down = sum(
        jnp.dot(activated[:, i], down_pair[i], preferred_element_type=jnp.float32)
        for i in range(2)
    ).reshape(4, 4, 2, 2, tokens, width)
    at_home = jnp.arange(2)[None, None, :, None, None] == yh
    down = jnp.stack([down[:, :, 0] + jnp.where(at_home, stream, 0.0), down[:, :, 1]])
    down = down.astype(jnp.bfloat16)
    down = absolute(absolute(down, place_2, 1), place_1, 2)
    down = jnp.where(core == 0, jnp.swapaxes(down, 1, 2), down)
    role = lax.axis_index("role")
    down = jnp.where(role == 0, down, down[::-1])
    down = down.reshape(2 * groups * 2, tokens, width)
    landed = lax.all_to_all(down, ("role", "grp", "yh"), split_axis=0, concat_axis=0)
    landed = landed.reshape(2, groups, 2, tokens, width)
    result = jnp.sum(wide(landed), axis=(0, 2)).astype(jnp.bfloat16)
    result = jnp.swapaxes(result, 0, 1).reshape(tokens, model_width)
    return lax.all_gather(result, ("yh", "core"), axis=0, tiled=True)


def solution(mesh):
    tp = ("yh", "core")
    in_specs = (
        P(("role", "grp") + tp, None, None),
        P(("role", "grp") + tp, None),
        P(("role", "grp") + tp, None, None),
        P(("role", "grp") + tp),
        P(("role", "grp") + tp),
        P("role", "grp"),
        P(tp, None, None),
        P(tp, "grp"),
        P("grp"),
        P("grp", ("role",) + tp),
        P("grp", ("role",) + tp),
        P(("role",) + tp, "grp"),
    )
    out_specs = P(("role", "grp"), None)
    sizes = dict(mesh.shape)
    split_mesh = Mesh(
        mesh.devices.reshape(sizes["role"], sizes["grp"], 2, 2), ("role", "grp", "yh", "core")
    )
    return jax.shard_map(
        body, mesh=split_mesh, in_specs=in_specs, out_specs=out_specs, check_vma=False
    )
```

```python
import functools

import jax
import jax.numpy as jnp
from jax import lax
from jax.experimental import pallas as pl
from jax.experimental.pallas import tpu as pltpu
from jax.sharding import Mesh
from jax.sharding import PartitionSpec as P

epsilon = 1e-06
VMEM_LIMIT = 20 * 1024 * 1024


SHIFTS = (0, 1, -1, 2)
FACING = (0, 2, 1, 3)


def attend_kernel(
    scale, latent, members_ref, lengths_ref, place_ref, q_ref, new_ref, kv_ref, near_ref, far_ref
):
    token = pl.program_id(0)
    length = lengths_ref[members_ref[token]]
    place = place_ref[0]
    queries = jnp.concatenate([q_ref[0, place ^ i] for i in range(4)], axis=0)
    cache = kv_ref[0]
    newest = new_ref[0]
    scores = scale * jnp.dot(queries, cache, preferred_element_type=jnp.float32)
    own = scale * jnp.sum(queries.astype(jnp.float32) * newest, axis=1, keepdims=True)
    usable = lax.broadcasted_iota(jnp.int32, scores.shape, 1) < length
    scores = jnp.where(usable, scores, -1e30)
    peak = jnp.maximum(jnp.max(scores, axis=1, keepdims=True), own)
    probs = jnp.exp(scores - peak).astype(jnp.bfloat16)
    self_weight = jnp.exp(own - peak)
    denom = jnp.sum(probs.astype(jnp.float32), axis=1, keepdims=True) + self_weight
    accum = lax.dot_general(
        probs, cache[:latent], (((1,), (1,)), ((), ())), preferred_element_type=jnp.float32
    )
    accum = accum + self_weight * newest[:, :latent]
    context = (accum / denom).astype(near_ref.dtype)
    half = context.shape[0] // 2
    near_ref[...] = context[:half].reshape(near_ref.shape)
    far_ref[...] = context[half:].reshape(far_ref.shape)


def attend(q_latent, kv_new, kv_cache, lengths, members, place, scale, latent):
    tokens, heads, kv = q_latent.shape
    ctx = kv_cache.shape[1]
    block = heads // 4
    grid_spec = pltpu.PrefetchScalarGridSpec(
        num_scalar_prefetch=3,
        grid=(tokens,),
        in_specs=[
            pl.BlockSpec((1, 4, block, kv), lambda t, m, n, p: (t, 0, 0, 0)),
            pl.BlockSpec((1, 1, kv), lambda t, m, n, p: (t, 0, 0)),
            pl.BlockSpec((1, kv, ctx), lambda t, m, n, p: (m[t], 0, 0)),
        ],
        out_specs=[pl.BlockSpec((2, 1, block, latent), lambda t, m, n, p: (0, t, 0, 0))] * 2,
    )
    return pl.pallas_call(
        functools.partial(attend_kernel, scale, latent),
        grid_spec=grid_spec,
        out_shape=[jax.ShapeDtypeStruct((2, tokens, block, latent), jnp.bfloat16)] * 2,
        compiler_params=pltpu.CompilerParams(vmem_limit_bytes=VMEM_LIMIT),
        cost_estimate=pl.CostEstimate(
            flops=2 * tokens * heads * ctx * (kv + latent),
            bytes_accessed=2 * tokens * ctx * kv,
            transcendentals=tokens * heads * ctx,
        ),
        name="attend",
    )(
        members,
        lengths,
        place,
        q_latent.reshape(tokens, 4, block, kv),
        kv_new.astype(jnp.float32)[:, None, :],
        jnp.swapaxes(kv_cache, 1, 2),
    )


def partial_kernel(jobs, *refs):
    count = 1 + max(rows for pieces in jobs for rows, _ in pieces)
    row_refs, gain_ref, weight_refs, outs = (
        refs[:count],
        refs[count],
        refs[count + 1 : count + 3],
        refs[count + 3 :],
    )
    half = weight_refs[0].shape[1]
    gain = gain_ref[...]
    ready = []
    for ref in row_refs:
        x = ref[...].reshape(-1, ref.shape[-1]).astype(jnp.float32)
        ready.append(((x * gain).astype(jnp.bfloat16), jnp.sum(x * x, axis=1, keepdims=True)))
    for pieces, out in zip(jobs, outs):
        start = 0
        for rows, side in pieces:
            scaled, square = ready[rows]
            out[:, start : start + half] = jnp.dot(
                scaled, weight_refs[side][...], preferred_element_type=jnp.float32
            ).astype(jnp.bfloat16)
            start += half
            if side == 0:
                high = square.astype(jnp.bfloat16).astype(jnp.float32)
                lane = lax.broadcasted_iota(jnp.int32, (scaled.shape[0], 128), 1)
                out[:, start : start + 128] = jnp.where(lane < 64, high, square - high).astype(
                    jnp.bfloat16
                )
                start += 128


def partial_sums(rows, places, gain, weights, jobs):
    _, _, per_group, width = rows.shape
    half = weights[0].shape[1]
    count = 4 * per_group
    whole = lambda i: (0, 0)

    def at(place):
        return lambda i: (0, place, 0, 0)

    widths = [sum(half + (128 if side == 0 else 0) for _, side in pieces) for pieces in jobs]
    return pl.pallas_call(
        functools.partial(partial_kernel, jobs),
        grid=(1,),
        in_specs=[pl.BlockSpec((4, 1, per_group, width), at(p)) for p in places]
        + [pl.BlockSpec((1, width), whole)]
        + [pl.BlockSpec((width, half), whole)] * 2,
        out_specs=[pl.BlockSpec((count, w), whole) for w in widths],
        out_shape=[jax.ShapeDtypeStruct((count, w), jnp.bfloat16) for w in widths],
        compiler_params=pltpu.CompilerParams(vmem_limit_bytes=VMEM_LIMIT),
        cost_estimate=pl.CostEstimate(
            flops=2 * count * width * sum(widths),
            bytes_accessed=2 * (2 * width * half + count * sum(widths)),
            transcendentals=0,
        ),
        name="partial_sums",
    )(*([rows] * len(places)), gain, *weights)


def merge_kernel(own_a, own_c, direct_a, direct_c, relay_a, relay_c, *outs):
    wide_a = own_a.shape[1]
    rows = outs[0].shape[0]
    for out, place in zip(outs, FACING):
        part = pl.ds(place * rows, rows)
        total = wide(own_a[part, :]) + wide(relay_a[part, :]) + wide(direct_a[part, :])
        out[:, :wide_a] = total.astype(jnp.bfloat16)
        total = wide(own_c[part, :]) + wide(relay_c[part, :]) + wide(direct_c[part, :])
        out[:, wide_a:] = total.astype(jnp.bfloat16)


def merge(*operands):
    own_a, own_c = operands[:2]
    rows = own_a.shape[0] // 4
    cols = own_a.shape[1] + own_c.shape[1]
    return pl.pallas_call(
        merge_kernel,
        out_shape=[jax.ShapeDtypeStruct((rows, cols), jnp.bfloat16)] * 4,
        in_specs=[pl.BlockSpec(memory_space=pltpu.VMEM)] * 6,
        out_specs=[pl.BlockSpec(memory_space=pltpu.VMEM)] * 4,
        compiler_params=pltpu.CompilerParams(vmem_limit_bytes=VMEM_LIMIT),
        cost_estimate=pl.CostEstimate(
            flops=12 * rows * cols, bytes_accessed=32 * rows * cols, transcendentals=0
        ),
        name="merge",
    )(*operands)


def ring(first):
    def shift(value, by):
        pairs = []
        for g in range(16):
            for tp in range(4):
                x, z = g // 4, g % 4
                if (tp % 2 == 0) == first:
                    x = (x + by) % 4
                else:
                    z = (z + by) % 4
                pairs.append((g * 4 + tp, (x * 4 + z) * 4 + tp))
        return lax.ppermute(value, ("grp", "yh", "core"), pairs)

    return shift


shift_1, shift_2 = ring(True), ring(False)


def shift_y(value, by):
    def moved(place):
        role, yh, core = place // 4, place // 2 % 2, place % 2
        y = (yh * 2 + role + by) % 4
        return y % 2 * 4 + y // 2 * 2 + core

    return lax.ppermute(value, ("role", "yh", "core"), [(p, moved(p)) for p in range(8)])


def swap(value, axis):
    return lax.ppermute(value, axis, [(0, 1), (1, 0)])


def gather(block, shift):
    return [block] + [shift(block, s) for s in SHIFTS[1:]]


def wide(value):
    return value.astype(jnp.float32)


def add(*values):
    return sum(wide(v) for v in values)


def absolute(blocks, place, axis):
    take = lambda i: lax.slice_in_dim(blocks, i, i + 1, axis=axis)
    doubled = jnp.concatenate([take(i) for i in (2, 3, 1, 0, 2, 3, 1)], axis=axis)
    return lax.dynamic_slice_in_dim(doubled, (3 - place) % 4, 4, axis=axis)


def relative(blocks, place, axis):
    doubled = jnp.concatenate([blocks, lax.slice_in_dim(blocks, 0, 3, axis=axis)], axis=axis)
    turned = lax.dynamic_slice_in_dim(doubled, place, 4, axis=axis)
    return jnp.concatenate(
        [lax.slice_in_dim(turned, i, i + 1, axis=axis) for i in (0, 3, 1, 2)], axis=axis
    )


def body(
    q_latent,
    kv_new,
    kv_cache,
    lengths,
    members,
    hidden_in,
    w_uv,
    w_o,
    norm_gain,
    w_gate,
    w_up,
    w_down,
):
    groups = lax.axis_size("grp")
    place_x, place_z = lax.axis_index("grp") // 4, lax.axis_index("grp") % 4
    core, yh = lax.axis_index("core"), lax.axis_index("yh")
    place_1 = jnp.where(core == 0, place_x, place_z)
    place_2 = jnp.where(core == 0, place_z, place_x)
    tokens, heads, kv = q_latent.shape
    latent = w_uv.shape[1]
    value_width = w_uv.shape[2]
    width = w_o.shape[1]
    model_width = width * groups
    hidden = w_gate.shape[1]
    score_scale = (value_width + kv - latent) ** (-0.5)

    uv_pair = (w_uv, swap(w_uv, "core"))
    o_chip = jnp.concatenate([w_o, swap(w_o, "core")], axis=0)
    down_chip = jnp.concatenate([w_down, swap(w_down, "core")], axis=0)
    in_pair = (
        jnp.where(core == 0, w_gate, w_up),
        swap(jnp.where(core == 0, w_up, w_gate), "core"),
    )

    residual = lax.dynamic_index_in_dim(
        hidden_in.reshape(4, 4, 2, 2, tokens, width), core, 3, keepdims=False
    )
    residual = jnp.where(core == 0, jnp.swapaxes(residual, 0, 1), residual)
    residual = wide(relative(relative(residual, place_2, 0), place_1, 1))

    near, far = attend(
        q_latent,
        kv_new,
        kv_cache,
        lengths,
        members,
        (2 * yh + core).astype(jnp.int32)[None],
        score_scale,
        latent,
    )
    far = swap(far, "yh")
    context = jnp.stack([jnp.where(yh == 0, near, far), jnp.where(yh == 0, far, near)], axis=1)
    context = context.reshape(2, 2 * tokens, heads // 4, latent)
    values = jnp.concatenate(
        [
            jnp.einsum("thl,hlv->thv", c, w, preferred_element_type=jnp.float32)
            .astype(jnp.bfloat16)
            .reshape(2 * tokens, -1)
            for c, w in zip(context, uv_pair)
        ],
        axis=1,
    )
    values = jnp.concatenate(gather(values, shift_1))
    attn_part = jnp.stack(
        [
            jnp.dot(v, o_chip, preferred_element_type=jnp.float32)
            for v in gather(values, shift_2)
        ]
    ).reshape(4, 4, 2, tokens, width)
    shared = 0.5 * residual + attn_part
    sent = shared.astype(jnp.bfloat16)
    behind, ahead, across = (shift_y(sent, s) for s in SHIFTS[1:])
    stream = shared + wide(across)
    rows = jnp.stack([stream, add(behind, ahead)]).astype(jnp.bfloat16)
    rows = jnp.stack([rows, jnp.swapaxes(swap(rows, "core"), 1, 2)])
    rows = jnp.transpose(rows, (2, 3, 0, 1, 4, 5, 6)).reshape(4, 4, 8 * tokens, width)

    gain = wide(norm_gain)[None]
    behind, ahead, far = FACING[2], FACING[1], FACING[3]
    far_a, far_c = partial_sums(rows, (far,), gain, in_pair, (((0, 0),), ((0, 1),)))
    ahead_c, behind_a = partial_sums(rows, (ahead, behind), gain, in_pair, (((0, 1),), ((1, 0),)))
    ahead_a, behind_c, own_a, own_c = partial_sums(
        rows, (ahead, behind, 0), gain, in_pair, (((0, 0),), ((1, 1),), ((2, 0),), ((2, 1),))
    )
    far_a, far_c = shift_1(far_a, 1), shift_1(far_c, -1)
    direct_c, direct_a = shift_1(ahead_c, 1), shift_1(behind_a, -1)
    relay_a = shift_1(add(ahead_a, far_a).astype(jnp.bfloat16), 1)
    relay_c = shift_1(add(behind_c, far_c).astype(jnp.bfloat16), -1)
    blocks = merge(own_a, own_c, direct_a, direct_c, relay_a, relay_c)
    sums = add(blocks[0], *(shift_2(blocks[i], SHIFTS[i]) for i in range(1, 4)))
    square = sums[:, hidden : hidden + 1] + sums[:, hidden + 64 : hidden + 65]
    scale = lax.rsqrt(square / model_width + epsilon)
    sums = [sums[:, :hidden] * scale, sums[:, hidden + 128 :] * scale]
    own = [s[: 4 * tokens] for s in sums]
    other = swap(
        jnp.concatenate([s[4 * tokens :].astype(jnp.bfloat16) for s in sums], axis=1), "core"
    )
    other = [wide(other[:, hidden:]), wide(other[:, :hidden])]
    activated = jnp.concatenate(
        [
            (jax.nn.silu(jnp.where(core == 0, a, b)) * jnp.where(core == 0, b, a)).astype(
                jnp.bfloat16
            )
            for a, b in zip(own, other)
        ],
        axis=1,
    )

    own, behind, ahead, far = gather(activated, shift_1)
    low, high = jnp.concatenate([own, behind]), jnp.concatenate([ahead, far])
    behind_low, ahead_high = shift_2(low, 1), shift_2(high, -1)
    behind_high, ahead_low = shift_2(high, 1), shift_2(low, -1)
    far_low, far_high = shift_2(behind_low, 1), shift_2(ahead_high, -1)
    pieces = (low, high, behind_low, behind_high, ahead_low, ahead_high, far_low, far_high)
    down = jnp.stack(
        [jnp.dot(p, down_chip, preferred_element_type=jnp.float32) for p in pieces]
    ).reshape(4, 4, 2, 2, tokens, width)
    at_home = jnp.arange(2)[None, None, :, None, None] == yh
    down = jnp.stack([down[:, :, 0] + jnp.where(at_home, stream, 0.0), down[:, :, 1]])
    down = down.astype(jnp.bfloat16)
    down = absolute(absolute(down, place_2, 1), place_1, 2)
    down = jnp.where(core == 0, jnp.swapaxes(down, 1, 2), down)
    role = lax.axis_index("role")
    down = jnp.where(role == 0, down, down[::-1])
    down = down.reshape(2 * groups * 2, tokens, width)
    landed = lax.all_to_all(down, ("role", "grp", "yh"), split_axis=0, concat_axis=0)
    landed = landed.reshape(2, groups, 2, tokens, width)
    result = jnp.sum(wide(landed), axis=(0, 2)).astype(jnp.bfloat16)
    result = jnp.swapaxes(result, 0, 1).reshape(tokens, model_width)
    return lax.all_gather(result, ("yh", "core"), axis=0, tiled=True)


def solution(mesh):
    tp = ("yh", "core")
    in_specs = (
        P(("role", "grp") + tp, None, None),
        P(("role", "grp") + tp, None),
        P(("role", "grp") + tp, None, None),
        P(("role", "grp") + tp),
        P(("role", "grp") + tp),
        P("role", "grp"),
        P(tp, None, None),
        P(tp, "grp"),
        P("grp"),
        P("grp", ("role",) + tp),
        P("grp", ("role",) + tp),
        P(("role",) + tp, "grp"),
    )
    out_specs = P(("role", "grp"), None)
    sizes = dict(mesh.shape)
    split_mesh = Mesh(
        mesh.devices.reshape(sizes["role"], sizes["grp"], 2, 2), ("role", "grp", "yh", "core")
    )
    return jax.shard_map(
        body, mesh=split_mesh, in_specs=in_specs, out_specs=out_specs, check_vma=False
    )
```

```python
import functools

import jax
import jax.numpy as jnp
from jax import lax
from jax.experimental import pallas as pl
from jax.experimental.pallas import tpu as pltpu
from jax.sharding import Mesh
from jax.sharding import PartitionSpec as P

epsilon = 1e-06
VMEM_LIMIT = 20 * 1024 * 1024


SHIFTS = (0, 1, -1, 2)
FACING = (0, 2, 1, 3)


def attend_kernel(
    scale, latent, members_ref, lengths_ref, place_ref, q_ref, new_ref, kv_ref, near_ref, far_ref
):
    token = pl.program_id(0)
    length = lengths_ref[members_ref[token]]
    place = place_ref[0]
    queries = jnp.concatenate([q_ref[0, place ^ i] for i in range(4)], axis=0)
    cache = kv_ref[0]
    newest = new_ref[0]
    scores = scale * jnp.dot(queries, cache, preferred_element_type=jnp.float32)
    own = scale * jnp.sum(queries.astype(jnp.float32) * newest, axis=1, keepdims=True)
    usable = lax.broadcasted_iota(jnp.int32, scores.shape, 1) < length
    scores = jnp.where(usable, scores, -1e30)
    peak = jnp.maximum(jnp.max(scores, axis=1, keepdims=True), own)
    probs = jnp.exp(scores - peak).astype(jnp.bfloat16)
    self_weight = jnp.exp(own - peak)
    denom = jnp.sum(probs.astype(jnp.float32), axis=1, keepdims=True) + self_weight
    accum = lax.dot_general(
        probs, cache[:latent], (((1,), (1,)), ((), ())), preferred_element_type=jnp.float32
    )
    accum = accum + self_weight * newest[:, :latent]
    context = (accum / denom).astype(near_ref.dtype)
    half = context.shape[0] // 2
    near_ref[...] = context[:half].reshape(near_ref.shape)
    far_ref[...] = context[half:].reshape(far_ref.shape)


def attend(q_latent, kv_new, kv_cache, lengths, members, place, scale, latent):
    tokens, heads, kv = q_latent.shape
    ctx = kv_cache.shape[1]
    block = heads // 4
    grid_spec = pltpu.PrefetchScalarGridSpec(
        num_scalar_prefetch=3,
        grid=(tokens,),
        in_specs=[
            pl.BlockSpec((1, 4, block, kv), lambda t, m, n, p: (t, 0, 0, 0)),
            pl.BlockSpec((1, 1, kv), lambda t, m, n, p: (t, 0, 0)),
            pl.BlockSpec((1, kv, ctx), lambda t, m, n, p: (m[t], 0, 0)),
        ],
        out_specs=[pl.BlockSpec((2, 1, block, latent), lambda t, m, n, p: (0, t, 0, 0))] * 2,
    )
    return pl.pallas_call(
        functools.partial(attend_kernel, scale, latent),
        grid_spec=grid_spec,
        out_shape=[jax.ShapeDtypeStruct((2, tokens, block, latent), jnp.bfloat16)] * 2,
        compiler_params=pltpu.CompilerParams(vmem_limit_bytes=VMEM_LIMIT),
        cost_estimate=pl.CostEstimate(
            flops=2 * tokens * heads * ctx * (kv + latent),
            bytes_accessed=2 * tokens * ctx * kv,
            transcendentals=tokens * heads * ctx,
        ),
        name="attend",
    )(
        members,
        lengths,
        place,
        q_latent.reshape(tokens, 4, block, kv),
        kv_new.astype(jnp.float32)[:, None, :],
        jnp.swapaxes(kv_cache, 1, 2),
    )


def whole_call(kernel, name, out_shapes, operands, cost, limit=VMEM_LIMIT):
    return pl.pallas_call(
        kernel,
        out_shape=out_shapes,
        in_specs=[pl.BlockSpec(memory_space=pltpu.VMEM)] * len(operands),
        out_specs=[pl.BlockSpec(memory_space=pltpu.VMEM)] * len(out_shapes),
        compiler_params=pltpu.CompilerParams(vmem_limit_bytes=limit),
        cost_estimate=pl.CostEstimate(flops=cost[0], bytes_accessed=cost[1], transcendentals=0),
        name=name,
    )(*operands)


BODY, TAIL = 512, 64


def tail_at(block, odd, upper):
    block = block.astype(jnp.float32)
    turned = pltpu.roll(block, TAIL, 1)
    return jnp.where((odd == 1) != upper, turned, block)


def cut_in_kernel(chunk_ref, gate, gate_tail, up, up_tail, gain_ref, out_ref):
    odd = chunk_ref[0] % 2
    gain = gain_ref[...]
    out_ref[:, :BODY] = (wide(gate[...]) * gain).astype(jnp.bfloat16)
    out_ref[:, BODY : 2 * BODY] = (wide(up[...]) * gain).astype(jnp.bfloat16)
    lane = lax.broadcasted_iota(jnp.int32, gate_tail.shape, 1)
    tails = jnp.where(
        lane < TAIL, tail_at(gate_tail[...], odd, False), tail_at(up_tail[...], odd, True)
    )
    out_ref[:, 2 * BODY :] = (tails * gain).astype(jnp.bfloat16)


def chunk_specs(width):
    tails = 4 * BODY // 128
    return [
        pl.BlockSpec((width, BODY), lambda i, c: (0, c[i])),
        pl.BlockSpec((width, 2 * TAIL), lambda i, c: (0, tails + c[i] // 2)),
    ]


def cut_in(chunk, w_gate, w_up, gain):
    width = w_gate.shape[0]
    cols = 2 * (BODY + TAIL)
    return pl.pallas_call(
        cut_in_kernel,
        grid_spec=pltpu.PrefetchScalarGridSpec(
            num_scalar_prefetch=1,
            grid=(1,),
            in_specs=chunk_specs(width) * 2 + [pl.BlockSpec((width, 1), lambda i, c: (0, 0))],
            out_specs=pl.BlockSpec((width, cols), lambda i, c: (0, 0)),
        ),
        out_shape=jax.ShapeDtypeStruct((width, cols), jnp.bfloat16),
        compiler_params=pltpu.CompilerParams(vmem_limit_bytes=VMEM_LIMIT),
        cost_estimate=pl.CostEstimate(
            flops=width * cols, bytes_accessed=4 * width * cols, transcendentals=0
        ),
        name="cut_in",
    )(chunk.astype(jnp.int32)[None], w_gate, w_gate, w_up, w_up, gain)


def cut_down_kernel(chunk_ref, down, down_tail, out_ref):
    out_ref[0, :, :BODY] = down[...]
    lane = lax.broadcasted_iota(jnp.int32, down_tail.shape, 1)
    tail = tail_at(down_tail[...], chunk_ref[pl.program_id(0)] % 2, False)
    out_ref[0, :, BODY:] = jnp.where(lane < TAIL, tail, 0.0).astype(jnp.bfloat16)


def cut_down(chunks, w_down):
    width = w_down.shape[1]
    cols = BODY + 2 * TAIL
    turned = jnp.swapaxes(w_down, 0, 1)
    return pl.pallas_call(
        cut_down_kernel,
        grid_spec=pltpu.PrefetchScalarGridSpec(
            num_scalar_prefetch=1,
            grid=(4,),
            in_specs=chunk_specs(width),
            out_specs=pl.BlockSpec((1, width, cols), lambda i, c: (i, 0, 0)),
        ),
        out_shape=jax.ShapeDtypeStruct((4, width, cols), jnp.bfloat16),
        compiler_params=pltpu.CompilerParams(vmem_limit_bytes=VMEM_LIMIT),
        cost_estimate=pl.CostEstimate(
            flops=4 * width * cols, bytes_accessed=16 * width * cols, transcendentals=0
        ),
        name="cut_down",
    )(chunks.astype(jnp.int32), turned, turned)


def source_place(place, source):
    return SHIFTS.index((SHIFTS[place] - SHIFTS[source] + 1) % 4 - 1)


def partial_kernel(part, *refs):
    rows, weights, out = refs[:4], refs[4:8], refs[8]
    cols = weights[0].shape[1]
    total, square = 0.0, 0.0
    for source in range(4):
        x = jnp.concatenate([rows[source][part, source_place(p, source)] for p in range(4)])
        total += jnp.dot(x, weights[source][...], preferred_element_type=jnp.float32)
        square += jnp.sum(wide(x) * wide(x), axis=1, keepdims=True)
    out[:, :cols] = total.astype(jnp.bfloat16)
    high = wide(square.astype(jnp.bfloat16))
    lane = lax.broadcasted_iota(jnp.int32, (total.shape[0], 128), 1)
    out[:, cols:] = jnp.where(lane < 64, high, square - high).astype(jnp.bfloat16)


def partial_sums(rows, part, weights):
    _, _, per_group, width = rows[0].shape
    count, cols = 4 * per_group, weights[0].shape[1]
    return whole_call(
        functools.partial(partial_kernel, part),
        "partial_sums",
        [jax.ShapeDtypeStruct((count, cols + 128), jnp.bfloat16)],
        (*rows, *weights),
        (8 * count * width * cols, 8 * width * cols + 2 * count * cols),
    )[0]


def activate_kernel(model_width, *refs):
    out = refs[4]
    total = sum(wide(r[...]) for r in refs[:4])
    cols = 2 * (BODY + TAIL)
    square = total[:, cols : cols + 1] + total[:, cols + 64 : cols + 65]
    scale = lax.rsqrt(square / model_width + epsilon)
    gated = lambda g, u: jax.nn.silu(g * scale) * (u * scale)
    out[:, :BODY] = gated(total[:, :BODY], total[:, BODY : 2 * BODY]).astype(jnp.bfloat16)
    tails = total[:, 2 * BODY : cols]
    lane = lax.broadcasted_iota(jnp.int32, tails.shape, 1)
    tails = jnp.where(lane < TAIL, gated(tails, pltpu.roll(tails, TAIL, 1)), 0.0)
    out[:, BODY:] = tails.astype(jnp.bfloat16)


def activate(sums, model_width):
    count = sums[0].shape[0]
    cols = BODY + 2 * TAIL
    return whole_call(
        functools.partial(activate_kernel, model_width),
        "activate",
        [jax.ShapeDtypeStruct((count, cols), jnp.bfloat16)],
        sums,
        (20 * count * cols, 20 * count * cols),
    )[0]


def down_kernel(low, high, weights, mine, theirs):
    count = low.shape[1] // 4
    total = 0.0
    for source in range(4):
        ref = (low, high)[source // 2]
        x = jnp.concatenate(
            [
                ref[source % 2, pl.ds(source_place(p, source) * count, count), :]
                for p in range(4)
            ]
        )
        total += lax.dot_general(
            x, weights[source], (((1,), (1,)), ((), ())), preferred_element_type=jnp.float32
        )
    for p in range(4):
        mine[p] = total[p * count : p * count + count // 2]
        theirs[p] = total[p * count + count // 2 : (p + 1) * count].astype(jnp.bfloat16)


def down_block(low, high, weights):
    count = low.shape[1] // 4
    width = weights.shape[1]
    shape = (4, count // 2, width)
    return whole_call(
        down_kernel,
        "down_block",
        [jax.ShapeDtypeStruct(shape, jnp.float32), jax.ShapeDtypeStruct(shape, jnp.bfloat16)],
        (low, high, weights),
        (32 * count * width * low.shape[2], 8 * width * low.shape[2]),
    )


def ring(first):
    def shift(value, by):
        pairs = []
        for g in range(16):
            for tp in range(4):
                x, z = g // 4, g % 4
                if (tp % 2 == 0) == first:
                    x = (x + by) % 4
                else:
                    z = (z + by) % 4
                pairs.append((g * 4 + tp, (x * 4 + z) * 4 + tp))
        return lax.ppermute(value, ("grp", "yh", "core"), pairs)

    return shift


shift_1, shift_2 = ring(True), ring(False)


def shift_y(value, by):
    def moved(place):
        role, yh, core = place // 4, place // 2 % 2, place % 2
        y = (yh * 2 + role + by) % 4
        return y % 2 * 4 + y // 2 * 2 + core

    return lax.ppermute(value, ("role", "yh", "core"), [(p, moved(p)) for p in range(8)])


def swap(value, axis):
    return lax.ppermute(value, axis, [(0, 1), (1, 0)])


def gather(block, shift):
    return [block] + [shift(block, s) for s in SHIFTS[1:]]


def wide(value):
    return value.astype(jnp.float32)


def add(*values):
    return sum(wide(v) for v in values)


def absolute(blocks, place, axis):
    take = lambda i: lax.slice_in_dim(blocks, i, i + 1, axis=axis)
    doubled = jnp.concatenate([take(i) for i in (2, 3, 1, 0, 2, 3, 1)], axis=axis)
    return lax.dynamic_slice_in_dim(doubled, (3 - place) % 4, 4, axis=axis)


def relative(blocks, place, axis):
    doubled = jnp.concatenate([blocks, lax.slice_in_dim(blocks, 0, 3, axis=axis)], axis=axis)
    turned = lax.dynamic_slice_in_dim(doubled, place, 4, axis=axis)
    return jnp.concatenate(
        [lax.slice_in_dim(turned, i, i + 1, axis=axis) for i in (0, 3, 1, 2)], axis=axis
    )


def body(
    q_latent,
    kv_new,
    kv_cache,
    lengths,
    members,
    hidden_in,
    w_uv,
    w_o,
    norm_gain,
    w_gate,
    w_up,
    w_down,
):
    groups = lax.axis_size("grp")
    place_x, place_z = lax.axis_index("grp") // 4, lax.axis_index("grp") % 4
    core, yh = lax.axis_index("core"), lax.axis_index("yh")
    place_1 = jnp.where(core == 0, place_x, place_z)
    place_2 = jnp.where(core == 0, place_z, place_x)
    tokens, heads, kv = q_latent.shape
    latent = w_uv.shape[1]
    value_width = w_uv.shape[2]
    width = w_o.shape[1]
    model_width = width * groups
    hidden = w_gate.shape[1]
    score_scale = (value_width + kv - latent) ** (-0.5)

    uv_pair = (w_uv, swap(w_uv, "core"))
    o_chip = jnp.concatenate([w_o, swap(w_o, "core")], axis=0)
    gain = wide(norm_gain)[:, None]
    steps = jnp.array(SHIFTS)
    in_weights = [
        shift_1(cut_in((place_1 + s) % 4, w_gate, w_up, gain), s) for s in SHIFTS[1:]
    ]
    in_weights = [cut_in(place_1, w_gate, w_up, gain)] + in_weights
    down_weights = cut_down((place_1 - steps) % 4, w_down)

    residual = lax.dynamic_index_in_dim(
        hidden_in.reshape(4, 4, 2, 2, tokens, width), core, 3, keepdims=False
    )
    residual = jnp.where(core == 0, jnp.swapaxes(residual, 0, 1), residual)
    residual = wide(relative(relative(residual, place_2, 0), place_1, 1))

    near, far = attend(
        q_latent,
        kv_new,
        kv_cache,
        lengths,
        members,
        (2 * yh + core).astype(jnp.int32)[None],
        score_scale,
        latent,
    )
    far = swap(far, "yh")
    context = jnp.stack([jnp.where(yh == 0, near, far), jnp.where(yh == 0, far, near)], axis=1)
    context = context.reshape(2, 2 * tokens, heads // 4, latent)
    values = jnp.concatenate(
        [
            jnp.einsum("thl,hlv->thv", c, w, preferred_element_type=jnp.float32)
            .astype(jnp.bfloat16)
            .reshape(2 * tokens, -1)
            for c, w in zip(context, uv_pair)
        ],
        axis=1,
    )
    values = jnp.concatenate(gather(values, shift_1))
    attn_part = jnp.stack(
        [
            jnp.dot(v, o_chip, preferred_element_type=jnp.float32)
            for v in gather(values, shift_2)
        ]
    ).reshape(4, 4, 2, tokens, width)
    shared = 0.5 * residual + attn_part
    sent = shared.astype(jnp.bfloat16)
    behind, ahead, across = (shift_y(sent, s) for s in SHIFTS[1:])
    stream = shared + wide(across)
    rows = jnp.stack([stream, add(behind, ahead)]).astype(jnp.bfloat16)
    rows = jnp.stack([rows, jnp.swapaxes(swap(rows, "core"), 1, 2)])
    rows = jnp.transpose(rows, (2, 3, 0, 1, 4, 5, 6)).reshape(4, 4, 8 * tokens, width)

    rows_low, rows_high = rows[:2], rows[2:]
    rows_high = gather(rows_high, shift_1)
    rows_low = gather(rows_low, shift_1)
    far = shift_2(partial_sums(rows_high, FACING[3] - 2, in_weights), SHIFTS[3])
    behind = shift_2(partial_sums(rows_high, FACING[1] - 2, in_weights), SHIFTS[1])
    ahead = shift_2(partial_sums(rows_low, FACING[2], in_weights), SHIFTS[2])
    own = partial_sums(rows_low, FACING[0], in_weights)
    activated = activate((own, behind, ahead, far), model_width)

    own, behind, ahead, far = gather(activated, shift_1)
    low, high = jnp.stack([own, behind]), jnp.stack([ahead, far])
    behind_low, ahead_high = shift_2(low, 1), shift_2(high, -1)
    behind_high, ahead_low = shift_2(high, 1), shift_2(low, -1)
    far_low, far_high = shift_2(behind_low, 1), shift_2(ahead_high, -1)
    pairs = (
        (low, high),
        (behind_low, behind_high),
        (ahead_low, ahead_high),
        (far_low, far_high),
    )
    mine, theirs = zip(*(down_block(a, b, down_weights) for a, b in pairs))
    theirs = swap(jnp.stack(theirs), "core")
    down = jnp.stack(mine) + wide(jnp.swapaxes(theirs, 0, 1))
    down = down.reshape(4, 4, 2, 2, tokens, width)
    at_home = jnp.arange(2)[None, None, :, None, None] == yh
    down = jnp.stack([down[:, :, 0] + jnp.where(at_home, stream, 0.0), down[:, :, 1]])
    down = down.astype(jnp.bfloat16)
    down = absolute(absolute(down, place_2, 1), place_1, 2)
    down = jnp.where(core == 0, jnp.swapaxes(down, 1, 2), down)
    role = lax.axis_index("role")
    down = jnp.where(role == 0, down, down[::-1])
    down = down.reshape(2 * groups * 2, tokens, width)
    landed = lax.all_to_all(down, ("role", "grp", "yh"), split_axis=0, concat_axis=0)
    landed = landed.reshape(2, groups, 2, tokens, width)
    result = jnp.sum(wide(landed), axis=(0, 2)).astype(jnp.bfloat16)
    result = jnp.swapaxes(result, 0, 1).reshape(tokens, model_width)
    return lax.all_gather(result, ("yh", "core"), axis=0, tiled=True)


def solution(mesh):
    tp = ("yh", "core")
    in_specs = (
        P(("role", "grp") + tp, None, None),
        P(("role", "grp") + tp, None),
        P(("role", "grp") + tp, None, None),
        P(("role", "grp") + tp),
        P(("role", "grp") + tp),
        P("role", "grp"),
        P(tp, None, None),
        P(tp, "grp"),
        P("grp"),
        P("grp", ("role",) + tp),
        P("grp", ("role",) + tp),
        P(("role",) + tp, "grp"),
    )
    out_specs = P(("role", "grp"), None)
    sizes = dict(mesh.shape)
    split_mesh = Mesh(
        mesh.devices.reshape(sizes["role"], sizes["grp"], 2, 2), ("role", "grp", "yh", "core")
    )
    return jax.shard_map(
        body, mesh=split_mesh, in_specs=in_specs, out_specs=out_specs, check_vma=False
    )
```

```python
import functools

import jax
import jax.numpy as jnp
from jax import lax
from jax.experimental import pallas as pl
from jax.experimental.pallas import tpu as pltpu
from jax.sharding import Mesh
from jax.sharding import PartitionSpec as P

epsilon = 1e-06
VMEM_LIMIT = 20 * 1024 * 1024


SHIFTS = (0, 1, -1, 2)
FACING = (0, 2, 1, 3)


def attend_kernel(
    scale, latent, members_ref, lengths_ref, place_ref, q_ref, new_ref, kv_ref, near_ref, far_ref
):
    token = pl.program_id(0)
    length = lengths_ref[members_ref[token]]
    place = place_ref[0]
    queries = jnp.concatenate([q_ref[0, place ^ i] for i in range(4)], axis=0)
    cache = kv_ref[0]
    newest = new_ref[0]
    scores = scale * jnp.dot(queries, cache, preferred_element_type=jnp.float32)
    own = scale * jnp.sum(queries.astype(jnp.float32) * newest, axis=1, keepdims=True)
    usable = lax.broadcasted_iota(jnp.int32, scores.shape, 1) < length
    scores = jnp.where(usable, scores, -1e30)
    peak = jnp.maximum(jnp.max(scores, axis=1, keepdims=True), own)
    probs = jnp.exp(scores - peak).astype(jnp.bfloat16)
    self_weight = jnp.exp(own - peak)
    denom = jnp.sum(probs.astype(jnp.float32), axis=1, keepdims=True) + self_weight
    accum = lax.dot_general(
        probs, cache[:latent], (((1,), (1,)), ((), ())), preferred_element_type=jnp.float32
    )
    accum = accum + self_weight * newest[:, :latent]
    context = (accum / denom).astype(near_ref.dtype)
    half = context.shape[0] // 2
    near_ref[...] = context[:half].reshape(near_ref.shape)
    far_ref[...] = context[half:].reshape(far_ref.shape)


def attend(q_latent, kv_new, kv_cache, lengths, members, place, scale, latent):
    tokens, heads, kv = q_latent.shape
    ctx = kv_cache.shape[1]
    block = heads // 4
    grid_spec = pltpu.PrefetchScalarGridSpec(
        num_scalar_prefetch=3,
        grid=(tokens,),
        in_specs=[
            pl.BlockSpec((1, 4, block, kv), lambda t, m, n, p: (t, 0, 0, 0)),
            pl.BlockSpec((1, 1, kv), lambda t, m, n, p: (t, 0, 0)),
            pl.BlockSpec((1, kv, ctx), lambda t, m, n, p: (m[t], 0, 0)),
        ],
        out_specs=[pl.BlockSpec((2, 1, block, latent), lambda t, m, n, p: (0, t, 0, 0))] * 2,
    )
    return pl.pallas_call(
        functools.partial(attend_kernel, scale, latent),
        grid_spec=grid_spec,
        out_shape=[jax.ShapeDtypeStruct((2, tokens, block, latent), jnp.bfloat16)] * 2,
        compiler_params=pltpu.CompilerParams(vmem_limit_bytes=VMEM_LIMIT),
        cost_estimate=pl.CostEstimate(
            flops=2 * tokens * heads * ctx * (kv + latent),
            bytes_accessed=2 * tokens * ctx * kv,
            transcendentals=tokens * heads * ctx,
        ),
        name="attend",
    )(
        members,
        lengths,
        place,
        q_latent.reshape(tokens, 4, block, kv),
        kv_new.astype(jnp.float32)[:, None, :],
        jnp.swapaxes(kv_cache, 1, 2),
    )


def whole_call(kernel, name, out_shapes, operands, cost, limit=VMEM_LIMIT):
    return pl.pallas_call(
        kernel,
        out_shape=out_shapes,
        in_specs=[pl.BlockSpec(memory_space=pltpu.VMEM)] * len(operands),
        out_specs=[pl.BlockSpec(memory_space=pltpu.VMEM)] * len(out_shapes),
        compiler_params=pltpu.CompilerParams(vmem_limit_bytes=limit),
        cost_estimate=pl.CostEstimate(flops=cost[0], bytes_accessed=cost[1], transcendentals=0),
        name=name,
    )(*operands)


BODY, TAIL = 512, 64


def tail_at(block, odd, upper):
    block = block.astype(jnp.float32)
    turned = pltpu.roll(block, TAIL, 1)
    return jnp.where((odd == 1) != upper, turned, block)


def cut_in_kernel(chunk_ref, gate, gate_tail, up, up_tail, gain_ref, out_ref):
    odd = chunk_ref[0] % 2
    gain = gain_ref[...]
    out_ref[:, :BODY] = (wide(gate[...]) * gain).astype(jnp.bfloat16)
    out_ref[:, BODY : 2 * BODY] = (wide(up[...]) * gain).astype(jnp.bfloat16)
    lane = lax.broadcasted_iota(jnp.int32, gate_tail.shape, 1)
    tails = jnp.where(
        lane < TAIL, tail_at(gate_tail[...], odd, False), tail_at(up_tail[...], odd, True)
    )
    out_ref[:, 2 * BODY :] = (tails * gain).astype(jnp.bfloat16)


def chunk_specs(width):
    tails = 4 * BODY // 128
    return [
        pl.BlockSpec((width, BODY), lambda i, c: (0, c[i])),
        pl.BlockSpec((width, 2 * TAIL), lambda i, c: (0, tails + c[i] // 2)),
    ]


def cut_in(chunk, w_gate, w_up, gain):
    width = w_gate.shape[0]
    cols = 2 * (BODY + TAIL)
    return pl.pallas_call(
        cut_in_kernel,
        grid_spec=pltpu.PrefetchScalarGridSpec(
            num_scalar_prefetch=1,
            grid=(1,),
            in_specs=chunk_specs(width) * 2 + [pl.BlockSpec((width, 1), lambda i, c: (0, 0))],
            out_specs=pl.BlockSpec((width, cols), lambda i, c: (0, 0)),
        ),
        out_shape=jax.ShapeDtypeStruct((width, cols), jnp.bfloat16),
        compiler_params=pltpu.CompilerParams(vmem_limit_bytes=VMEM_LIMIT),
        cost_estimate=pl.CostEstimate(
            flops=width * cols, bytes_accessed=4 * width * cols, transcendentals=0
        ),
        name="cut_in",
    )(chunk.astype(jnp.int32)[None], w_gate, w_gate, w_up, w_up, gain)


def cut_down_kernel(chunk_ref, down, down_tail, out_ref):
    out_ref[0, :, :BODY] = down[...]
    lane = lax.broadcasted_iota(jnp.int32, down_tail.shape, 1)
    tail = tail_at(down_tail[...], chunk_ref[pl.program_id(0)] % 2, False)
    out_ref[0, :, BODY:] = jnp.where(lane < TAIL, tail, 0.0).astype(jnp.bfloat16)


def cut_down(chunks, w_down):
    width = w_down.shape[1]
    cols = BODY + 2 * TAIL
    turned = jnp.swapaxes(w_down, 0, 1)
    return pl.pallas_call(
        cut_down_kernel,
        grid_spec=pltpu.PrefetchScalarGridSpec(
            num_scalar_prefetch=1,
            grid=(4,),
            in_specs=chunk_specs(width),
            out_specs=pl.BlockSpec((1, width, cols), lambda i, c: (i, 0, 0)),
        ),
        out_shape=jax.ShapeDtypeStruct((4, width, cols), jnp.bfloat16),
        compiler_params=pltpu.CompilerParams(vmem_limit_bytes=VMEM_LIMIT),
        cost_estimate=pl.CostEstimate(
            flops=4 * width * cols, bytes_accessed=16 * width * cols, transcendentals=0
        ),
        name="cut_down",
    )(chunks.astype(jnp.int32), turned, turned)


def source_place(place, source):
    return SHIFTS.index((SHIFTS[place] - SHIFTS[source] + 1) % 4 - 1)


def partial_kernel(part, *refs):
    rows, weights, out = refs[:4], refs[4:8], refs[8]
    cols = weights[0].shape[1]
    total, square = 0.0, 0.0
    for source in range(4):
        x = jnp.concatenate([rows[source][part, source_place(p, source)] for p in range(4)])
        total += jnp.dot(x, weights[source][...], preferred_element_type=jnp.float32)
        square += jnp.sum(wide(x) * wide(x), axis=1, keepdims=True)
    out[:, :cols] = total.astype(jnp.bfloat16)
    high = wide(square.astype(jnp.bfloat16))
    lane = lax.broadcasted_iota(jnp.int32, (total.shape[0], 128), 1)
    out[:, cols:] = jnp.where(lane < 64, high, square - high).astype(jnp.bfloat16)


def partial_sums(rows, part, weights):
    _, _, per_group, width = rows[0].shape
    count, cols = 4 * per_group, weights[0].shape[1]
    return whole_call(
        functools.partial(partial_kernel, part),
        "partial_sums",
        [jax.ShapeDtypeStruct((count, cols + 128), jnp.bfloat16)],
        (*rows, *weights),
        (8 * count * width * cols, 8 * width * cols + 2 * count * cols),
    )[0]


def activate_kernel(model_width, *refs):
    out = refs[4]
    total = sum(wide(r[...]) for r in refs[:4])
    cols = 2 * (BODY + TAIL)
    square = total[:, cols : cols + 1] + total[:, cols + 64 : cols + 65]
    scale = lax.rsqrt(square / model_width + epsilon)
    gated = lambda g, u: jax.nn.silu(g * scale) * (u * scale)
    out[:, :BODY] = gated(total[:, :BODY], total[:, BODY : 2 * BODY]).astype(jnp.bfloat16)
    tails = total[:, 2 * BODY : cols]
    lane = lax.broadcasted_iota(jnp.int32, tails.shape, 1)
    tails = jnp.where(lane < TAIL, gated(tails, pltpu.roll(tails, TAIL, 1)), 0.0)
    out[:, BODY:] = tails.astype(jnp.bfloat16)


def activate(sums, model_width):
    count = sums[0].shape[0]
    cols = BODY + 2 * TAIL
    return whole_call(
        functools.partial(activate_kernel, model_width),
        "activate",
        [jax.ShapeDtypeStruct((count, cols), jnp.bfloat16)],
        sums,
        (20 * count * cols, 20 * count * cols),
    )[0]


def down_kernel(low, high, weights, mine, theirs):
    count = low.shape[1] // 4
    total = 0.0
    for source in range(4):
        ref = (low, high)[source // 2]
        x = jnp.concatenate(
            [
                ref[source % 2, pl.ds(source_place(p, source) * count, count), :]
                for p in range(4)
            ]
        )
        total += lax.dot_general(
            x, weights[source], (((1,), (1,)), ((), ())), preferred_element_type=jnp.float32
        )
    for p in range(4):
        mine[p] = total[p * count : p * count + count // 2]
        theirs[p] = total[p * count + count // 2 : (p + 1) * count].astype(jnp.bfloat16)


def down_block(low, high, weights):
    count = low.shape[1] // 4
    width = weights.shape[1]
    shape = (4, count // 2, width)
    return whole_call(
        down_kernel,
        "down_block",
        [jax.ShapeDtypeStruct(shape, jnp.float32), jax.ShapeDtypeStruct(shape, jnp.bfloat16)],
        (low, high, weights),
        (32 * count * width * low.shape[2], 8 * width * low.shape[2]),
    )


def ring(first):
    def shift(value, by):
        pairs = []
        for g in range(16):
            for tp in range(4):
                x, z = g // 4, g % 4
                if (tp % 2 == 0) == first:
                    x = (x + by) % 4
                else:
                    z = (z + by) % 4
                pairs.append((g * 4 + tp, (x * 4 + z) * 4 + tp))
        return lax.ppermute(value, ("grp", "yh", "core"), pairs)

    return shift


shift_1, shift_2 = ring(True), ring(False)


def shift_y(value, by):
    def moved(place):
        role, yh, core = place // 4, place // 2 % 2, place % 2
        y = (yh * 2 + role + by) % 4
        return y % 2 * 4 + y // 2 * 2 + core

    return lax.ppermute(value, ("role", "yh", "core"), [(p, moved(p)) for p in range(8)])


def swap(value, axis):
    return lax.ppermute(value, axis, [(0, 1), (1, 0)])


def gather(block, shift):
    return [block] + [shift(block, s) for s in SHIFTS[1:]]


def wide(value):
    return value.astype(jnp.float32)


def add(*values):
    return sum(wide(v) for v in values)


def absolute(blocks, place, axis):
    take = lambda i: lax.slice_in_dim(blocks, i, i + 1, axis=axis)
    doubled = jnp.concatenate([take(i) for i in (2, 3, 1, 0, 2, 3, 1)], axis=axis)
    return lax.dynamic_slice_in_dim(doubled, (3 - place) % 4, 4, axis=axis)


def relative(blocks, place, axis):
    doubled = jnp.concatenate([blocks, lax.slice_in_dim(blocks, 0, 3, axis=axis)], axis=axis)
    turned = lax.dynamic_slice_in_dim(doubled, place, 4, axis=axis)
    return jnp.concatenate(
        [lax.slice_in_dim(turned, i, i + 1, axis=axis) for i in (0, 3, 1, 2)], axis=axis
    )


def body(
    q_latent,
    kv_new,
    kv_cache,
    lengths,
    members,
    hidden_in,
    w_uv,
    w_o,
    norm_gain,
    w_gate,
    w_up,
    w_down,
):
    groups = lax.axis_size("grp")
    place_x, place_z = lax.axis_index("grp") // 4, lax.axis_index("grp") % 4
    core, yh = lax.axis_index("core"), lax.axis_index("yh")
    place_1 = jnp.where(core == 0, place_x, place_z)
    place_2 = jnp.where(core == 0, place_z, place_x)
    tokens, heads, kv = q_latent.shape
    latent = w_uv.shape[1]
    value_width = w_uv.shape[2]
    width = w_o.shape[1]
    model_width = width * groups
    hidden = w_gate.shape[1]
    score_scale = (value_width + kv - latent) ** (-0.5)

    uv_pair = (w_uv, swap(w_uv, "core"))
    o_chip = jnp.concatenate([w_o, swap(w_o, "core")], axis=0)
    gain = wide(norm_gain)[:, None]
    steps = jnp.array(SHIFTS)
    in_weights = [
        shift_1(cut_in((place_1 + s) % 4, w_gate, w_up, gain), s) for s in SHIFTS[1:]
    ]
    in_weights = [cut_in(place_1, w_gate, w_up, gain)] + in_weights
    down_weights = cut_down((place_1 - steps) % 4, w_down)

    near, far = attend(
        q_latent,
        kv_new,
        kv_cache,
        lengths,
        members,
        (2 * yh + core).astype(jnp.int32)[None],
        score_scale,
        latent,
    )
    far, in_weights[1], in_weights[2] = lax.optimization_barrier(
        (far, in_weights[1], in_weights[2])
    )
    far = swap(far, "yh")
    far, hidden_in = lax.optimization_barrier((far, hidden_in))
    residual = lax.dynamic_index_in_dim(
        hidden_in.reshape(4, 4, 2, 2, tokens, width), core, 3, keepdims=False
    )
    residual = jnp.where(core == 0, jnp.swapaxes(residual, 0, 1), residual)
    residual = wide(relative(relative(residual, place_2, 0), place_1, 1))

    context = jnp.stack([jnp.where(yh == 0, near, far), jnp.where(yh == 0, far, near)], axis=1)
    context = context.reshape(2, 2 * tokens, heads // 4, latent)
    values = jnp.concatenate(
        [
            jnp.einsum("thl,hlv->thv", c, w, preferred_element_type=jnp.float32)
            .astype(jnp.bfloat16)
            .reshape(2 * tokens, -1)
            for c, w in zip(context, uv_pair)
        ],
        axis=1,
    )
    values = jnp.concatenate(gather(values, shift_1))
    values, in_weights[3] = lax.optimization_barrier((values, in_weights[3]))
    attn_part = jnp.stack(
        [
            jnp.dot(v, o_chip, preferred_element_type=jnp.float32)
            for v in gather(values, shift_2)
        ]
    ).reshape(4, 4, 2, tokens, width)
    shared = 0.5 * residual + attn_part
    sent = shared.astype(jnp.bfloat16)
    behind, ahead, across = (shift_y(sent, s) for s in SHIFTS[1:])
    stream = shared + wide(across)
    rows = jnp.stack([stream, add(behind, ahead)]).astype(jnp.bfloat16)
    rows = jnp.stack([rows, jnp.swapaxes(swap(rows, "core"), 1, 2)])
    rows = jnp.transpose(rows, (2, 3, 0, 1, 4, 5, 6)).reshape(4, 4, 8 * tokens, width)

    rows_low, rows_high = rows[:2], rows[2:]
    rows_high = gather(rows_high, shift_1)
    rows_low = gather(rows_low, shift_1)
    far = shift_2(partial_sums(rows_high, FACING[3] - 2, in_weights), SHIFTS[3])
    behind = shift_2(partial_sums(rows_high, FACING[1] - 2, in_weights), SHIFTS[1])
    ahead = shift_2(partial_sums(rows_low, FACING[2], in_weights), SHIFTS[2])
    own = partial_sums(rows_low, FACING[0], in_weights)
    activated = activate((own, behind, ahead, far), model_width)

    own, behind, ahead, far = gather(activated, shift_1)
    low, high = jnp.stack([own, behind]), jnp.stack([ahead, far])
    behind_low, ahead_high = shift_2(low, 1), shift_2(high, -1)
    behind_high, ahead_low = shift_2(high, 1), shift_2(low, -1)
    far_low, far_high = shift_2(behind_low, 1), shift_2(ahead_high, -1)
    pairs = (
        (low, high),
        (behind_low, behind_high),
        (ahead_low, ahead_high),
        (far_low, far_high),
    )
    mine, theirs = zip(*(down_block(a, b, down_weights) for a, b in pairs))
    theirs = swap(jnp.stack(theirs), "core")
    down = jnp.stack(mine) + wide(jnp.swapaxes(theirs, 0, 1))
    down = down.reshape(4, 4, 2, 2, tokens, width)
    at_home = jnp.arange(2)[None, None, :, None, None] == yh
    down = jnp.stack([down[:, :, 0] + jnp.where(at_home, stream, 0.0), down[:, :, 1]])
    down = down.astype(jnp.bfloat16)
    down = absolute(absolute(down, place_2, 1), place_1, 2)
    down = jnp.where(core == 0, jnp.swapaxes(down, 1, 2), down)
    role = lax.axis_index("role")
    down = jnp.where(role == 0, down, down[::-1])
    down = down.reshape(2 * groups * 2, tokens, width)
    landed = lax.all_to_all(down, ("role", "grp", "yh"), split_axis=0, concat_axis=0)
    landed = landed.reshape(2, groups, 2, tokens, width)
    result = jnp.sum(wide(landed), axis=(0, 2)).astype(jnp.bfloat16)
    result = jnp.swapaxes(result, 0, 1).reshape(tokens, model_width)
    return lax.all_gather(result, ("yh", "core"), axis=0, tiled=True)


def solution(mesh):
    tp = ("yh", "core")
    in_specs = (
        P(("role", "grp") + tp, None, None),
        P(("role", "grp") + tp, None),
        P(("role", "grp") + tp, None, None),
        P(("role", "grp") + tp),
        P(("role", "grp") + tp),
        P("role", "grp"),
        P(tp, None, None),
        P(tp, "grp"),
        P("grp"),
        P("grp", ("role",) + tp),
        P("grp", ("role",) + tp),
        P(("role",) + tp, "grp"),
    )
    out_specs = P(("role", "grp"), None)
    sizes = dict(mesh.shape)
    split_mesh = Mesh(
        mesh.devices.reshape(sizes["role"], sizes["grp"], 2, 2), ("role", "grp", "yh", "core")
    )
    return jax.shard_map(
        body, mesh=split_mesh, in_specs=in_specs, out_specs=out_specs, check_vma=False
    )
```

```python
import functools

import jax
import jax.numpy as jnp
from jax import lax
from jax.experimental import pallas as pl
from jax.experimental.pallas import tpu as pltpu
from jax.sharding import Mesh
from jax.sharding import PartitionSpec as P

epsilon = 1e-06
VMEM_LIMIT = 20 * 1024 * 1024
STREAM_LIMIT = 50 * 1024 * 1024


SHIFTS = (0, 1, -1, 2)
FACING = (0, 2, 1, 3)


def attend_kernel(
    scale, latent, members_ref, lengths_ref, place_ref, q_ref, new_ref, kv_ref, near_ref, far_ref
):
    token = pl.program_id(0)
    length = lengths_ref[members_ref[token]]
    place = place_ref[0]
    queries = jnp.concatenate([q_ref[0, place ^ i] for i in range(4)], axis=0)
    cache = kv_ref[0]
    newest = new_ref[0]
    scores = scale * jnp.dot(queries, cache, preferred_element_type=jnp.float32)
    own = scale * jnp.sum(queries.astype(jnp.float32) * newest, axis=1, keepdims=True)
    usable = lax.broadcasted_iota(jnp.int32, scores.shape, 1) < length
    scores = jnp.where(usable, scores, -1e30)
    peak = jnp.maximum(jnp.max(scores, axis=1, keepdims=True), own)
    probs = jnp.exp(scores - peak).astype(jnp.bfloat16)
    self_weight = jnp.exp(own - peak)
    denom = jnp.sum(probs.astype(jnp.float32), axis=1, keepdims=True) + self_weight
    accum = lax.dot_general(
        probs, cache[:latent], (((1,), (1,)), ((), ())), preferred_element_type=jnp.float32
    )
    accum = accum + self_weight * newest[:, :latent]
    context = (accum / denom).astype(near_ref.dtype)
    half = context.shape[0] // 2
    near_ref[...] = context[:half].reshape(near_ref.shape)
    far_ref[...] = context[half:].reshape(far_ref.shape)


def attend(q_latent, kv_new, kv_cache, lengths, members, place, scale, latent):
    tokens, heads, kv = q_latent.shape
    ctx = kv_cache.shape[1]
    block = heads // 4
    grid_spec = pltpu.PrefetchScalarGridSpec(
        num_scalar_prefetch=3,
        grid=(tokens,),
        in_specs=[
            pl.BlockSpec((1, 4, block, kv), lambda t, m, n, p: (t, 0, 0, 0)),
            pl.BlockSpec((1, 1, kv), lambda t, m, n, p: (t, 0, 0)),
            pl.BlockSpec((1, kv, ctx), lambda t, m, n, p: (m[t], 0, 0)),
        ],
        out_specs=[pl.BlockSpec((2, 1, block, latent), lambda t, m, n, p: (0, t, 0, 0))] * 2,
    )
    return pl.pallas_call(
        functools.partial(attend_kernel, scale, latent),
        grid_spec=grid_spec,
        out_shape=[jax.ShapeDtypeStruct((2, tokens, block, latent), jnp.bfloat16)] * 2,
        compiler_params=pltpu.CompilerParams(vmem_limit_bytes=STREAM_LIMIT),
        cost_estimate=pl.CostEstimate(
            flops=2 * tokens * heads * ctx * (kv + latent),
            bytes_accessed=2 * tokens * ctx * kv,
            transcendentals=tokens * heads * ctx,
        ),
        name="attend",
    )(
        members,
        lengths,
        place,
        q_latent.reshape(tokens, 4, block, kv),
        kv_new.astype(jnp.float32)[:, None, :],
        jnp.swapaxes(kv_cache, 1, 2),
    )


def partial_kernel(jobs, *refs):
    count = 1 + max(rows for pieces in jobs for rows, _ in pieces)
    row_refs, gain_ref, weight_refs, outs = (
        refs[:count],
        refs[count],
        refs[count + 1 : count + 3],
        refs[count + 3 :],
    )
    half = weight_refs[0].shape[1]
    gain = gain_ref[...]
    ready = []
    for ref in row_refs:
        x = ref[...].reshape(-1, ref.shape[-1]).astype(jnp.float32)
        ready.append(((x * gain).astype(jnp.bfloat16), jnp.sum(x * x, axis=1, keepdims=True)))
    for pieces, out in zip(jobs, outs):
        start = 0
        for rows, side in pieces:
            scaled, square = ready[rows]
            out[:, start : start + half] = jnp.dot(
                scaled, weight_refs[side][...], preferred_element_type=jnp.float32
            ).astype(jnp.bfloat16)
            start += half
            if side == 0:
                high = square.astype(jnp.bfloat16).astype(jnp.float32)
                lane = lax.broadcasted_iota(jnp.int32, (scaled.shape[0], 128), 1)
                out[:, start : start + 128] = jnp.where(lane < 64, high, square - high).astype(
                    jnp.bfloat16
                )
                start += 128


def partial_sums(rows, places, gain, weights, jobs):
    _, _, per_group, width = rows.shape
    half = weights[0].shape[1]
    count = 4 * per_group
    whole = lambda i: (0, 0)

    def at(place):
        return lambda i: (0, place, 0, 0)

    widths = [sum(half + (128 if side == 0 else 0) for _, side in pieces) for pieces in jobs]
    return pl.pallas_call(
        functools.partial(partial_kernel, jobs),
        grid=(1,),
        in_specs=[pl.BlockSpec((4, 1, per_group, width), at(p)) for p in places]
        + [pl.BlockSpec((1, width), whole)]
        + [pl.BlockSpec((width, half), whole)] * 2,
        out_specs=[pl.BlockSpec((count, w), whole) for w in widths],
        out_shape=[jax.ShapeDtypeStruct((count, w), jnp.bfloat16) for w in widths],
        compiler_params=pltpu.CompilerParams(vmem_limit_bytes=VMEM_LIMIT),
        cost_estimate=pl.CostEstimate(
            flops=2 * count * width * sum(widths),
            bytes_accessed=2 * (2 * width * half + count * sum(widths)),
            transcendentals=0,
        ),
        name="partial_sums",
    )(*([rows] * len(places)), gain, *weights)


def merge_kernel(own_a, own_c, direct_a, direct_c, relay_a, relay_c, *outs):
    wide_a = own_a.shape[1]
    rows = outs[0].shape[0]
    for out, place in zip(outs, FACING):
        part = pl.ds(place * rows, rows)
        total = wide(own_a[part, :]) + wide(relay_a[part, :]) + wide(direct_a[part, :])
        out[:, :wide_a] = total.astype(jnp.bfloat16)
        total = wide(own_c[part, :]) + wide(relay_c[part, :]) + wide(direct_c[part, :])
        out[:, wide_a:] = total.astype(jnp.bfloat16)


def merge(*operands):
    own_a, own_c = operands[:2]
    rows = own_a.shape[0] // 4
    cols = own_a.shape[1] + own_c.shape[1]
    return pl.pallas_call(
        merge_kernel,
        out_shape=[jax.ShapeDtypeStruct((rows, cols), jnp.bfloat16)] * 4,
        in_specs=[pl.BlockSpec(memory_space=pltpu.VMEM)] * 6,
        out_specs=[pl.BlockSpec(memory_space=pltpu.VMEM)] * 4,
        compiler_params=pltpu.CompilerParams(vmem_limit_bytes=VMEM_LIMIT),
        cost_estimate=pl.CostEstimate(
            flops=12 * rows * cols, bytes_accessed=32 * rows * cols, transcendentals=0
        ),
        name="merge",
    )(*operands)


def whole_call(kernel, name, out_shapes, operands, cost):
    return pl.pallas_call(
        kernel,
        out_shape=out_shapes,
        in_specs=[pl.BlockSpec(memory_space=pltpu.VMEM)] * len(operands),
        out_specs=[pl.BlockSpec(memory_space=pltpu.VMEM)] * len(out_shapes),
        compiler_params=pltpu.CompilerParams(vmem_limit_bytes=VMEM_LIMIT),
        cost_estimate=pl.CostEstimate(flops=cost, bytes_accessed=cost, transcendentals=0),
        name=name,
    )(*operands)


def join_kernel(*refs):
    *blocks, out = refs
    count = blocks[0].shape[0]
    for i, block in enumerate(blocks):
        out[i * count : (i + 1) * count] = block[...]


def join(*blocks):
    count, cols = blocks[0].shape
    shape = jax.ShapeDtypeStruct((len(blocks) * count, cols), blocks[0].dtype)
    return whole_call(join_kernel, "join", [shape], blocks, 4 * shape.size)[0]


def settle_kernel(model_width, hidden, *refs):
    parts, (mine, theirs) = refs[:4], refs[4:]
    total = sum(wide(r[...]) for r in parts)
    square = total[:, hidden : hidden + 1] + total[:, hidden + 64 : hidden + 65]
    scale = lax.rsqrt(square / model_width + epsilon)
    count = mine.shape[0]
    for start, cols in ((0, slice(0, hidden)), (hidden, slice(hidden + 128, None))):
        scaled = total[:, cols] * scale
        mine[:, start : start + hidden] = scaled[:count]
        theirs[:, start : start + hidden] = scaled[count:].astype(jnp.bfloat16)


def settle(parts, model_width, hidden):
    count = parts[0].shape[0] // 2
    shapes = [jax.ShapeDtypeStruct((count, 2 * hidden), t) for t in (jnp.float32, jnp.bfloat16)]
    kernel = functools.partial(settle_kernel, model_width, hidden)
    return whole_call(kernel, "settle", shapes, parts, 32 * count * hidden)


def activate_kernel(hidden, core_ref, mine, theirs, out):
    core = core_ref[0]
    for start, other in ((0, hidden), (hidden, 0)):
        a = mine[:, start : start + hidden]
        b = wide(theirs[:, other : other + hidden])
        gate, up = jnp.where(core == 0, a, b), jnp.where(core == 0, b, a)
        out[:, start : start + hidden] = (jax.nn.silu(gate) * up).astype(out.dtype)


def activate(core, mine, theirs):
    count, cols = mine.shape
    return pl.pallas_call(
        functools.partial(activate_kernel, cols // 2),
        out_shape=jax.ShapeDtypeStruct((count, cols), jnp.bfloat16),
        in_specs=[pl.BlockSpec(memory_space=pltpu.SMEM)]
        + [pl.BlockSpec(memory_space=pltpu.VMEM)] * 2,
        out_specs=pl.BlockSpec(memory_space=pltpu.VMEM),
        compiler_params=pltpu.CompilerParams(vmem_limit_bytes=VMEM_LIMIT),
        cost_estimate=pl.CostEstimate(
            flops=8 * count * cols, bytes_accessed=8 * count * cols, transcendentals=count * cols
        ),
        name="activate",
    )(core.astype(jnp.int32)[None], mine, theirs)


def ring(first):
    def shift(value, by):
        pairs = []
        for g in range(16):
            for tp in range(4):
                x, z = g // 4, g % 4
                if (tp % 2 == 0) == first:
                    x = (x + by) % 4
                else:
                    z = (z + by) % 4
                pairs.append((g * 4 + tp, (x * 4 + z) * 4 + tp))
        return lax.ppermute(value, ("grp", "yh", "core"), pairs)

    return shift


shift_1, shift_2 = ring(True), ring(False)


def shift_y(value, by):
    def moved(place):
        role, yh, core = place // 4, place // 2 % 2, place % 2
        y = (yh * 2 + role + by) % 4
        return y % 2 * 4 + y // 2 * 2 + core

    return lax.ppermute(value, ("role", "yh", "core"), [(p, moved(p)) for p in range(8)])


def swap(value, axis):
    return lax.ppermute(value, axis, [(0, 1), (1, 0)])


def gather(block, shift):
    return [block] + [shift(block, s) for s in SHIFTS[1:]]


def gather_from(blocks, shift):
    return [blocks[0]] + [shift(b, s) for b, s in zip(blocks[1:], SHIFTS[1:])]


def wide(value):
    return value.astype(jnp.float32)


def add(*values):
    return sum(wide(v) for v in values)


def absolute(blocks, place, axis):
    take = lambda i: lax.slice_in_dim(blocks, i, i + 1, axis=axis)
    doubled = jnp.concatenate([take(i) for i in (2, 3, 1, 0, 2, 3, 1)], axis=axis)
    return lax.dynamic_slice_in_dim(doubled, (3 - place) % 4, 4, axis=axis)


def relative(blocks, place, axis):
    doubled = jnp.concatenate([blocks, lax.slice_in_dim(blocks, 0, 3, axis=axis)], axis=axis)
    turned = lax.dynamic_slice_in_dim(doubled, place, 4, axis=axis)
    return jnp.concatenate(
        [lax.slice_in_dim(turned, i, i + 1, axis=axis) for i in (0, 3, 1, 2)], axis=axis
    )


def body(
    q_latent,
    kv_new,
    kv_cache,
    lengths,
    members,
    hidden_in,
    w_uv,
    w_o,
    norm_gain,
    w_gate,
    w_up,
    w_down,
):
    groups = lax.axis_size("grp")
    place_x, place_z = lax.axis_index("grp") // 4, lax.axis_index("grp") % 4
    core, yh = lax.axis_index("core"), lax.axis_index("yh")
    place_1 = jnp.where(core == 0, place_x, place_z)
    place_2 = jnp.where(core == 0, place_z, place_x)
    tokens, heads, kv = q_latent.shape
    latent = w_uv.shape[1]
    value_width = w_uv.shape[2]
    width = w_o.shape[1]
    model_width = width * groups
    hidden = w_gate.shape[1]
    score_scale = (value_width + kv - latent) ** (-0.5)

    uv_pair = (w_uv, swap(w_uv, "core"))
    o_chip = jnp.concatenate([w_o, swap(w_o, "core")], axis=0)
    down_chip = jnp.concatenate([w_down, swap(w_down, "core")], axis=0)
    in_pair = (
        jnp.where(core == 0, w_gate, w_up),
        swap(jnp.where(core == 0, w_up, w_gate), "core"),
    )

    residual = lax.dynamic_index_in_dim(
        hidden_in.reshape(4, 4, 2, 2, tokens, width), core, 3, keepdims=False
    )
    residual = jnp.where(core == 0, jnp.swapaxes(residual, 0, 1), residual)
    residual = wide(relative(relative(residual, place_2, 0), place_1, 1))

    near, far = attend(
        q_latent,
        kv_new,
        kv_cache,
        lengths,
        members,
        (2 * yh + core).astype(jnp.int32)[None],
        score_scale,
        latent,
    )
    far = swap(far, "yh")

    def head_values(context):
        parts = [
            jnp.einsum("thl,hlv->thv", c, w, preferred_element_type=jnp.float32)
            for c, w in zip(context, uv_pair)
        ]
        return jnp.stack(parts, axis=1).astype(jnp.bfloat16).reshape(tokens, -1)

    near, far = head_values(near), head_values(far)
    values = jnp.where(
        yh == 0, jnp.concatenate([near, far]), jnp.concatenate([far, near])
    )
    pieces = gather(join(*gather(values, shift_1)), shift_2)
    rows, stream = [], []
    for half in range(2):
        attn_part = jnp.stack(
            [
                jnp.dot(v, o_chip, preferred_element_type=jnp.float32)
                for v in pieces[2 * half : 2 * half + 2]
            ]
        ).reshape(2, 4, 2, tokens, width)
        shared = 0.5 * residual[2 * half : 2 * half + 2] + attn_part
        sent = shared.astype(jnp.bfloat16)
        behind, ahead, across = (shift_y(sent, s) for s in SHIFTS[1:])
        stream.append(shared + wide(across))
        rows.append(jnp.stack([stream[-1], add(behind, ahead)]).astype(jnp.bfloat16))
    stream = jnp.concatenate(stream)
    rows = jnp.concatenate(rows, axis=1)
    rows = jnp.stack([rows, jnp.swapaxes(swap(rows, "core"), 1, 2)])
    rows = jnp.transpose(rows, (2, 3, 0, 1, 4, 5, 6)).reshape(4, 4, 8 * tokens, width)

    gain = wide(norm_gain)[None]
    behind, ahead, far = FACING[2], FACING[1], FACING[3]
    far_a, far_c = partial_sums(rows, (far,), gain, in_pair, (((0, 0),), ((0, 1),)))
    ahead_c, behind_a = partial_sums(rows, (ahead, behind), gain, in_pair, (((0, 1),), ((1, 0),)))
    ahead_a, behind_c, own_a, own_c = partial_sums(
        rows, (ahead, behind, 0), gain, in_pair, (((0, 0),), ((1, 1),), ((2, 0),), ((2, 1),))
    )
    far_a, far_c = shift_1(far_a, 1), shift_1(far_c, -1)
    direct_c, direct_a = shift_1(ahead_c, 1), shift_1(behind_a, -1)
    relay_a = shift_1(add(ahead_a, far_a).astype(jnp.bfloat16), 1)
    relay_c = shift_1(add(behind_c, far_c).astype(jnp.bfloat16), -1)
    blocks = merge(own_a, own_c, direct_a, direct_c, relay_a, relay_c)
    parts = gather_from(blocks, shift_2)
    mine, theirs = settle(parts, model_width, hidden)
    activated = activate(core, mine, swap(theirs, "core"))

    own, behind, ahead, far = gather(activated, shift_1)
    low, high = join(own, behind), join(ahead, far)
    behind_low, ahead_high = shift_2(low, 1), shift_2(high, -1)
    behind_high, ahead_low = shift_2(high, 1), shift_2(low, -1)
    far_low, far_high = shift_2(behind_low, 1), shift_2(ahead_high, -1)
    pieces = (low, high, behind_low, behind_high, ahead_low, ahead_high, far_low, far_high)
    down = jnp.stack(
        [jnp.dot(p, down_chip, preferred_element_type=jnp.float32) for p in pieces]
    ).reshape(4, 4, 2, 2, tokens, width)
    at_home = jnp.arange(2)[None, None, :, None, None] == yh
    down = jnp.stack([down[:, :, 0] + jnp.where(at_home, stream, 0.0), down[:, :, 1]])
    down = down.astype(jnp.bfloat16)
    down = absolute(absolute(down, place_2, 1), place_1, 2)
    down = jnp.where(core == 0, jnp.swapaxes(down, 1, 2), down)
    role = lax.axis_index("role")
    down = jnp.where(role == 0, down, down[::-1])
    down = down.reshape(2 * groups * 2, tokens, width)
    landed = lax.all_to_all(down, ("role", "grp", "yh"), split_axis=0, concat_axis=0)
    landed = landed.reshape(2, groups, 2, tokens, width)
    result = jnp.sum(wide(landed), axis=(0, 2)).astype(jnp.bfloat16)
    result = jnp.swapaxes(result, 0, 1).reshape(tokens, model_width)
    return lax.all_gather(result, ("yh", "core"), axis=0, tiled=True)


def solution(mesh):
    tp = ("yh", "core")
    in_specs = (
        P(("role", "grp") + tp, None, None),
        P(("role", "grp") + tp, None),
        P(("role", "grp") + tp, None, None),
        P(("role", "grp") + tp),
        P(("role", "grp") + tp),
        P("role", "grp"),
        P(tp, None, None),
        P(tp, "grp"),
        P("grp"),
        P("grp", ("role",) + tp),
        P("grp", ("role",) + tp),
        P(("role",) + tp, "grp"),
    )
    out_specs = P(("role", "grp"), None)
    sizes = dict(mesh.shape)
    split_mesh = Mesh(
        mesh.devices.reshape(sizes["role"], sizes["grp"], 2, 2), ("role", "grp", "yh", "core")
    )
    return jax.shard_map(
        body, mesh=split_mesh, in_specs=in_specs, out_specs=out_specs, check_vma=False
    )
```

```python
import functools

import jax
import jax.numpy as jnp
from jax import lax
from jax.experimental import pallas as pl
from jax.experimental.pallas import tpu as pltpu
from jax.sharding import Mesh
from jax.sharding import PartitionSpec as P

epsilon = 1e-06
VMEM_LIMIT = 20 * 1024 * 1024
STREAM_LIMIT = 50 * 1024 * 1024


SHIFTS = (0, 1, -1, 2)
FACING = (0, 2, 1, 3)


def attend_kernel(
    scale, latent, plan_ref, q_ref, new_ref, kv_ref, near_ref, far_ref
):
    token = pl.program_id(0)
    tokens = pl.num_programs(0)
    length = plan_ref[tokens + plan_ref[token]]
    place = plan_ref[2 * tokens]
    queries = jnp.concatenate([q_ref[0, place ^ i] for i in range(4)], axis=0)
    cache = kv_ref[0]
    newest = wide(new_ref[...])
    picked = lax.broadcasted_iota(jnp.int32, newest.shape, 0) == token
    newest = jnp.sum(jnp.where(picked, newest, 0.0), axis=0, keepdims=True)
    scores = scale * jnp.dot(queries, cache, preferred_element_type=jnp.float32)
    own = scale * jnp.sum(queries.astype(jnp.float32) * newest, axis=1, keepdims=True)
    usable = lax.broadcasted_iota(jnp.int32, scores.shape, 1) < length
    scores = jnp.where(usable, scores, -1e30)
    peak = jnp.maximum(jnp.max(scores, axis=1, keepdims=True), own)
    probs = jnp.exp(scores - peak).astype(jnp.bfloat16)
    self_weight = jnp.exp(own - peak)
    denom = jnp.sum(probs.astype(jnp.float32), axis=1, keepdims=True) + self_weight
    accum = lax.dot_general(
        probs, cache[:latent], (((1,), (1,)), ((), ())), preferred_element_type=jnp.float32
    )
    accum = accum + self_weight * newest[:, :latent]
    context = (accum / denom).astype(near_ref.dtype)
    half = context.shape[0] // 2
    near_ref[...] = context[:half].reshape(near_ref.shape)
    far_ref[...] = context[half:].reshape(far_ref.shape)


def attend(q_latent, kv_new, kv_cache, lengths, members, place, scale, latent):
    tokens, heads, kv = q_latent.shape
    ctx = kv_cache.shape[1]
    block = heads // 4
    grid_spec = pltpu.PrefetchScalarGridSpec(
        num_scalar_prefetch=1,
        grid=(tokens,),
        in_specs=[
            pl.BlockSpec((1, 4, block, kv), lambda t, m: (t, 0, 0, 0)),
            pl.BlockSpec((tokens, kv), lambda t, m: (0, 0)),
            pl.BlockSpec((1, kv, ctx), lambda t, m: (m[t], 0, 0)),
        ],
        out_specs=[pl.BlockSpec((2, 1, block, latent), lambda t, m: (0, t, 0, 0))] * 2,
    )
    return pl.pallas_call(
        functools.partial(attend_kernel, scale, latent),
        grid_spec=grid_spec,
        out_shape=[jax.ShapeDtypeStruct((2, tokens, block, latent), jnp.bfloat16)] * 2,
        compiler_params=pltpu.CompilerParams(vmem_limit_bytes=STREAM_LIMIT),
        cost_estimate=pl.CostEstimate(
            flops=2 * tokens * heads * ctx * (kv + latent),
            bytes_accessed=2 * tokens * ctx * kv,
            transcendentals=tokens * heads * ctx,
        ),
        name="attend",
    )(
        jnp.concatenate([members, lengths, place]),
        q_latent.reshape(tokens, 4, block, kv),
        kv_new,
        jnp.swapaxes(kv_cache, 1, 2),
    )


def partial_kernel(jobs, *refs):
    count = 1 + max(rows for pieces in jobs for rows, _ in pieces)
    row_refs, gain_ref, weight_refs, outs = (
        refs[:count],
        refs[count],
        refs[count + 1 : count + 3],
        refs[count + 3 :],
    )
    half = weight_refs[0].shape[1]
    gain = gain_ref[...]
    ready = []
    for ref in row_refs:
        x = ref[...].reshape(-1, ref.shape[-1]).astype(jnp.float32)
        ready.append(((x * gain).astype(jnp.bfloat16), jnp.sum(x * x, axis=1, keepdims=True)))
    for pieces, out in zip(jobs, outs):
        start = 0
        for rows, side in pieces:
            scaled, square = ready[rows]
            out[:, start : start + half] = jnp.dot(
                scaled, weight_refs[side][...], preferred_element_type=jnp.float32
            ).astype(jnp.bfloat16)
            start += half
            if side == 0:
                high = square.astype(jnp.bfloat16).astype(jnp.float32)
                lane = lax.broadcasted_iota(jnp.int32, (scaled.shape[0], 128), 1)
                out[:, start : start + 128] = jnp.where(lane < 64, high, square - high).astype(
                    jnp.bfloat16
                )
                start += 128


def partial_sums(rows, places, gain, weights, jobs):
    _, _, per_group, width = rows.shape
    half = weights[0].shape[1]
    count = 4 * per_group
    whole = lambda i: (0, 0)

    def at(place):
        return lambda i: (0, place, 0, 0)

    widths = [sum(half + (128 if side == 0 else 0) for _, side in pieces) for pieces in jobs]
    return pl.pallas_call(
        functools.partial(partial_kernel, jobs),
        grid=(1,),
        in_specs=[pl.BlockSpec((4, 1, per_group, width), at(p)) for p in places]
        + [pl.BlockSpec((1, width), whole)]
        + [pl.BlockSpec((width, half), whole)] * 2,
        out_specs=[pl.BlockSpec((count, w), whole) for w in widths],
        out_shape=[jax.ShapeDtypeStruct((count, w), jnp.bfloat16) for w in widths],
        compiler_params=pltpu.CompilerParams(vmem_limit_bytes=VMEM_LIMIT),
        cost_estimate=pl.CostEstimate(
            flops=2 * count * width * sum(widths),
            bytes_accessed=2 * (2 * width * half + count * sum(widths)),
            transcendentals=0,
        ),
        name="partial_sums",
    )(*([rows] * len(places)), gain, *weights)


def merge_kernel(own_a, own_c, direct_a, direct_c, relay_a, relay_c, *outs):
    wide_a = own_a.shape[1]
    rows = outs[0].shape[0]
    for out, place in zip(outs, FACING):
        part = pl.ds(place * rows, rows)
        total = wide(own_a[part, :]) + wide(relay_a[part, :]) + wide(direct_a[part, :])
        out[:, :wide_a] = total.astype(jnp.bfloat16)
        total = wide(own_c[part, :]) + wide(relay_c[part, :]) + wide(direct_c[part, :])
        out[:, wide_a:] = total.astype(jnp.bfloat16)


def merge(*operands):
    own_a, own_c = operands[:2]
    rows = own_a.shape[0] // 4
    cols = own_a.shape[1] + own_c.shape[1]
    return pl.pallas_call(
        merge_kernel,
        out_shape=[jax.ShapeDtypeStruct((rows, cols), jnp.bfloat16)] * 4,
        in_specs=[pl.BlockSpec(memory_space=pltpu.VMEM)] * 6,
        out_specs=[pl.BlockSpec(memory_space=pltpu.VMEM)] * 4,
        compiler_params=pltpu.CompilerParams(vmem_limit_bytes=VMEM_LIMIT),
        cost_estimate=pl.CostEstimate(
            flops=12 * rows * cols, bytes_accessed=32 * rows * cols, transcendentals=0
        ),
        name="merge",
    )(*operands)


def whole_call(kernel, name, out_shapes, operands, cost):
    return pl.pallas_call(
        kernel,
        out_shape=out_shapes,
        in_specs=[pl.BlockSpec(memory_space=pltpu.VMEM)] * len(operands),
        out_specs=[pl.BlockSpec(memory_space=pltpu.VMEM)] * len(out_shapes),
        compiler_params=pltpu.CompilerParams(vmem_limit_bytes=VMEM_LIMIT),
        cost_estimate=pl.CostEstimate(flops=cost, bytes_accessed=cost, transcendentals=0),
        name=name,
    )(*operands)


def join_kernel(*refs):
    *blocks, out = refs
    count = blocks[0].shape[0]
    for i, block in enumerate(blocks):
        out[i * count : (i + 1) * count] = block[...]


def join(*blocks):
    count, cols = blocks[0].shape
    shape = jax.ShapeDtypeStruct((len(blocks) * count, cols), blocks[0].dtype)
    return whole_call(join_kernel, "join", [shape], blocks, 4 * shape.size)[0]


def pair_dot_kernel(*refs):
    *blocks, weights, out = refs
    half, width = weights.shape[1], out.shape[1]
    step = half // 4 if half % 512 == 0 else half // 3
    total = 0.0
    for side in range(2):
        for k in range(0, half, step):
            cols = slice(side * half + k, side * half + k + step)
            rows = jnp.concatenate([b[:, cols] for b in blocks])
            total += lax.dot_general(
                rows,
                weights[side * width : (side + 1) * width, k : k + step],
                (((1,), (1,)), ((), ())),
                preferred_element_type=jnp.float32,
            )
    out[...] = total


def pair_dot(blocks, weights):
    count = sum(b.shape[0] for b in blocks)
    width, half = weights.shape[0] // 2, weights.shape[1]
    shape = jax.ShapeDtypeStruct((count, width), jnp.float32)
    return whole_call(pair_dot_kernel, "pair_dot", [shape], (*blocks, weights), 4 * width * half)[0]


def head_values_kernel(yh_ref, near, far, *refs):
    *weights, out = refs
    yh = yh_ref[0]
    count, heads = near.shape[1:3]
    width = weights[0].shape[2]
    for c, weight in enumerate(weights):
        own, other = wide(near[c]), wide(far[c])
        rows = jnp.concatenate([jnp.where(yh == 0, own, other), jnp.where(yh == 0, other, own)])
        rows = jnp.swapaxes(rows, 0, 1).astype(jnp.bfloat16)
        for h in range(heads):
            start = (c * heads + h) * width
            out[:, start : start + width] = jnp.dot(
                rows[h], weight[h], preferred_element_type=jnp.float32
            ).astype(out.dtype)


def head_values(yh, near, far, weights):
    tokens, heads = near.shape[1:3]
    shape = jax.ShapeDtypeStruct((2 * tokens, 2 * heads * weights[0].shape[2]), jnp.bfloat16)
    return pl.pallas_call(
        head_values_kernel,
        out_shape=shape,
        in_specs=[pl.BlockSpec(memory_space=pltpu.SMEM)]
        + [pl.BlockSpec(memory_space=pltpu.VMEM)] * 4,
        out_specs=pl.BlockSpec(memory_space=pltpu.VMEM),
        compiler_params=pltpu.CompilerParams(vmem_limit_bytes=VMEM_LIMIT),
        cost_estimate=pl.CostEstimate(
            flops=2 * shape.size * near.shape[3],
            bytes_accessed=4 * weights[0].size,
            transcendentals=0,
        ),
        name="head_values",
    )(yh.astype(jnp.int32)[None], near, far, *weights)


def settle_kernel(model_width, hidden, *refs):
    parts, (mine, theirs) = refs[:4], refs[4:]
    total = sum(wide(r[...]) for r in parts)
    square = total[:, hidden : hidden + 1] + total[:, hidden + 64 : hidden + 65]
    scale = lax.rsqrt(square / model_width + epsilon)
    count = mine.shape[0]
    for start, cols in ((0, slice(0, hidden)), (hidden, slice(hidden + 128, None))):
        scaled = total[:, cols] * scale
        mine[:, start : start + hidden] = scaled[:count]
        theirs[:, start : start + hidden] = scaled[count:].astype(jnp.bfloat16)


def settle(parts, model_width, hidden):
    count = parts[0].shape[0] // 2
    shapes = [jax.ShapeDtypeStruct((count, 2 * hidden), t) for t in (jnp.float32, jnp.bfloat16)]
    kernel = functools.partial(settle_kernel, model_width, hidden)
    return whole_call(kernel, "settle", shapes, parts, 32 * count * hidden)


def activate_kernel(hidden, core_ref, mine, theirs, out):
    core = core_ref[0]
    for start, other in ((0, hidden), (hidden, 0)):
        a = mine[:, start : start + hidden]
        b = wide(theirs[:, other : other + hidden])
        gate, up = jnp.where(core == 0, a, b), jnp.where(core == 0, b, a)
        out[:, start : start + hidden] = (jax.nn.silu(gate) * up).astype(out.dtype)


def activate(core, mine, theirs):
    count, cols = mine.shape
    return pl.pallas_call(
        functools.partial(activate_kernel, cols // 2),
        out_shape=jax.ShapeDtypeStruct((count, cols), jnp.bfloat16),
        in_specs=[pl.BlockSpec(memory_space=pltpu.SMEM)]
        + [pl.BlockSpec(memory_space=pltpu.VMEM)] * 2,
        out_specs=pl.BlockSpec(memory_space=pltpu.VMEM),
        compiler_params=pltpu.CompilerParams(vmem_limit_bytes=VMEM_LIMIT),
        cost_estimate=pl.CostEstimate(
            flops=8 * count * cols, bytes_accessed=8 * count * cols, transcendentals=count * cols
        ),
        name="activate",
    )(core.astype(jnp.int32)[None], mine, theirs)


def ring(first):
    def shift(value, by):
        pairs = []
        for g in range(16):
            for tp in range(4):
                x, z = g // 4, g % 4
                if (tp % 2 == 0) == first:
                    x = (x + by) % 4
                else:
                    z = (z + by) % 4
                pairs.append((g * 4 + tp, (x * 4 + z) * 4 + tp))
        return lax.ppermute(value, ("grp", "yh", "core"), pairs)

    return shift


shift_1, shift_2 = ring(True), ring(False)


def shift_y(value, by):
    def moved(place):
        role, yh, core = place // 4, place // 2 % 2, place % 2
        y = (yh * 2 + role + by) % 4
        return y % 2 * 4 + y // 2 * 2 + core

    return lax.ppermute(value, ("role", "yh", "core"), [(p, moved(p)) for p in range(8)])


def swap(value, axis):
    return lax.ppermute(value, axis, [(0, 1), (1, 0)])


def gather(block, shift):
    return [block] + [shift(block, s) for s in SHIFTS[1:]]


def gather_from(blocks, shift):
    return [blocks[0]] + [shift(b, s) for b, s in zip(blocks[1:], SHIFTS[1:])]


def wide(value):
    return value.astype(jnp.float32)


def add(*values):
    return sum(wide(v) for v in values)


def absolute(blocks, place, axis):
    take = lambda i: lax.slice_in_dim(blocks, i, i + 1, axis=axis)
    doubled = jnp.concatenate([take(i) for i in (2, 3, 1, 0, 2, 3, 1)], axis=axis)
    return lax.dynamic_slice_in_dim(doubled, (3 - place) % 4, 4, axis=axis)


def relative(blocks, place, axis):
    doubled = jnp.concatenate([blocks, lax.slice_in_dim(blocks, 0, 3, axis=axis)], axis=axis)
    turned = lax.dynamic_slice_in_dim(doubled, place, 4, axis=axis)
    return jnp.concatenate(
        [lax.slice_in_dim(turned, i, i + 1, axis=axis) for i in (0, 3, 1, 2)], axis=axis
    )


def body(
    q_latent,
    kv_new,
    kv_cache,
    lengths,
    members,
    hidden_in,
    w_uv,
    w_o,
    norm_gain,
    w_gate,
    w_up,
    w_down,
):
    groups = lax.axis_size("grp")
    place_x, place_z = lax.axis_index("grp") // 4, lax.axis_index("grp") % 4
    core, yh = lax.axis_index("core"), lax.axis_index("yh")
    place_1 = jnp.where(core == 0, place_x, place_z)
    place_2 = jnp.where(core == 0, place_z, place_x)
    tokens, heads, kv = q_latent.shape
    latent = w_uv.shape[1]
    value_width = w_uv.shape[2]
    width = w_o.shape[1]
    model_width = width * groups
    hidden = w_gate.shape[1]
    score_scale = (value_width + kv - latent) ** (-0.5)

    uv_pair = (w_uv, swap(w_uv, "core"))
    o_pair = join(*(jnp.swapaxes(w, 0, 1) for w in (w_o, swap(w_o, "core"))))
    down_pair = join(*(jnp.swapaxes(w, 0, 1) for w in (w_down, swap(w_down, "core"))))
    near, far = attend(
        q_latent,
        kv_new,
        kv_cache,
        lengths,
        members,
        (2 * yh + core).astype(jnp.int32)[None],
        score_scale,
        latent,
    )
    far = swap(far, "yh")
    values = head_values(yh, near, far, uv_pair)
    values, hidden_in, w_gate, w_up = lax.optimization_barrier(
        (values, hidden_in, w_gate, w_up)
    )
    in_pair = (
        jnp.where(core == 0, w_gate, w_up),
        swap(jnp.where(core == 0, w_up, w_gate), "core"),
    )

    residual = lax.dynamic_index_in_dim(
        hidden_in.reshape(4, 4, 2, 2, tokens, width), core, 3, keepdims=False
    )
    residual = jnp.where(core == 0, jnp.swapaxes(residual, 0, 1), residual)
    residual = wide(relative(relative(residual, place_2, 0), place_1, 1))


    pieces = gather(join(*gather(values, shift_1)), shift_2)
    attn_part = jnp.concatenate([pair_dot(p, o_pair) for p in (pieces[:1], pieces[1:])]).reshape(4, 4, 2, tokens, width)
    shared = 0.5 * residual + attn_part
    sent = shared.astype(jnp.bfloat16)
    behind, ahead, across = (shift_y(sent, s) for s in SHIFTS[1:])
    stream = shared + wide(across)
    rows = jnp.stack([stream, add(behind, ahead)]).astype(jnp.bfloat16)
    rows = jnp.stack([rows, jnp.swapaxes(swap(rows, "core"), 1, 2)])
    rows = jnp.transpose(rows, (2, 3, 0, 1, 4, 5, 6)).reshape(4, 4, 8 * tokens, width)

    gain = wide(norm_gain)[None]
    behind, ahead, far = FACING[2], FACING[1], FACING[3]
    far_a, far_c = partial_sums(rows, (far,), gain, in_pair, (((0, 0),), ((0, 1),)))
    ahead_c, behind_a = partial_sums(rows, (ahead, behind), gain, in_pair, (((0, 1),), ((1, 0),)))
    ahead_a, behind_c, own_a, own_c = partial_sums(
        rows, (ahead, behind, 0), gain, in_pair, (((0, 0),), ((1, 1),), ((2, 0),), ((2, 1),))
    )
    far_a, far_c = shift_1(far_a, 1), shift_1(far_c, -1)
    direct_c, direct_a = shift_1(ahead_c, 1), shift_1(behind_a, -1)
    relay_a = shift_1(add(ahead_a, far_a).astype(jnp.bfloat16), 1)
    relay_c = shift_1(add(behind_c, far_c).astype(jnp.bfloat16), -1)
    blocks = merge(own_a, own_c, direct_a, direct_c, relay_a, relay_c)
    parts = gather_from(blocks, shift_2)
    mine, theirs = settle(parts, model_width, hidden)
    activated = activate(core, mine, swap(theirs, "core"))

    own, behind, ahead, far = gather(activated, shift_1)
    low, high = join(own, behind), join(ahead, far)
    behind_low, ahead_high = shift_2(low, 1), shift_2(high, -1)
    behind_high, ahead_low = shift_2(high, 1), shift_2(low, -1)
    far_low, far_high = shift_2(behind_low, 1), shift_2(ahead_high, -1)
    pieces = (
        (low, high),
        (behind_low, behind_high, ahead_low, ahead_high),
        (far_low, far_high),
    )
    down = jnp.concatenate(
        [pair_dot(p, down_pair) for p in pieces]
    ).reshape(4, 4, 2, 2, tokens, width)
    at_home = jnp.arange(2)[None, None, :, None, None] == yh
    down = jnp.stack([down[:, :, 0] + jnp.where(at_home, stream, 0.0), down[:, :, 1]])
    down = down.astype(jnp.bfloat16)
    down = absolute(absolute(down, place_2, 1), place_1, 2)
    down = jnp.where(core == 0, jnp.swapaxes(down, 1, 2), down)
    role = lax.axis_index("role")
    down = jnp.where(role == 0, down, down[::-1]).reshape(2, groups, 1, 2 * tokens, width)
    down = jnp.broadcast_to(down, (2, groups, 2, 2 * tokens, width))
    down = down.reshape(2 * groups * 2, 2 * tokens, width)
    landed = lax.all_to_all(down, ("role", "grp", "yh"), split_axis=0, concat_axis=0)
    landed = landed.reshape(2, groups, 2, 2 * tokens, width)
    result = jnp.sum(wide(landed), axis=(0, 2)).astype(jnp.bfloat16)
    result = jnp.swapaxes(result, 0, 1).reshape(2, tokens, model_width)
    other = swap(result, "core")
    result = jnp.stack(
        [jnp.where(core == 0, result, other), jnp.where(core == 0, other, result)], axis=1
    )
    return result.reshape(4 * tokens, model_width)


def solution(mesh):
    tp = ("yh", "core")
    in_specs = (
        P(("role", "grp") + tp, None, None),
        P(("role", "grp") + tp, None),
        P(("role", "grp") + tp, None, None),
        P(("role", "grp") + tp),
        P(("role", "grp") + tp),
        P("role", "grp"),
        P(tp, None, None),
        P(tp, "grp"),
        P("grp"),
        P("grp", ("role",) + tp),
        P("grp", ("role",) + tp),
        P(("role",) + tp, "grp"),
    )
    out_specs = P(("role", "grp"), None)
    sizes = dict(mesh.shape)
    split_mesh = Mesh(
        mesh.devices.reshape(sizes["role"], sizes["grp"], 2, 2), ("role", "grp", "yh", "core")
    )
    return jax.shard_map(
        body, mesh=split_mesh, in_specs=in_specs, out_specs=out_specs, check_vma=False
    )
```

```python
import functools

import jax
import jax.numpy as jnp
from jax import lax
from jax.experimental import pallas as pl
from jax.experimental.pallas import tpu as pltpu
from jax.sharding import Mesh
from jax.sharding import PartitionSpec as P

epsilon = 1e-06
VMEM_LIMIT = 20 * 1024 * 1024
STREAM_LIMIT = 61 * 1024 * 1024


SHIFTS = (0, 1, -1, 2)
FACING = (0, 2, 1, 3)


def attend_kernel(scale, latent, per_step, plan_ref, q_ref, new_ref, *refs):
    kv_refs, near_ref, far_ref = refs[:per_step], refs[per_step], refs[per_step + 1]
    step = pl.program_id(0)
    tokens = per_step * pl.num_programs(0)
    place = plan_ref[2 * tokens]
    for i, kv_ref in enumerate(kv_refs):
        token = step * per_step + i
        length = plan_ref[tokens + plan_ref[token]]
        queries = jnp.concatenate([q_ref[i, place ^ k] for k in range(4)], axis=0)
        cache = kv_ref[0]
        newest = wide(new_ref[...])
        picked = lax.broadcasted_iota(jnp.int32, newest.shape, 0) == token
        newest = jnp.sum(jnp.where(picked, newest, 0.0), axis=0, keepdims=True)
        scores = scale * jnp.dot(queries, cache, preferred_element_type=jnp.float32)
        own = scale * jnp.sum(queries.astype(jnp.float32) * newest, axis=1, keepdims=True)
        usable = lax.broadcasted_iota(jnp.int32, scores.shape, 1) < length
        scores = jnp.where(usable, scores, -1e30)
        peak = jnp.maximum(jnp.max(scores, axis=1, keepdims=True), own)
        probs = jnp.exp(scores - peak).astype(jnp.bfloat16)
        self_weight = jnp.exp(own - peak)
        denom = jnp.sum(probs.astype(jnp.float32), axis=1, keepdims=True) + self_weight
        accum = lax.dot_general(
            cache[:latent], probs, (((1,), (1,)), ((), ())), preferred_element_type=jnp.float32
        ).T
        accum = accum + self_weight * newest[:, :latent]
        context = (accum / denom).astype(near_ref.dtype)
        half = context.shape[0] // 2
        near_ref[:, i] = context[:half].reshape(near_ref.shape[0], -1, latent)
        far_ref[:, i] = context[half:].reshape(far_ref.shape[0], -1, latent)


def attend(q_latent, kv_new, kv_cache, lengths, members, place, scale, latent):
    tokens, heads, kv = q_latent.shape
    ctx = kv_cache.shape[1]
    block = heads // 4
    per_step = 2

    def request(i):
        return lambda t, m: (m[t * per_step + i], 0, 0)

    grid_spec = pltpu.PrefetchScalarGridSpec(
        num_scalar_prefetch=1,
        grid=(tokens // per_step,),
        in_specs=[
            pl.BlockSpec((per_step, 4, block, kv), lambda t, m: (t, 0, 0, 0)),
            pl.BlockSpec((tokens, kv), lambda t, m: (0, 0)),
        ]
        + [pl.BlockSpec((1, kv, ctx), request(i)) for i in range(per_step)],
        out_specs=[pl.BlockSpec((2, per_step, block, latent), lambda t, m: (0, t, 0, 0))] * 2,
    )
    return pl.pallas_call(
        functools.partial(attend_kernel, scale, latent, per_step),
        grid_spec=grid_spec,
        out_shape=[jax.ShapeDtypeStruct((2, tokens, block, latent), jnp.bfloat16)] * 2,
        compiler_params=pltpu.CompilerParams(vmem_limit_bytes=STREAM_LIMIT),
        cost_estimate=pl.CostEstimate(
            flops=2 * tokens * heads * ctx * (kv + latent),
            bytes_accessed=2 * tokens * ctx * kv,
            transcendentals=tokens * heads * ctx,
        ),
        name="attend",
    )(
        jnp.concatenate([members, lengths, place]),
        q_latent.reshape(tokens, 4, block, kv),
        kv_new,
        *([jnp.swapaxes(kv_cache, 1, 2)] * per_step),
    )


def partial_kernel(jobs, *refs):
    count = 1 + max(rows for pieces in jobs for rows, _ in pieces)
    row_refs, gain_ref, weight_refs, outs = (
        refs[:count],
        refs[count],
        refs[count + 1 : count + 3],
        refs[count + 3 :],
    )
    half = weight_refs[0].shape[1]
    gain = gain_ref[...]
    ready = []
    for ref in row_refs:
        x = ref[...].reshape(-1, ref.shape[-1]).astype(jnp.float32)
        ready.append(((x * gain).astype(jnp.bfloat16), jnp.sum(x * x, axis=1, keepdims=True)))
    for pieces, out in zip(jobs, outs):
        start = 0
        for rows, side in pieces:
            scaled, square = ready[rows]
            out[:, start : start + half] = jnp.dot(
                scaled, weight_refs[side][...], preferred_element_type=jnp.float32
            ).astype(jnp.bfloat16)
            start += half
            if side == 0:
                high = square.astype(jnp.bfloat16).astype(jnp.float32)
                lane = lax.broadcasted_iota(jnp.int32, (scaled.shape[0], 128), 1)
                out[:, start : start + 128] = jnp.where(lane < 64, high, square - high).astype(
                    jnp.bfloat16
                )
                start += 128


def partial_sums(rows, places, gain, weights, jobs):
    _, _, per_group, width = rows.shape
    half = weights[0].shape[1]
    count = 4 * per_group
    whole = lambda i: (0, 0)

    def at(place):
        return lambda i: (0, place, 0, 0)

    widths = [sum(half + (128 if side == 0 else 0) for _, side in pieces) for pieces in jobs]
    return pl.pallas_call(
        functools.partial(partial_kernel, jobs),
        grid=(1,),
        in_specs=[pl.BlockSpec((4, 1, per_group, width), at(p)) for p in places]
        + [pl.BlockSpec((1, width), whole)]
        + [pl.BlockSpec((width, half), whole)] * 2,
        out_specs=[pl.BlockSpec((count, w), whole) for w in widths],
        out_shape=[jax.ShapeDtypeStruct((count, w), jnp.bfloat16) for w in widths],
        compiler_params=pltpu.CompilerParams(vmem_limit_bytes=VMEM_LIMIT),
        cost_estimate=pl.CostEstimate(
            flops=2 * count * width * sum(widths),
            bytes_accessed=2 * (2 * width * half + count * sum(widths)),
            transcendentals=0,
        ),
        name="partial_sums",
    )(*([rows] * len(places)), gain, *weights)


def merge_kernel(own_a, own_c, direct_a, direct_c, relay_a, relay_c, *outs):
    wide_a = own_a.shape[1]
    rows = outs[0].shape[0]
    for out, place in zip(outs, FACING):
        part = pl.ds(place * rows, rows)
        total = wide(own_a[part, :]) + wide(relay_a[part, :]) + wide(direct_a[part, :])
        out[:, :wide_a] = total.astype(jnp.bfloat16)
        total = wide(own_c[part, :]) + wide(relay_c[part, :]) + wide(direct_c[part, :])
        out[:, wide_a:] = total.astype(jnp.bfloat16)


def merge(*operands):
    own_a, own_c = operands[:2]
    rows = own_a.shape[0] // 4
    cols = own_a.shape[1] + own_c.shape[1]
    return pl.pallas_call(
        merge_kernel,
        out_shape=[jax.ShapeDtypeStruct((rows, cols), jnp.bfloat16)] * 4,
        in_specs=[pl.BlockSpec(memory_space=pltpu.VMEM)] * 6,
        out_specs=[pl.BlockSpec(memory_space=pltpu.VMEM)] * 4,
        compiler_params=pltpu.CompilerParams(vmem_limit_bytes=VMEM_LIMIT),
        cost_estimate=pl.CostEstimate(
            flops=12 * rows * cols, bytes_accessed=32 * rows * cols, transcendentals=0
        ),
        name="merge",
    )(*operands)


def whole_call(kernel, name, out_shapes, operands, cost):
    return pl.pallas_call(
        kernel,
        out_shape=out_shapes,
        in_specs=[pl.BlockSpec(memory_space=pltpu.VMEM)] * len(operands),
        out_specs=[pl.BlockSpec(memory_space=pltpu.VMEM)] * len(out_shapes),
        compiler_params=pltpu.CompilerParams(vmem_limit_bytes=VMEM_LIMIT),
        cost_estimate=pl.CostEstimate(flops=cost, bytes_accessed=cost, transcendentals=0),
        name=name,
    )(*operands)


def join_kernel(*refs):
    *blocks, out = refs
    count = blocks[0].shape[0]
    for i, block in enumerate(blocks):
        out[i * count : (i + 1) * count] = block[...]


def join(*blocks):
    count, cols = blocks[0].shape
    shape = jax.ShapeDtypeStruct((len(blocks) * count, cols), blocks[0].dtype)
    return whole_call(join_kernel, "join", [shape], blocks, 4 * shape.size)[0]


def pair_dot_kernel(*refs):
    *blocks, weights, out = refs
    half, width = weights.shape[1], out.shape[1]
    step = half // 4 if half % 512 == 0 else half // 3
    total = 0.0
    for side in range(2):
        for k in range(0, half, step):
            cols = slice(side * half + k, side * half + k + step)
            rows = jnp.concatenate([b[:, cols] for b in blocks])
            total += lax.dot_general(
                rows,
                weights[side * width : (side + 1) * width, k : k + step],
                (((1,), (1,)), ((), ())),
                preferred_element_type=jnp.float32,
            )
    out[...] = total


def pair_dot(blocks, weights):
    count = sum(b.shape[0] for b in blocks)
    width, half = weights.shape[0] // 2, weights.shape[1]
    shape = jax.ShapeDtypeStruct((count, width), jnp.float32)
    return whole_call(pair_dot_kernel, "pair_dot", [shape], (*blocks, weights), 4 * width * half)[0]


def head_values_kernel(yh_ref, near, far, *refs):
    *weights, out = refs
    yh = yh_ref[0]
    count, heads = near.shape[1:3]
    width = weights[0].shape[2]
    for c, weight in enumerate(weights):
        own, other = wide(near[c]), wide(far[c])
        rows = jnp.concatenate([jnp.where(yh == 0, own, other), jnp.where(yh == 0, other, own)])
        rows = jnp.swapaxes(rows, 0, 1).astype(jnp.bfloat16)
        for h in range(heads):
            start = (c * heads + h) * width
            out[:, start : start + width] = jnp.dot(
                rows[h], weight[h], preferred_element_type=jnp.float32
            ).astype(out.dtype)


def head_values(yh, near, far, weights):
    tokens, heads = near.shape[1:3]
    shape = jax.ShapeDtypeStruct((2 * tokens, 2 * heads * weights[0].shape[2]), jnp.bfloat16)
    return pl.pallas_call(
        head_values_kernel,
        out_shape=shape,
        in_specs=[pl.BlockSpec(memory_space=pltpu.SMEM)]
        + [pl.BlockSpec(memory_space=pltpu.VMEM)] * 4,
        out_specs=pl.BlockSpec(memory_space=pltpu.VMEM),
        compiler_params=pltpu.CompilerParams(vmem_limit_bytes=VMEM_LIMIT),
        cost_estimate=pl.CostEstimate(
            flops=2 * shape.size * near.shape[3],
            bytes_accessed=4 * weights[0].size,
            transcendentals=0,
        ),
        name="head_values",
    )(yh.astype(jnp.int32)[None], near, far, *weights)


def settle_kernel(model_width, hidden, *refs):
    parts, (mine, theirs) = refs[:4], refs[4:]
    total = sum(wide(r[...]) for r in parts)
    square = total[:, hidden : hidden + 1] + total[:, hidden + 64 : hidden + 65]
    scale = lax.rsqrt(square / model_width + epsilon)
    count = mine.shape[0]
    for start, cols in ((0, slice(0, hidden)), (hidden, slice(hidden + 128, None))):
        scaled = total[:, cols] * scale
        mine[:, start : start + hidden] = scaled[:count]
        theirs[:, start : start + hidden] = scaled[count:].astype(jnp.bfloat16)


def settle(parts, model_width, hidden):
    count = parts[0].shape[0] // 2
    shapes = [jax.ShapeDtypeStruct((count, 2 * hidden), t) for t in (jnp.float32, jnp.bfloat16)]
    kernel = functools.partial(settle_kernel, model_width, hidden)
    return whole_call(kernel, "settle", shapes, parts, 32 * count * hidden)


def activate_kernel(hidden, core_ref, mine, theirs, out):
    core = core_ref[0]
    for start, other in ((0, hidden), (hidden, 0)):
        a = mine[:, start : start + hidden]
        b = wide(theirs[:, other : other + hidden])
        gate, up = jnp.where(core == 0, a, b), jnp.where(core == 0, b, a)
        out[:, start : start + hidden] = (jax.nn.silu(gate) * up).astype(out.dtype)


def activate(core, mine, theirs):
    count, cols = mine.shape
    return pl.pallas_call(
        functools.partial(activate_kernel, cols // 2),
        out_shape=jax.ShapeDtypeStruct((count, cols), jnp.bfloat16),
        in_specs=[pl.BlockSpec(memory_space=pltpu.SMEM)]
        + [pl.BlockSpec(memory_space=pltpu.VMEM)] * 2,
        out_specs=pl.BlockSpec(memory_space=pltpu.VMEM),
        compiler_params=pltpu.CompilerParams(vmem_limit_bytes=VMEM_LIMIT),
        cost_estimate=pl.CostEstimate(
            flops=8 * count * cols, bytes_accessed=8 * count * cols, transcendentals=count * cols
        ),
        name="activate",
    )(core.astype(jnp.int32)[None], mine, theirs)


def ring(first):
    def shift(value, by):
        pairs = []
        for g in range(16):
            for tp in range(4):
                x, z = g // 4, g % 4
                if (tp % 2 == 0) == first:
                    x = (x + by) % 4
                else:
                    z = (z + by) % 4
                pairs.append((g * 4 + tp, (x * 4 + z) * 4 + tp))
        return lax.ppermute(value, ("grp", "yh", "core"), pairs)

    return shift


shift_1, shift_2 = ring(True), ring(False)


def shift_y(value, by):
    def moved(place):
        role, yh, core = place // 4, place // 2 % 2, place % 2
        y = (yh * 2 + role + by) % 4
        return y % 2 * 4 + y // 2 * 2 + core

    return lax.ppermute(value, ("role", "yh", "core"), [(p, moved(p)) for p in range(8)])


def swap(value, axis):
    return lax.ppermute(value, axis, [(0, 1), (1, 0)])


def gather(block, shift):
    return [block] + [shift(block, s) for s in SHIFTS[1:]]


def gather_from(blocks, shift):
    return [blocks[0]] + [shift(b, s) for b, s in zip(blocks[1:], SHIFTS[1:])]


def wide(value):
    return value.astype(jnp.float32)


def add(*values):
    return sum(wide(v) for v in values)


def absolute(blocks, place, axis):
    take = lambda i: lax.slice_in_dim(blocks, i, i + 1, axis=axis)
    doubled = jnp.concatenate([take(i) for i in (2, 3, 1, 0, 2, 3, 1)], axis=axis)
    return lax.dynamic_slice_in_dim(doubled, (3 - place) % 4, 4, axis=axis)


def relative(blocks, place, axis):
    doubled = jnp.concatenate([blocks, lax.slice_in_dim(blocks, 0, 3, axis=axis)], axis=axis)
    turned = lax.dynamic_slice_in_dim(doubled, place, 4, axis=axis)
    return jnp.concatenate(
        [lax.slice_in_dim(turned, i, i + 1, axis=axis) for i in (0, 3, 1, 2)], axis=axis
    )


def body(
    q_latent,
    kv_new,
    kv_cache,
    lengths,
    members,
    hidden_in,
    w_uv,
    w_o,
    norm_gain,
    w_gate,
    w_up,
    w_down,
):
    groups = lax.axis_size("grp")
    place_x, place_z = lax.axis_index("grp") // 4, lax.axis_index("grp") % 4
    core, yh = lax.axis_index("core"), lax.axis_index("yh")
    place_1 = jnp.where(core == 0, place_x, place_z)
    place_2 = jnp.where(core == 0, place_z, place_x)
    tokens, heads, kv = q_latent.shape
    latent = w_uv.shape[1]
    value_width = w_uv.shape[2]
    width = w_o.shape[1]
    model_width = width * groups
    hidden = w_gate.shape[1]
    score_scale = (value_width + kv - latent) ** (-0.5)

    uv_pair = (w_uv, swap(w_uv, "core"))
    o_pair = join(*(jnp.swapaxes(w, 0, 1) for w in (w_o, swap(w_o, "core"))))
    down_pair = join(*(jnp.swapaxes(w, 0, 1) for w in (w_down, swap(w_down, "core"))))
    near, far = attend(
        q_latent,
        kv_new,
        kv_cache,
        lengths,
        members,
        (2 * yh + core).astype(jnp.int32)[None],
        score_scale,
        latent,
    )
    far = swap(far, "yh")
    values = head_values(yh, near, far, uv_pair)
    values, hidden_in, w_gate, w_up = lax.optimization_barrier(
        (values, hidden_in, w_gate, w_up)
    )
    in_pair = (
        jnp.where(core == 0, w_gate, w_up),
        swap(jnp.where(core == 0, w_up, w_gate), "core"),
    )

    residual = lax.dynamic_index_in_dim(
        hidden_in.reshape(4, 4, 2, 2, tokens, width), core, 3, keepdims=False
    )
    residual = jnp.where(core == 0, jnp.swapaxes(residual, 0, 1), residual)
    residual = wide(relative(relative(residual, place_2, 0), place_1, 1))


    pieces = gather(join(*gather(values, shift_1)), shift_2)
    attn_part = jnp.concatenate([pair_dot(p, o_pair) for p in (pieces[:1], pieces[1:])]).reshape(4, 4, 2, tokens, width)
    shared = 0.5 * residual + attn_part
    sent = shared.astype(jnp.bfloat16)
    behind, ahead, across = (shift_y(sent, s) for s in SHIFTS[1:])
    stream = shared + wide(across)
    rows = jnp.stack([stream, add(behind, ahead)]).astype(jnp.bfloat16)
    rows = jnp.stack([rows, jnp.swapaxes(swap(rows, "core"), 1, 2)])
    rows = jnp.transpose(rows, (2, 3, 0, 1, 4, 5, 6)).reshape(4, 4, 8 * tokens, width)

    gain = wide(norm_gain)[None]
    behind, ahead, far = FACING[2], FACING[1], FACING[3]
    far_a, far_c = partial_sums(rows, (far,), gain, in_pair, (((0, 0),), ((0, 1),)))
    ahead_c, behind_a = partial_sums(rows, (ahead, behind), gain, in_pair, (((0, 1),), ((1, 0),)))
    ahead_a, behind_c, own_a, own_c = partial_sums(
        rows, (ahead, behind, 0), gain, in_pair, (((0, 0),), ((1, 1),), ((2, 0),), ((2, 1),))
    )
    far_a, far_c = shift_1(far_a, 1), shift_1(far_c, -1)
    direct_c, direct_a = shift_1(ahead_c, 1), shift_1(behind_a, -1)
    relay_a = shift_1(add(ahead_a, far_a).astype(jnp.bfloat16), 1)
    relay_c = shift_1(add(behind_c, far_c).astype(jnp.bfloat16), -1)
    blocks = merge(own_a, own_c, direct_a, direct_c, relay_a, relay_c)
    parts = gather_from(blocks, shift_2)
    mine, theirs = settle(parts, model_width, hidden)
    activated = activate(core, mine, swap(theirs, "core"))

    own, behind, ahead, far = gather(activated, shift_1)
    low, high = join(own, behind), join(ahead, far)
    behind_low, ahead_high = shift_2(low, 1), shift_2(high, -1)
    behind_high, ahead_low = shift_2(high, 1), shift_2(low, -1)
    far_low, far_high = shift_2(behind_low, 1), shift_2(ahead_high, -1)
    pieces = (
        (low, high),
        (behind_low, behind_high, ahead_low, ahead_high),
        (far_low, far_high),
    )
    down = jnp.concatenate(
        [pair_dot(p, down_pair) for p in pieces]
    ).reshape(4, 4, 2, 2, tokens, width)
    at_home = jnp.arange(2)[None, None, :, None, None] == yh
    down = jnp.stack([down[:, :, 0] + jnp.where(at_home, stream, 0.0), down[:, :, 1]])
    down = down.astype(jnp.bfloat16)
    down = absolute(absolute(down, place_2, 1), place_1, 2)
    down = jnp.where(core == 0, jnp.swapaxes(down, 1, 2), down)
    role = lax.axis_index("role")
    down = jnp.where(role == 0, down, down[::-1]).reshape(2, groups, 1, 2 * tokens, width)
    down = jnp.broadcast_to(down, (2, groups, 2, 2 * tokens, width))
    down = down.reshape(2 * groups * 2, 2 * tokens, width)
    landed = lax.all_to_all(down, ("role", "grp", "yh"), split_axis=0, concat_axis=0)
    landed = landed.reshape(2, groups, 2, 2 * tokens, width)
    result = jnp.sum(wide(landed), axis=(0, 2)).astype(jnp.bfloat16)
    result = jnp.swapaxes(result, 0, 1).reshape(2, tokens, model_width)
    other = swap(result, "core")
    result = jnp.stack(
        [jnp.where(core == 0, result, other), jnp.where(core == 0, other, result)], axis=1
    )
    return result.reshape(4 * tokens, model_width)


def solution(mesh):
    tp = ("yh", "core")
    in_specs = (
        P(("role", "grp") + tp, None, None),
        P(("role", "grp") + tp, None),
        P(("role", "grp") + tp, None, None),
        P(("role", "grp") + tp),
        P(("role", "grp") + tp),
        P("role", "grp"),
        P(tp, None, None),
        P(tp, "grp"),
        P("grp"),
        P("grp", ("role",) + tp),
        P("grp", ("role",) + tp),
        P(("role",) + tp, "grp"),
    )
    out_specs = P(("role", "grp"), None)
    sizes = dict(mesh.shape)
    split_mesh = Mesh(
        mesh.devices.reshape(sizes["role"], sizes["grp"], 2, 2), ("role", "grp", "yh", "core")
    )
    return jax.shard_map(
        body, mesh=split_mesh, in_specs=in_specs, out_specs=out_specs, check_vma=False
    )
```

```python
import functools

import jax
import jax.numpy as jnp
from jax import lax
from jax.experimental import pallas as pl
from jax.experimental.pallas import tpu as pltpu
from jax.sharding import Mesh
from jax.sharding import PartitionSpec as P

epsilon = 1e-06
VMEM_LIMIT = 20 * 1024 * 1024
STREAM_LIMIT = 61 * 1024 * 1024


SHIFTS = (0, 1, -1, 2)
FACING = (0, 2, 1, 3)


def attend_kernel(scale, latent, per_step, plan_ref, q_ref, new_ref, *refs):
    kv_refs, near_ref, far_ref = refs[:per_step], refs[per_step], refs[per_step + 1]
    step = pl.program_id(0)
    tokens = per_step * pl.num_programs(0)
    place = plan_ref[2 * tokens]
    for i, kv_ref in enumerate(kv_refs):
        token = step * per_step + i
        length = plan_ref[tokens + plan_ref[token]]
        queries = jnp.concatenate([q_ref[i, place ^ k] for k in range(4)], axis=0)
        cache = kv_ref[0]
        newest = wide(new_ref[...])
        picked = lax.broadcasted_iota(jnp.int32, newest.shape, 0) == token
        newest = jnp.sum(jnp.where(picked, newest, 0.0), axis=0, keepdims=True)
        scores = scale * jnp.dot(queries, cache, preferred_element_type=jnp.float32)
        own = scale * jnp.sum(queries.astype(jnp.float32) * newest, axis=1, keepdims=True)
        usable = lax.broadcasted_iota(jnp.int32, scores.shape, 1) < length
        scores = jnp.where(usable, scores, -1e30)
        peak = jnp.maximum(jnp.max(scores, axis=1, keepdims=True), own)
        probs = jnp.exp(scores - peak).astype(jnp.bfloat16)
        self_weight = jnp.exp(own - peak)
        denom = jnp.sum(probs.astype(jnp.float32), axis=1, keepdims=True) + self_weight
        accum = lax.dot_general(
            cache[:latent], probs, (((1,), (1,)), ((), ())), preferred_element_type=jnp.float32
        ).T
        accum = accum + self_weight * newest[:, :latent]
        context = (accum / denom).astype(near_ref.dtype)
        half = context.shape[0] // 2
        near_ref[:, i] = context[:half].reshape(near_ref.shape[0], -1, latent)
        far_ref[:, i] = context[half:].reshape(far_ref.shape[0], -1, latent)


def attend(q_latent, kv_new, kv_cache, lengths, members, place, scale, latent):
    tokens, heads, kv = q_latent.shape
    ctx = kv_cache.shape[1]
    block = heads // 4
    per_step = 2

    def request(i):
        return lambda t, m: (m[t * per_step + i], 0, 0)

    grid_spec = pltpu.PrefetchScalarGridSpec(
        num_scalar_prefetch=1,
        grid=(tokens // per_step,),
        in_specs=[
            pl.BlockSpec((per_step, 4, block, kv), lambda t, m: (t, 0, 0, 0)),
            pl.BlockSpec((tokens, kv), lambda t, m: (0, 0)),
        ]
        + [pl.BlockSpec((1, kv, ctx), request(i)) for i in range(per_step)],
        out_specs=[pl.BlockSpec((2, per_step, block, latent), lambda t, m: (0, t, 0, 0))] * 2,
    )
    return pl.pallas_call(
        functools.partial(attend_kernel, scale, latent, per_step),
        grid_spec=grid_spec,
        out_shape=[jax.ShapeDtypeStruct((2, tokens, block, latent), jnp.bfloat16)] * 2,
        compiler_params=pltpu.CompilerParams(vmem_limit_bytes=STREAM_LIMIT),
        cost_estimate=pl.CostEstimate(
            flops=2 * tokens * heads * ctx * (kv + latent),
            bytes_accessed=2 * tokens * ctx * kv,
            transcendentals=tokens * heads * ctx,
        ),
        name="attend",
    )(
        jnp.concatenate([members, lengths, place]),
        q_latent.reshape(tokens, 4, block, kv),
        kv_new,
        *([jnp.swapaxes(kv_cache, 1, 2)] * per_step),
    )


def partial_kernel(jobs, *refs):
    count = 1 + max(rows for pieces in jobs for rows, _ in pieces)
    row_refs, gain_ref, weight_refs, outs = (
        refs[:count],
        refs[count],
        refs[count + 1 : count + 3],
        refs[count + 3 :],
    )
    half = weight_refs[0].shape[1]
    gain = gain_ref[...]
    ready = []
    for ref in row_refs:
        x = ref[...].reshape(-1, ref.shape[-1]).astype(jnp.float32)
        ready.append(((x * gain).astype(jnp.bfloat16), jnp.sum(x * x, axis=1, keepdims=True)))
    for pieces, out in zip(jobs, outs):
        start = 0
        for rows, side in pieces:
            scaled, square = ready[rows]
            out[:, start : start + half] = jnp.dot(
                scaled, weight_refs[side][...], preferred_element_type=jnp.float32
            ).astype(jnp.bfloat16)
            start += half
            if side == 0:
                high = square.astype(jnp.bfloat16).astype(jnp.float32)
                lane = lax.broadcasted_iota(jnp.int32, (scaled.shape[0], 128), 1)
                out[:, start : start + 128] = jnp.where(lane < 64, high, square - high).astype(
                    jnp.bfloat16
                )
                start += 128


def partial_sums(rows, places, gain, weights, jobs):
    _, _, per_group, width = rows.shape
    half = weights[0].shape[1]
    count = 4 * per_group
    whole = lambda i: (0, 0)

    def at(place):
        return lambda i: (0, place, 0, 0)

    widths = [sum(half + (128 if side == 0 else 0) for _, side in pieces) for pieces in jobs]
    return pl.pallas_call(
        functools.partial(partial_kernel, jobs),
        grid=(1,),
        in_specs=[pl.BlockSpec((4, 1, per_group, width), at(p)) for p in places]
        + [pl.BlockSpec((1, width), whole)]
        + [pl.BlockSpec((width, half), whole)] * 2,
        out_specs=[pl.BlockSpec((count, w), whole) for w in widths],
        out_shape=[jax.ShapeDtypeStruct((count, w), jnp.bfloat16) for w in widths],
        compiler_params=pltpu.CompilerParams(vmem_limit_bytes=VMEM_LIMIT),
        cost_estimate=pl.CostEstimate(
            flops=2 * count * width * sum(widths),
            bytes_accessed=2 * (2 * width * half + count * sum(widths)),
            transcendentals=0,
        ),
        name="partial_sums",
    )(*([rows] * len(places)), gain, *weights)


def merge_kernel(first_row, own_a, own_c, direct_a, direct_c, relay_a, relay_c, *outs):
    wide_a = own_a.shape[1]
    rows = outs[0].shape[0]
    for place, out in enumerate(outs):
        here = pl.ds(place * rows, rows)
        part = pl.ds(first_row + place * rows, rows)
        total = wide(own_a[part, :]) + wide(relay_a[here, :]) + wide(direct_a[part, :])
        out[:, :wide_a] = total.astype(jnp.bfloat16)
        total = wide(own_c[part, :]) + wide(relay_c[here, :]) + wide(direct_c[part, :])
        out[:, wide_a:] = total.astype(jnp.bfloat16)


def merge(first_row, *operands):
    own_a, own_c = operands[:2]
    rows = own_a.shape[0] // 4
    cols = own_a.shape[1] + own_c.shape[1]
    shapes = [jax.ShapeDtypeStruct((rows, cols), jnp.bfloat16)] * 2
    kernel = functools.partial(merge_kernel, first_row)
    return whole_call(kernel, "merge", shapes, operands, 16 * rows * cols)


def whole_call(kernel, name, out_shapes, operands, cost):
    return pl.pallas_call(
        kernel,
        out_shape=out_shapes,
        in_specs=[pl.BlockSpec(memory_space=pltpu.VMEM)] * len(operands),
        out_specs=[pl.BlockSpec(memory_space=pltpu.VMEM)] * len(out_shapes),
        compiler_params=pltpu.CompilerParams(vmem_limit_bytes=VMEM_LIMIT),
        cost_estimate=pl.CostEstimate(flops=cost, bytes_accessed=cost, transcendentals=0),
        name=name,
    )(*operands)


def join_kernel(*refs):
    *blocks, out = refs
    count = blocks[0].shape[0]
    for i, block in enumerate(blocks):
        out[i * count : (i + 1) * count] = block[...]


def join(*blocks):
    count, cols = blocks[0].shape
    shape = jax.ShapeDtypeStruct((len(blocks) * count, cols), blocks[0].dtype)
    return whole_call(join_kernel, "join", [shape], blocks, 4 * shape.size)[0]


def pair_dot_kernel(*refs):
    *blocks, weights, out = refs
    half, width = weights.shape[1], out.shape[1]
    step = half // 4 if half % 512 == 0 else half // 3
    total = 0.0
    for side in range(2):
        for k in range(0, half, step):
            cols = slice(side * half + k, side * half + k + step)
            rows = jnp.concatenate([b[:, cols] for b in blocks])
            total += lax.dot_general(
                rows,
                weights[side * width : (side + 1) * width, k : k + step],
                (((1,), (1,)), ((), ())),
                preferred_element_type=jnp.float32,
            )
    out[...] = total


def pair_dot(blocks, weights):
    count = sum(b.shape[0] for b in blocks)
    width, half = weights.shape[0] // 2, weights.shape[1]
    shape = jax.ShapeDtypeStruct((count, width), jnp.float32)
    return whole_call(pair_dot_kernel, "pair_dot", [shape], (*blocks, weights), 4 * width * half)[0]


def head_values_kernel(yh_ref, near, far, *refs):
    *weights, out = refs
    yh = yh_ref[0]
    count, heads = near.shape[1:3]
    width = weights[0].shape[2]
    for c, weight in enumerate(weights):
        own, other = wide(near[c]), wide(far[c])
        rows = jnp.concatenate([jnp.where(yh == 0, own, other), jnp.where(yh == 0, other, own)])
        rows = jnp.swapaxes(rows, 0, 1).astype(jnp.bfloat16)
        for h in range(heads):
            start = (c * heads + h) * width
            out[:, start : start + width] = jnp.dot(
                rows[h], weight[h], preferred_element_type=jnp.float32
            ).astype(out.dtype)


def head_values(yh, near, far, weights):
    tokens, heads = near.shape[1:3]
    shape = jax.ShapeDtypeStruct((2 * tokens, 2 * heads * weights[0].shape[2]), jnp.bfloat16)
    return pl.pallas_call(
        head_values_kernel,
        out_shape=shape,
        in_specs=[pl.BlockSpec(memory_space=pltpu.SMEM)]
        + [pl.BlockSpec(memory_space=pltpu.VMEM)] * 4,
        out_specs=pl.BlockSpec(memory_space=pltpu.VMEM),
        compiler_params=pltpu.CompilerParams(vmem_limit_bytes=VMEM_LIMIT),
        cost_estimate=pl.CostEstimate(
            flops=2 * shape.size * near.shape[3],
            bytes_accessed=4 * weights[0].size,
            transcendentals=0,
        ),
        name="head_values",
    )(yh.astype(jnp.int32)[None], near, far, *weights)


def settle_kernel(model_width, hidden, *refs):
    parts, (mine, theirs) = refs[:4], refs[4:]
    total = sum(wide(r[...]) for r in parts)
    square = total[:, hidden : hidden + 1] + total[:, hidden + 64 : hidden + 65]
    scale = lax.rsqrt(square / model_width + epsilon)
    count = mine.shape[0]
    for start, cols in ((0, slice(0, hidden)), (hidden, slice(hidden + 128, None))):
        scaled = total[:, cols] * scale
        mine[:, start : start + hidden] = scaled[:count]
        theirs[:, start : start + hidden] = scaled[count:].astype(jnp.bfloat16)


def settle(parts, model_width, hidden):
    count = parts[0].shape[0] // 2
    shapes = [jax.ShapeDtypeStruct((count, 2 * hidden), t) for t in (jnp.float32, jnp.bfloat16)]
    kernel = functools.partial(settle_kernel, model_width, hidden)
    return whole_call(kernel, "settle", shapes, parts, 32 * count * hidden)


def activate_kernel(hidden, core_ref, mine, theirs, out):
    core = core_ref[0]
    for start, other in ((0, hidden), (hidden, 0)):
        a = mine[:, start : start + hidden]
        b = wide(theirs[:, other : other + hidden])
        gate, up = jnp.where(core == 0, a, b), jnp.where(core == 0, b, a)
        out[:, start : start + hidden] = (jax.nn.silu(gate) * up).astype(out.dtype)


def activate(core, mine, theirs):
    count, cols = mine.shape
    return pl.pallas_call(
        functools.partial(activate_kernel, cols // 2),
        out_shape=jax.ShapeDtypeStruct((count, cols), jnp.bfloat16),
        in_specs=[pl.BlockSpec(memory_space=pltpu.SMEM)]
        + [pl.BlockSpec(memory_space=pltpu.VMEM)] * 2,
        out_specs=pl.BlockSpec(memory_space=pltpu.VMEM),
        compiler_params=pltpu.CompilerParams(vmem_limit_bytes=VMEM_LIMIT),
        cost_estimate=pl.CostEstimate(
            flops=8 * count * cols, bytes_accessed=8 * count * cols, transcendentals=count * cols
        ),
        name="activate",
    )(core.astype(jnp.int32)[None], mine, theirs)


def ring(first):
    def shift(value, by):
        pairs = []
        for g in range(16):
            for tp in range(4):
                x, z = g // 4, g % 4
                if (tp % 2 == 0) == first:
                    x = (x + by) % 4
                else:
                    z = (z + by) % 4
                pairs.append((g * 4 + tp, (x * 4 + z) * 4 + tp))
        return lax.ppermute(value, ("grp", "yh", "core"), pairs)

    return shift


shift_1, shift_2 = ring(True), ring(False)


def shift_y(value, by):
    def moved(place):
        role, yh, core = place // 4, place // 2 % 2, place % 2
        y = (yh * 2 + role + by) % 4
        return y % 2 * 4 + y // 2 * 2 + core

    return lax.ppermute(value, ("role", "yh", "core"), [(p, moved(p)) for p in range(8)])


def swap(value, axis):
    return lax.ppermute(value, axis, [(0, 1), (1, 0)])


def gather(block, shift):
    return [block] + [shift(block, s) for s in SHIFTS[1:]]


def gather_from(blocks, shift):
    return [blocks[0]] + [shift(b, s) for b, s in zip(blocks[1:], SHIFTS[1:])]


def wide(value):
    return value.astype(jnp.float32)


def add(*values):
    return sum(wide(v) for v in values)


def absolute(blocks, place, axis):
    take = lambda i: lax.slice_in_dim(blocks, i, i + 1, axis=axis)
    doubled = jnp.concatenate([take(i) for i in (2, 3, 1, 0, 2, 3, 1)], axis=axis)
    return lax.dynamic_slice_in_dim(doubled, (3 - place) % 4, 4, axis=axis)


def relative(blocks, place, axis):
    doubled = jnp.concatenate([blocks, lax.slice_in_dim(blocks, 0, 3, axis=axis)], axis=axis)
    turned = lax.dynamic_slice_in_dim(doubled, place, 4, axis=axis)
    return jnp.concatenate(
        [lax.slice_in_dim(turned, i, i + 1, axis=axis) for i in (0, 3, 1, 2)], axis=axis
    )


def body(
    q_latent,
    kv_new,
    kv_cache,
    lengths,
    members,
    hidden_in,
    w_uv,
    w_o,
    norm_gain,
    w_gate,
    w_up,
    w_down,
):
    groups = lax.axis_size("grp")
    place_x, place_z = lax.axis_index("grp") // 4, lax.axis_index("grp") % 4
    core, yh = lax.axis_index("core"), lax.axis_index("yh")
    place_1 = jnp.where(core == 0, place_x, place_z)
    place_2 = jnp.where(core == 0, place_z, place_x)
    tokens, heads, kv = q_latent.shape
    latent = w_uv.shape[1]
    value_width = w_uv.shape[2]
    width = w_o.shape[1]
    model_width = width * groups
    hidden = w_gate.shape[1]
    score_scale = (value_width + kv - latent) ** (-0.5)

    uv_pair = (w_uv, swap(w_uv, "core"))
    o_pair = join(*(jnp.swapaxes(w, 0, 1) for w in (w_o, swap(w_o, "core"))))
    down_pair = join(*(jnp.swapaxes(w, 0, 1) for w in (w_down, swap(w_down, "core"))))
    near, far = attend(
        q_latent,
        kv_new,
        kv_cache,
        lengths,
        members,
        (2 * yh + core).astype(jnp.int32)[None],
        score_scale,
        latent,
    )
    far = swap(far, "yh")
    values = head_values(yh, near, far, uv_pair)
    values, hidden_in, w_gate, w_up = lax.optimization_barrier(
        (values, hidden_in, w_gate, w_up)
    )
    in_pair = (
        jnp.where(core == 0, w_gate, w_up),
        swap(jnp.where(core == 0, w_up, w_gate), "core"),
    )

    residual = lax.dynamic_index_in_dim(
        hidden_in.reshape(4, 4, 2, 2, tokens, width), core, 3, keepdims=False
    )
    residual = jnp.where(core == 0, jnp.swapaxes(residual, 0, 1), residual)
    residual = wide(relative(relative(residual, place_2, 0), place_1, 1))


    pieces = gather(join(*gather(values, shift_1)), shift_2)
    attn_part = jnp.concatenate([pair_dot(p, o_pair) for p in (pieces[:1], pieces[1:])]).reshape(4, 4, 2, tokens, width)
    shared = 0.5 * residual + attn_part
    sent = shared.astype(jnp.bfloat16)
    behind, ahead, across = (shift_y(sent, s) for s in SHIFTS[1:])
    stream = shared + wide(across)
    rows = jnp.stack([stream, add(behind, ahead)]).astype(jnp.bfloat16)
    home = jnp.where(yh == 0, stream[:, :, 0], stream[:, :, 1])
    rows = jnp.stack([rows, jnp.swapaxes(swap(rows, "core"), 1, 2)])
    rows = jnp.transpose(rows, (2, 3, 0, 1, 4, 5, 6)).reshape(4, 4, 8 * tokens, width)

    gain = wide(norm_gain)[None]
    behind, ahead, far = FACING[2], FACING[1], FACING[3]
    far_a, far_c = partial_sums(rows, (far,), gain, in_pair, (((0, 0),), ((0, 1),)))
    ahead_c, behind_a = partial_sums(rows, (ahead, behind), gain, in_pair, (((0, 1),), ((1, 0),)))
    ahead_a, behind_c, own_a, own_c = partial_sums(
        rows, (ahead, behind, 0), gain, in_pair, (((0, 0),), ((1, 1),), ((2, 0),), ((2, 1),))
    )
    far_a, far_c = shift_1(far_a, 1), shift_1(far_c, -1)
    direct_c, direct_a = shift_1(ahead_c, 1), shift_1(behind_a, -1)
    middle = far_a.shape[0] // 2
    blocks = {}
    for places, cut in (((2, 3), slice(middle, None)), ((0, 1), slice(0, middle))):
        relay_a = shift_1(add(ahead_a[cut], far_a[cut]).astype(jnp.bfloat16), 1)
        relay_c = shift_1(add(behind_c[cut], far_c[cut]).astype(jnp.bfloat16), -1)
        merged = merge(cut.start, own_a, own_c, direct_a, direct_c, relay_a, relay_c)
        blocks.update(zip(places, merged))
    parts = gather_from([blocks[FACING[i]] for i in range(4)], shift_2)
    mine, theirs = settle(parts, model_width, hidden)
    activated = activate(core, mine, swap(theirs, "core"))

    own, behind, ahead, far = gather(activated, shift_1)
    low, high = join(own, behind), join(ahead, far)
    behind_low, ahead_high = shift_2(low, 1), shift_2(high, -1)
    behind_high, ahead_low = shift_2(high, 1), shift_2(low, -1)
    far_low, far_high = shift_2(behind_low, 1), shift_2(ahead_high, -1)
    pieces = (
        (low, high),
        (behind_low, behind_high, ahead_low, ahead_high),
        (far_low, far_high),
    )
    down = jnp.concatenate(
        [pair_dot(p, down_pair) for p in pieces]
    ).reshape(4, 4, 2, 2, tokens, width)
    at_home = jnp.arange(2)[None, None, :, None, None] == yh
    down = jnp.stack([down[:, :, 0] + jnp.where(at_home, home[:, :, None], 0.0), down[:, :, 1]])
    down = down.astype(jnp.bfloat16)
    down = absolute(absolute(down, place_2, 1), place_1, 2)
    down = jnp.where(core == 0, jnp.swapaxes(down, 1, 2), down)
    role = lax.axis_index("role")
    down = jnp.where(role == 0, down, down[::-1]).reshape(2, groups, 1, 2 * tokens, width)
    down = jnp.broadcast_to(down, (2, groups, 2, 2 * tokens, width))
    down = down.reshape(2 * groups * 2, 2 * tokens, width)
    landed = lax.all_to_all(down, ("role", "grp", "yh"), split_axis=0, concat_axis=0)
    landed = landed.reshape(2, groups, 2, 2 * tokens, width)
    result = jnp.sum(wide(landed), axis=(0, 2)).astype(jnp.bfloat16)
    result = jnp.swapaxes(result, 0, 1).reshape(2, tokens, model_width)
    other = swap(result, "core")
    result = jnp.stack(
        [jnp.where(core == 0, result, other), jnp.where(core == 0, other, result)], axis=1
    )
    return result.reshape(4 * tokens, model_width)


def solution(mesh):
    tp = ("yh", "core")
    in_specs = (
        P(("role", "grp") + tp, None, None),
        P(("role", "grp") + tp, None),
        P(("role", "grp") + tp, None, None),
        P(("role", "grp") + tp),
        P(("role", "grp") + tp),
        P("role", "grp"),
        P(tp, None, None),
        P(tp, "grp"),
        P("grp"),
        P("grp", ("role",) + tp),
        P("grp", ("role",) + tp),
        P(("role",) + tp, "grp"),
    )
    out_specs = P(("role", "grp"), None)
    sizes = dict(mesh.shape)
    split_mesh = Mesh(
        mesh.devices.reshape(sizes["role"], sizes["grp"], 2, 2), ("role", "grp", "yh", "core")
    )
    return jax.shard_map(
        body, mesh=split_mesh, in_specs=in_specs, out_specs=out_specs, check_vma=False
    )
```

```python
import functools

import jax
import jax.numpy as jnp
from jax import lax
from jax.experimental import pallas as pl
from jax.experimental.pallas import tpu as pltpu
from jax.sharding import Mesh
from jax.sharding import PartitionSpec as P

epsilon = 1e-06
VMEM_LIMIT = 17 * 1024 * 1024
STREAM_LIMIT = 61 * 1024 * 1024


SHIFTS = (0, 1, -1, 2)
FACING = (0, 2, 1, 3)


def attend_kernel(scale, latent, per_step, plan_ref, q_ref, new_ref, *refs):
    kv_refs, near_ref, far_ref = refs[:per_step], refs[per_step], refs[per_step + 1]
    step = pl.program_id(0)
    tokens = per_step * pl.num_programs(0)
    place = plan_ref[2 * tokens]
    for i, kv_ref in enumerate(kv_refs):
        token = step * per_step + i
        length = plan_ref[tokens + plan_ref[token]]
        queries = jnp.concatenate([q_ref[i, place ^ k] for k in range(4)], axis=0)
        cache = kv_ref[0]
        newest = wide(new_ref[...])
        picked = lax.broadcasted_iota(jnp.int32, newest.shape, 0) == token
        newest = jnp.sum(jnp.where(picked, newest, 0.0), axis=0, keepdims=True)
        scores = scale * jnp.dot(queries, cache, preferred_element_type=jnp.float32)
        own = scale * jnp.sum(queries.astype(jnp.float32) * newest, axis=1, keepdims=True)
        usable = lax.broadcasted_iota(jnp.int32, scores.shape, 1) < length
        scores = jnp.where(usable, scores, -1e30)
        peak = jnp.maximum(jnp.max(scores, axis=1, keepdims=True), own)
        probs = jnp.exp(scores - peak).astype(jnp.bfloat16)
        self_weight = jnp.exp(own - peak)
        denom = jnp.sum(probs.astype(jnp.float32), axis=1, keepdims=True) + self_weight
        accum = lax.dot_general(
            cache[:latent], probs, (((1,), (1,)), ((), ())), preferred_element_type=jnp.float32
        ).T
        accum = accum + self_weight * newest[:, :latent]
        context = (accum / denom).astype(near_ref.dtype)
        half = context.shape[0] // 2
        near_ref[:, i] = context[:half].reshape(near_ref.shape[0], -1, latent)
        far_ref[:, i] = context[half:].reshape(far_ref.shape[0], -1, latent)


def attend(q_latent, kv_new, kv_cache, lengths, members, place, scale, latent):
    tokens, heads, kv = q_latent.shape
    ctx = kv_cache.shape[1]
    block = heads // 4
    per_step = 2

    def request(i):
        return lambda t, m: (m[t * per_step + i], 0, 0)

    grid_spec = pltpu.PrefetchScalarGridSpec(
        num_scalar_prefetch=1,
        grid=(tokens // per_step,),
        in_specs=[
            pl.BlockSpec((per_step, 4, block, kv), lambda t, m: (t, 0, 0, 0)),
            pl.BlockSpec((tokens, kv), lambda t, m: (0, 0)),
        ]
        + [pl.BlockSpec((1, kv, ctx), request(i)) for i in range(per_step)],
        out_specs=[pl.BlockSpec((2, per_step, block, latent), lambda t, m: (0, t, 0, 0))] * 2,
    )
    return pl.pallas_call(
        functools.partial(attend_kernel, scale, latent, per_step),
        grid_spec=grid_spec,
        out_shape=[jax.ShapeDtypeStruct((2, tokens, block, latent), jnp.bfloat16)] * 2,
        compiler_params=pltpu.CompilerParams(vmem_limit_bytes=STREAM_LIMIT),
        cost_estimate=pl.CostEstimate(
            flops=2 * tokens * heads * ctx * (kv + latent),
            bytes_accessed=2 * tokens * ctx * kv,
            transcendentals=tokens * heads * ctx,
        ),
        name="attend",
    )(
        jnp.concatenate([members, lengths, place]),
        q_latent.reshape(tokens, 4, block, kv),
        kv_new,
        *([jnp.swapaxes(kv_cache, 1, 2)] * per_step),
    )


def partial_kernel(jobs, *refs):
    count = 1 + max(rows for pieces in jobs for rows, _ in pieces)
    row_refs, gain_ref, weight_refs, outs = (
        refs[:count],
        refs[count],
        refs[count + 1 : count + 3],
        refs[count + 3 :],
    )
    half = weight_refs[0].shape[1]
    gain = gain_ref[...]
    ready = []
    for ref in row_refs:
        x = ref[...].reshape(-1, ref.shape[-1]).astype(jnp.float32)
        ready.append(((x * gain).astype(jnp.bfloat16), jnp.sum(x * x, axis=1, keepdims=True)))
    for pieces, out in zip(jobs, outs):
        start = 0
        for rows, side in pieces:
            scaled, square = ready[rows]
            out[:, start : start + half] = jnp.dot(
                scaled, weight_refs[side][...], preferred_element_type=jnp.float32
            ).astype(jnp.bfloat16)
            start += half
            if side == 0:
                high = square.astype(jnp.bfloat16).astype(jnp.float32)
                lane = lax.broadcasted_iota(jnp.int32, (scaled.shape[0], 128), 1)
                out[:, start : start + 128] = jnp.where(lane < 64, high, square - high).astype(
                    jnp.bfloat16
                )
                start += 128


def partial_sums(rows, places, gain, weights, jobs):
    _, _, per_group, width = rows.shape
    half = weights[0].shape[1]
    count = 4 * per_group
    whole = lambda i: (0, 0)

    def at(place):
        return lambda i: (0, place, 0, 0)

    widths = [sum(half + (128 if side == 0 else 0) for _, side in pieces) for pieces in jobs]
    return pl.pallas_call(
        functools.partial(partial_kernel, jobs),
        grid=(1,),
        in_specs=[pl.BlockSpec((4, 1, per_group, width), at(p)) for p in places]
        + [pl.BlockSpec((1, width), whole)]
        + [pl.BlockSpec((width, half), whole)] * 2,
        out_specs=[pl.BlockSpec((count, w), whole) for w in widths],
        out_shape=[jax.ShapeDtypeStruct((count, w), jnp.bfloat16) for w in widths],
        compiler_params=pltpu.CompilerParams(vmem_limit_bytes=VMEM_LIMIT),
        cost_estimate=pl.CostEstimate(
            flops=2 * count * width * sum(widths),
            bytes_accessed=2 * (2 * width * half + count * sum(widths)),
            transcendentals=0,
        ),
        name="partial_sums",
    )(*([rows] * len(places)), gain, *weights)


def merge_kernel(first_row, own_a, own_c, direct_a, direct_c, relay_a, relay_c, *outs):
    wide_a = own_a.shape[1]
    rows = outs[0].shape[0]
    for place, out in enumerate(outs):
        here = pl.ds(place * rows, rows)
        part = pl.ds(first_row + place * rows, rows)
        total = wide(own_a[part, :]) + wide(relay_a[here, :]) + wide(direct_a[part, :])
        out[:, :wide_a] = total.astype(jnp.bfloat16)
        total = wide(own_c[part, :]) + wide(relay_c[here, :]) + wide(direct_c[part, :])
        out[:, wide_a:] = total.astype(jnp.bfloat16)


def merge(first_row, *operands):
    own_a, own_c = operands[:2]
    rows = own_a.shape[0] // 4
    cols = own_a.shape[1] + own_c.shape[1]
    shapes = [jax.ShapeDtypeStruct((rows, cols), jnp.bfloat16)] * 2
    kernel = functools.partial(merge_kernel, first_row)
    return whole_call(kernel, "merge", shapes, operands, 16 * rows * cols)


def whole_call(kernel, name, out_shapes, operands, cost):
    return pl.pallas_call(
        kernel,
        out_shape=out_shapes,
        in_specs=[pl.BlockSpec(memory_space=pltpu.VMEM)] * len(operands),
        out_specs=[pl.BlockSpec(memory_space=pltpu.VMEM)] * len(out_shapes),
        compiler_params=pltpu.CompilerParams(vmem_limit_bytes=VMEM_LIMIT),
        cost_estimate=pl.CostEstimate(flops=cost, bytes_accessed=cost, transcendentals=0),
        name=name,
    )(*operands)


def join_kernel(*refs):
    *blocks, out = refs
    count = blocks[0].shape[0]
    for i, block in enumerate(blocks):
        out[i * count : (i + 1) * count] = block[...]


def join(*blocks):
    count, cols = blocks[0].shape
    shape = jax.ShapeDtypeStruct((len(blocks) * count, cols), blocks[0].dtype)
    return whole_call(join_kernel, "join", [shape], blocks, 4 * shape.size)[0]


def pair_dot_kernel(*refs):
    *blocks, weights, out = refs
    half, width = weights.shape[1], out.shape[1]
    step = half // 4 if half % 512 == 0 else half // 3
    total = 0.0
    for side in range(2):
        for k in range(0, half, step):
            cols = slice(side * half + k, side * half + k + step)
            rows = jnp.concatenate([b[:, cols] for b in blocks])
            total += lax.dot_general(
                rows,
                weights[side * width : (side + 1) * width, k : k + step],
                (((1,), (1,)), ((), ())),
                preferred_element_type=jnp.float32,
            )
    out[...] = total


def pair_dot(blocks, weights):
    count = sum(b.shape[0] for b in blocks)
    width, half = weights.shape[0] // 2, weights.shape[1]
    shape = jax.ShapeDtypeStruct((count, width), jnp.float32)
    return whole_call(pair_dot_kernel, "pair_dot", [shape], (*blocks, weights), 4 * width * half)[0]


def head_values_kernel(yh_ref, near, far, *refs):
    *weights, out = refs
    yh = yh_ref[0]
    count, heads = near.shape[1:3]
    width = weights[0].shape[2]
    for c, weight in enumerate(weights):
        own, other = wide(near[c]), wide(far[c])
        rows = jnp.concatenate([jnp.where(yh == 0, own, other), jnp.where(yh == 0, other, own)])
        rows = jnp.swapaxes(rows, 0, 1).astype(jnp.bfloat16)
        for h in range(heads):
            start = (c * heads + h) * width
            out[:, start : start + width] = jnp.dot(
                rows[h], weight[h], preferred_element_type=jnp.float32
            ).astype(out.dtype)


def head_values(yh, near, far, weights):
    tokens, heads = near.shape[1:3]
    shape = jax.ShapeDtypeStruct((2 * tokens, 2 * heads * weights[0].shape[2]), jnp.bfloat16)
    return pl.pallas_call(
        head_values_kernel,
        out_shape=shape,
        in_specs=[pl.BlockSpec(memory_space=pltpu.SMEM)]
        + [pl.BlockSpec(memory_space=pltpu.VMEM)] * 4,
        out_specs=pl.BlockSpec(memory_space=pltpu.VMEM),
        compiler_params=pltpu.CompilerParams(vmem_limit_bytes=VMEM_LIMIT),
        cost_estimate=pl.CostEstimate(
            flops=2 * shape.size * near.shape[3],
            bytes_accessed=4 * weights[0].size,
            transcendentals=0,
        ),
        name="head_values",
    )(yh.astype(jnp.int32)[None], near, far, *weights)


def settle_kernel(model_width, hidden, *refs):
    parts, (mine, theirs) = refs[:4], refs[4:]
    total = sum(wide(r[...]) for r in parts)
    square = total[:, hidden : hidden + 1] + total[:, hidden + 64 : hidden + 65]
    scale = lax.rsqrt(square / model_width + epsilon)
    count = mine.shape[0]
    for start, cols in ((0, slice(0, hidden)), (hidden, slice(hidden + 128, None))):
        scaled = total[:, cols] * scale
        mine[:, start : start + hidden] = scaled[:count]
        theirs[:, start : start + hidden] = scaled[count:].astype(jnp.bfloat16)


def settle(parts, model_width, hidden):
    count = parts[0].shape[0] // 2
    shapes = [jax.ShapeDtypeStruct((count, 2 * hidden), t) for t in (jnp.float32, jnp.bfloat16)]
    kernel = functools.partial(settle_kernel, model_width, hidden)
    return whole_call(kernel, "settle", shapes, parts, 32 * count * hidden)


def activate_kernel(hidden, core_ref, mine, theirs, out):
    core = core_ref[0]
    for start, other in ((0, hidden), (hidden, 0)):
        a = mine[:, start : start + hidden]
        b = wide(theirs[:, other : other + hidden])
        gate, up = jnp.where(core == 0, a, b), jnp.where(core == 0, b, a)
        out[:, start : start + hidden] = (jax.nn.silu(gate) * up).astype(out.dtype)


def activate(core, mine, theirs):
    count, cols = mine.shape
    return pl.pallas_call(
        functools.partial(activate_kernel, cols // 2),
        out_shape=jax.ShapeDtypeStruct((count, cols), jnp.bfloat16),
        in_specs=[pl.BlockSpec(memory_space=pltpu.SMEM)]
        + [pl.BlockSpec(memory_space=pltpu.VMEM)] * 2,
        out_specs=pl.BlockSpec(memory_space=pltpu.VMEM),
        compiler_params=pltpu.CompilerParams(vmem_limit_bytes=VMEM_LIMIT),
        cost_estimate=pl.CostEstimate(
            flops=8 * count * cols, bytes_accessed=8 * count * cols, transcendentals=count * cols
        ),
        name="activate",
    )(core.astype(jnp.int32)[None], mine, theirs)


def ring(first):
    def shift(value, by):
        pairs = []
        for g in range(16):
            for tp in range(4):
                x, z = g // 4, g % 4
                if (tp % 2 == 0) == first:
                    x = (x + by) % 4
                else:
                    z = (z + by) % 4
                pairs.append((g * 4 + tp, (x * 4 + z) * 4 + tp))
        return lax.ppermute(value, ("grp", "yh", "core"), pairs)

    return shift


shift_1, shift_2 = ring(True), ring(False)


def shift_y(value, by):
    def moved(place):
        role, yh, core = place // 4, place // 2 % 2, place % 2
        y = (yh * 2 + role + by) % 4
        return y % 2 * 4 + y // 2 * 2 + core

    return lax.ppermute(value, ("role", "yh", "core"), [(p, moved(p)) for p in range(8)])


def swap(value, axis):
    return lax.ppermute(value, axis, [(0, 1), (1, 0)])


def gather(block, shift):
    return [block] + [shift(block, s) for s in SHIFTS[1:]]


def gather_from(blocks, shift):
    return [blocks[0]] + [shift(b, s) for b, s in zip(blocks[1:], SHIFTS[1:])]


def wide(value):
    return value.astype(jnp.float32)


def add(*values):
    return sum(wide(v) for v in values)


def absolute(blocks, place, axis):
    take = lambda i: lax.slice_in_dim(blocks, i, i + 1, axis=axis)
    doubled = jnp.concatenate([take(i) for i in (2, 3, 1, 0, 2, 3, 1)], axis=axis)
    return lax.dynamic_slice_in_dim(doubled, (3 - place) % 4, 4, axis=axis)


def relative(blocks, place, axis):
    doubled = jnp.concatenate([blocks, lax.slice_in_dim(blocks, 0, 3, axis=axis)], axis=axis)
    turned = lax.dynamic_slice_in_dim(doubled, place, 4, axis=axis)
    return jnp.concatenate(
        [lax.slice_in_dim(turned, i, i + 1, axis=axis) for i in (0, 3, 1, 2)], axis=axis
    )


def body(
    q_latent,
    kv_new,
    kv_cache,
    lengths,
    members,
    hidden_in,
    w_uv,
    w_o,
    norm_gain,
    w_gate,
    w_up,
    w_down,
):
    groups = lax.axis_size("grp")
    place_x, place_z = lax.axis_index("grp") // 4, lax.axis_index("grp") % 4
    core, yh = lax.axis_index("core"), lax.axis_index("yh")
    place_1 = jnp.where(core == 0, place_x, place_z)
    place_2 = jnp.where(core == 0, place_z, place_x)
    tokens, heads, kv = q_latent.shape
    latent = w_uv.shape[1]
    value_width = w_uv.shape[2]
    width = w_o.shape[1]
    model_width = width * groups
    hidden = w_gate.shape[1]
    score_scale = (value_width + kv - latent) ** (-0.5)

    uv_pair = (w_uv, swap(w_uv, "core"))
    o_pair = join(*(jnp.swapaxes(w, 0, 1) for w in (w_o, swap(w_o, "core"))))
    down_pair = join(*(jnp.swapaxes(w, 0, 1) for w in (w_down, swap(w_down, "core"))))
    near, far = attend(
        q_latent,
        kv_new,
        kv_cache,
        lengths,
        members,
        (2 * yh + core).astype(jnp.int32)[None],
        score_scale,
        latent,
    )
    far = swap(far, "yh")
    values = head_values(yh, near, far, uv_pair)
    values, hidden_in, w_gate, w_up = lax.optimization_barrier(
        (values, hidden_in, w_gate, w_up)
    )
    in_pair = (
        jnp.where(core == 0, w_gate, w_up),
        swap(jnp.where(core == 0, w_up, w_gate), "core"),
    )

    residual = lax.dynamic_index_in_dim(
        hidden_in.reshape(4, 4, 2, 2, tokens, width), core, 3, keepdims=False
    )
    residual = jnp.where(core == 0, jnp.swapaxes(residual, 0, 1), residual)
    residual = wide(relative(relative(residual, place_2, 0), place_1, 1))


    pieces = gather(join(*gather(values, shift_1)), shift_2)
    attn_part = jnp.concatenate([pair_dot(p, o_pair) for p in (pieces[:1], pieces[1:])]).reshape(4, 4, 2, tokens, width)
    shared = 0.5 * residual + attn_part
    sent = shared.astype(jnp.bfloat16)
    behind, ahead, across = (shift_y(sent, s) for s in SHIFTS[1:])
    stream = shared + wide(across)
    rows = jnp.stack([stream, add(behind, ahead)]).astype(jnp.bfloat16)
    home = jnp.where(yh == 0, stream[:, :, 0], stream[:, :, 1])
    rows = jnp.stack([rows, jnp.swapaxes(swap(rows, "core"), 1, 2)])
    rows = jnp.transpose(rows, (2, 3, 0, 1, 4, 5, 6)).reshape(4, 4, 8 * tokens, width)

    gain = wide(norm_gain)[None]
    behind, ahead, far = FACING[2], FACING[1], FACING[3]
    far_a, far_c = partial_sums(rows, (far,), gain, in_pair, (((0, 0),), ((0, 1),)))
    ahead_c, behind_a = partial_sums(rows, (ahead, behind), gain, in_pair, (((0, 1),), ((1, 0),)))
    ahead_a, behind_c, own_a, own_c = partial_sums(
        rows, (ahead, behind, 0), gain, in_pair, (((0, 0),), ((1, 1),), ((2, 0),), ((2, 1),))
    )
    far_a, far_c = shift_1(far_a, 1), shift_1(far_c, -1)
    direct_c, direct_a = shift_1(ahead_c, 1), shift_1(behind_a, -1)
    middle = far_a.shape[0] // 2
    blocks = {}
    for places, cut in (((2, 3), slice(middle, None)), ((0, 1), slice(0, middle))):
        relay_a = shift_1(add(ahead_a[cut], far_a[cut]).astype(jnp.bfloat16), 1)
        relay_c = shift_1(add(behind_c[cut], far_c[cut]).astype(jnp.bfloat16), -1)
        merged = merge(cut.start, own_a, own_c, direct_a, direct_c, relay_a, relay_c)
        blocks.update(zip(places, merged))
    parts = gather_from([blocks[FACING[i]] for i in range(4)], shift_2)
    mine, theirs = settle(parts, model_width, hidden)
    activated = activate(core, mine, swap(theirs, "core"))

    own, behind, ahead, far = gather(activated, shift_1)
    low, high = join(own, behind), join(ahead, far)
    behind_low, ahead_high = shift_2(low, 1), shift_2(high, -1)
    behind_high, ahead_low = shift_2(high, 1), shift_2(low, -1)
    far_low, far_high = shift_2(behind_low, 1), shift_2(ahead_high, -1)
    pieces = (
        (low, high),
        (behind_low, behind_high, ahead_low, ahead_high),
        (far_low, far_high),
    )
    down = jnp.concatenate(
        [pair_dot(p, down_pair) for p in pieces]
    ).reshape(4, 4, 2, 2, tokens, width)
    at_home = jnp.arange(2)[None, None, :, None, None] == yh
    down = jnp.stack([down[:, :, 0] + jnp.where(at_home, home[:, :, None], 0.0), down[:, :, 1]])
    down = down.astype(jnp.bfloat16)
    down = absolute(absolute(down, place_2, 1), place_1, 2)
    down = jnp.where(core == 0, jnp.swapaxes(down, 1, 2), down)
    role = lax.axis_index("role")
    down = jnp.where(role == 0, down, down[::-1]).reshape(2, groups, 2, tokens, width)
    down = jnp.concatenate([down[:, :, 0], down[:, :, 1]], axis=-1)[:, :, None]
    down = jnp.broadcast_to(down, (2, groups, 2, tokens, 2 * width))
    down = down.reshape(2 * groups * 2, tokens, 2 * width)
    landed = lax.all_to_all(down, ("role", "grp", "yh"), split_axis=0, concat_axis=0)
    landed = landed.reshape(2, groups, 2, tokens, 2 * width)
    result = jnp.sum(wide(landed), axis=(0, 2)).astype(jnp.bfloat16)
    result = jnp.stack([result[:, :, :width], result[:, :, width:]])
    result = jnp.swapaxes(result, 1, 2).reshape(2, tokens, model_width)
    other = swap(result, "core")
    result = jnp.stack(
        [jnp.where(core == 0, result, other), jnp.where(core == 0, other, result)], axis=1
    )
    return result.reshape(4 * tokens, model_width)


def solution(mesh):
    tp = ("yh", "core")
    in_specs = (
        P(("role", "grp") + tp, None, None),
        P(("role", "grp") + tp, None),
        P(("role", "grp") + tp, None, None),
        P(("role", "grp") + tp),
        P(("role", "grp") + tp),
        P("role", "grp"),
        P(tp, None, None),
        P(tp, "grp"),
        P("grp"),
        P("grp", ("role",) + tp),
        P("grp", ("role",) + tp),
        P(("role",) + tp, "grp"),
    )
    out_specs = P(("role", "grp"), None)
    sizes = dict(mesh.shape)
    split_mesh = Mesh(
        mesh.devices.reshape(sizes["role"], sizes["grp"], 2, 2), ("role", "grp", "yh", "core")
    )
    return jax.shard_map(
        body, mesh=split_mesh, in_specs=in_specs, out_specs=out_specs, check_vma=False
    )
```
